32 devices in a mesh: grp: 2 (over x), dp: 4 (over y, core), tensor: 4 (over z).
Axes of the slice: x: 2, y: 2, z: 4, core: 2. Of those that a mesh axis runs over, the one named last changes fastest.
Arguments:
- tokens: int32 [2, 2, 4, 512], P(None, None, 'dp'), may hold values from 0 to 50430
- positions: int32 [2, 2, 4, 512], P(None, None, 'dp'), may hold values from 0 to 1023, as said below
- lengths: int32 [2, 2, 4], P(None, None, 'dp'), may hold values from 1 to 512, as said below
- embedding: float32 [50432, 768], P(('grp', 'dp', 'tensor')), may hold values from -1 to 1
- embedding_mom: float32 [50432, 768], P(('grp', 'dp', 'tensor')), may hold values from -3.8146973e-05 to 3.8146973e-05
- embedding_avg: float32 [50432, 768], P(('grp', 'dp', 'tensor')), may hold values from -0.21875 to 0.21875
- qkv_w: float32 [2, 768, 3, 768], P(None, ('grp', 'dp'), None, 'tensor'), may hold values from -0.21875 to 0.21875
- qkv_mom: float32 [2, 768, 3, 768], P(None, ('grp', 'dp'), None, 'tensor'), may hold values from -3.8146973e-05 to 3.8146973e-05
- qkv_avg: float32 [2, 768, 3, 768], P(None, ('grp', 'dp'), None, 'tensor'), may hold values from -0.21875 to 0.21875
- out_w: float32 [2, 768, 768], P(None, 'tensor', ('grp', 'dp')), may hold values from -1.25 to 1.25
- out_mom: float32 [2, 768, 768], P(None, 'tensor', ('grp', 'dp')), may hold values from -3.8146973e-05 to 3.8146973e-05
- out_avg: float32 [2, 768, 768], P(None, 'tensor', ('grp', 'dp')), may hold values from -1.25 to 1.25
- up_w: float32 [2, 768, 3072], P(None, ('grp', 'dp'), 'tensor'), may hold values from -0.21875 to 0.21875
- up_mom: float32 [2, 768, 3072], P(None, ('grp', 'dp'), 'tensor'), may hold values from -3.8146973e-05 to 3.8146973e-05
- up_avg: float32 [2, 768, 3072], P(None, ('grp', 'dp'), 'tensor'), may hold values from -0.21875 to 0.21875
- down_w: float32 [2, 3072, 768], P(None, 'tensor', ('grp', 'dp')), may hold values from -0.109375 to 0.109375
- down_mom: float32 [2, 3072, 768], P(None, 'tensor', ('grp', 'dp')), may hold values from -3.8146973e-05 to 3.8146973e-05
- down_avg: float32 [2, 3072, 768], P(None, 'tensor', ('grp', 'dp')), may hold values from -0.109375 to 0.109375
- norm_gains: float32 [5, 2, 768], replicated, may hold values from -1 to 3
- gains_mom: float32 [5, 2, 768], replicated, may hold values from -0.00021362305 to 0.00021362305
- gains_avg: float32 [5, 2, 768], replicated, may hold values from 0.5 to 1.5
Outputs:
- loss_sum: float32 [], replicated
- mask_count: float32 [], replicated
- grad_norm: float32 [], replicated
- new_embedding_mom: float32 [50432, 768], P(('grp', 'dp', 'tensor'))
- new_embedding: float32 [50432, 768], P(('grp', 'dp', 'tensor'))
- new_embedding_avg: float32 [50432, 768], P(('grp', 'dp', 'tensor'))
- new_qkv_mom: float32 [2, 768, 3, 768], P(None, ('grp', 'dp'), None, 'tensor')
- new_qkv_w: float32 [2, 768, 3, 768], P(None, ('grp', 'dp'), None, 'tensor')
- new_qkv_avg: float32 [2, 768, 3, 768], P(None, ('grp', 'dp'), None, 'tensor')
- new_out_mom: float32 [2, 768, 768], P(None, 'tensor', ('grp', 'dp'))
- new_out_w: float32 [2, 768, 768], P(None, 'tensor', ('grp', 'dp'))
- new_out_avg: float32 [2, 768, 768], P(None, 'tensor', ('grp', 'dp'))
- new_up_mom: float32 [2, 768, 3072], P(None, ('grp', 'dp'), 'tensor')
- new_up_w: float32 [2, 768, 3072], P(None, ('grp', 'dp'), 'tensor')
- new_up_avg: float32 [2, 768, 3072], P(None, ('grp', 'dp'), 'tensor')
- new_down_mom: float32 [2, 3072, 768], P(None, 'tensor', ('grp', 'dp'))
- new_down_w: float32 [2, 3072, 768], P(None, 'tensor', ('grp', 'dp'))
- new_down_avg: float32 [2, 3072, 768], P(None, 'tensor', ('grp', 'dp'))
- new_gains_mom: float32 [5, 2, 768], replicated
- new_gains: float32 [5, 2, 768], replicated
- new_gains_avg: float32 [5, 2, 768], replicated
The draws below stay inside these ranges and needn't reach their ends.
Inputs may be any that keep to these rules, and one draw needn't show every extreme that they name: In each micro-batch and row, positions[m, 0, r] and positions[m, 1, r] together hold every number of 0 to 1023 once. `lengths`: the slots in use are the first ones of each row; in every micro-batch some row has all 512 clean and some row all 512 masked slots in use.
All inputs are finite; a program needn't handle non-finite values.
Results may differ from the reference program's by a relative error of at most 0.012.
Values may be sent and summed in bfloat16 or wider, within the bound.
No kernel may reach another device: no remote copies, remote signals or barrier semaphores. Data moves between devices by JAX's collectives and lax.ppermute only.
A program may use at most 512 MiB of HBM per device.

```python
import math
import jax
import jax.numpy as jnp
import numpy as np
from jax import lax

D = 768
HEADS = 12
HEAD = 64
FF = 3072
V = 50432
L = 2
MB = 2
S = 512
ROWS = 4
N_GRP = 2
N_DP = 4
N_TENSOR = 4


def draw_positions(key, part):
    key = jax.random.fold_in(key, 11)
    row_keys = jax.random.split(key, MB * ROWS)
    orders = jax.vmap(lambda row_key: jax.random.permutation(row_key, 2 * S))(row_keys)
    return orders.reshape(MB, ROWS, 2, S).transpose(0, 2, 1, 3).astype(jnp.int32)


def draw_lengths(key, part):
    key = jax.random.fold_in(key, 12)
    row_ids = jnp.arange(ROWS, dtype=jnp.int32)
    floor_len = S // 3
    base_len = floor_len + (S - floor_len) * row_ids // max(ROWS - 1, 1)
    jitter = jax.random.randint(key, (MB, 2, ROWS), 0, S // 8 + 1)
    chosen = jnp.clip(base_len[None, None, :] - jitter, 1, S)
    chosen = chosen.at[:, :, ROWS - 1].set(S)
    return chosen.astype(jnp.int32)


def draw_embedding(key, part):
    key = jax.random.fold_in(key, 13)
    block_rows = V // (N_GRP * N_DP * N_TENSOR)
    row_ids = jnp.arange(V, dtype=jnp.int32)
    owner = (row_ids // block_rows % N_TENSOR).astype(jnp.float32) / max(N_TENSOR - 1, 1)
    ramp_up = row_ids.astype(jnp.float32) / V
    entries = jax.random.normal(key, (V, D), jnp.float32)
    scaling = (1.0 + 2.0 * owner) * (0.9 + 0.2 * ramp_up)
    return jnp.clip(entries * (scaling / math.sqrt(D))[:, None], -1.0, 1.0)


def draw_norm_gains(key, part):
    key = jax.random.fold_in(key, 14)
    gain_key, bias_key = jax.random.split(key)
    ramp_up = jnp.arange(D, dtype=jnp.float32) / D
    noise = jnp.clip(jax.random.normal(gain_key, (2 * L + 1, D), jnp.float32), -4.0, 4.0)
    biases = 0.1 * jnp.clip(jax.random.normal(bias_key, (2 * L + 1, D), jnp.float32), -4.0, 4.0)
    gains_part = (0.6 + 1.2 * ramp_up)[None, :] * (1.0 + 0.1 * noise)
    return jnp.stack([gains_part, biases], 1)


def place_ends(values, own_key, smallest, largest):
    index_at = [jax.random.randint(jax.random.fold_in(own_key, axis), (), 0, length) for axis, length in enumerate(values.shape)]
    widest = values.shape.index(max(values.shape))
    neighbour = index_at[:widest] + [(index_at[widest] + 1) % values.shape[widest]] + index_at[widest + 1:]
    return values.at[tuple(index_at)].set(smallest).at[tuple(neighbour)].set(largest)


def shard_levels(key, extent, cuts, low, largest):
    loudness = 1.0
    for dim, blocks in cuts:
        steps = jax.random.uniform(jax.random.fold_in(jax.random.fold_in(key, 6), dim), (blocks,), jnp.float32, low / len(cuts), largest / len(cuts))
        loudness = loudness * jnp.repeat(jnp.exp(steps), extent[dim] // blocks).reshape((-1,) + (1,) * (len(extent) - 1 - dim))
    return loudness


def rank_bounds(amount, lean):
    weights = [(1 << 20) // math.isqrt(grade ** lean) + 1 for grade in range(1, amount + 1)]
    scale = 1 + sum(weights) // (1 << 30)
    return np.cumsum(np.array([max(1, weight // scale) for weight in weights]))


def ranked(key, dims, number_of, slope):
    listing = rank_bounds(number_of, slope)
    ticket = jax.random.randint(jax.random.fold_in(key, 1), dims, 0, int(listing[number_of - 1]))
    rank = jnp.searchsorted(jnp.asarray(listing, jnp.int32), ticket, side="right")
    return jax.random.permutation(jax.random.fold_in(key, 2), number_of)[rank].astype(jnp.int32)


def centred(own_key, extent, scale, bound, shards=(), kind=jnp.bfloat16):
    drawn = scale * jax.random.normal(own_key, extent, jnp.float32)
    if shards:
        drawn = drawn * shard_levels(own_key, extent, shards, -0.22, 0.18)
    return jnp.clip(drawn, -bound, bound).astype(kind)


def setup_inputs(seed: int = 0) -> dict:
    splits = jax.random.split(jax.random.key(seed), 22)
    return {
        "tokens": place_ends(ranked(splits[0], (MB, 2, ROWS, S), V - 1, 2), jax.random.fold_in(splits[0], 3), 0, (V - 1) - 1).astype(jnp.int32),
        "positions": draw_positions(jax.random.fold_in(splits[21], 71), 0),
        "lengths": draw_lengths(jax.random.fold_in(splits[21], 71), 0),
        "embedding": draw_embedding(jax.random.fold_in(splits[21], 71), 0),
        "embedding_mom": centred(splits[4], (V, D), (0.05 * (V * D + 12 * L * D * D) ** -0.5), 3.814697265625e-05, ((0, 32),), jnp.float32),
        "embedding_avg": centred(splits[5], (V, D), D ** -0.5, 0.21875, ((0, 32),), jnp.float32),
        "qkv_w": centred(splits[6], (L, D, 3, D), D ** -0.5, 0.21875, ((1, 8), (3, 4)), jnp.float32),
        "qkv_mom": centred(splits[7], (L, D, 3, D), (0.05 * (V * D + 12 * L * D * D) ** -0.5), 3.814697265625e-05, ((1, 8), (3, 4)), jnp.float32),
        "qkv_avg": centred(splits[8], (L, D, 3, D), D ** -0.5, 0.21875, ((1, 8), (3, 4)), jnp.float32),
        "out_w": centred(splits[9], (L, D, D), (D * 16 // S) ** -0.5, 1.25, ((1, 4), (2, 8)), jnp.float32),
        "out_mom": centred(splits[10], (L, D, D), (0.05 * (V * D + 12 * L * D * D) ** -0.5), 3.814697265625e-05, ((1, 4), (2, 8)), jnp.float32),
        "out_avg": centred(splits[11], (L, D, D), (D * 16 // S) ** -0.5, 1.25, ((1, 4), (2, 8)), jnp.float32),
        "up_w": centred(splits[12], (L, D, FF), D ** -0.5, 0.21875, ((1, 8), (2, 4)), jnp.float32),
        "up_mom": centred(splits[13], (L, D, FF), (0.05 * (V * D + 12 * L * D * D) ** -0.5), 3.814697265625e-05, ((1, 8), (2, 4)), jnp.float32),
        "up_avg": centred(splits[14], (L, D, FF), D ** -0.5, 0.21875, ((1, 8), (2, 4)), jnp.float32),
        "down_w": centred(splits[15], (L, FF, D), FF ** -0.5, 0.109375, ((1, 4), (2, 8)), jnp.float32),
        "down_mom": centred(splits[16], (L, FF, D), (0.05 * (V * D + 12 * L * D * D) ** -0.5), 3.814697265625e-05, ((1, 4), (2, 8)), jnp.float32),
        "down_avg": centred(splits[17], (L, FF, D), FF ** -0.5, 0.109375, ((1, 4), (2, 8)), jnp.float32),
        "norm_gains": draw_norm_gains(jax.random.fold_in(splits[21], 71), 0),
        "gains_mom": centred(splits[19], (2 * L + 1, 2, D), (0.25 * (V * D + 12 * L * D * D) ** -0.5), 0.00021362305, (), jnp.float32),
        "gains_avg": jnp.clip(1.0 + 0.1 * jax.random.normal(splits[20], (2 * L + 1, 2, D), jnp.float32), 0.5, 1.5),
    }


epsilon = 1e-05
threshold = 0.05
momentum = 0.9
average_decay = 0.75
rate_matrix = 2000.0
rate_gains = 5000.0
far_below = -1e+30
highest = lax.Precision.HIGHEST

@jax.custom_vjp
def low(v):
    return lax.optimization_barrier(v.astype(jnp.bfloat16)).astype(jnp.float32)

@jax.custom_vjp
def low_back(v):
    return v

def low_keep(v):
    return (low(v), None)

def low_pass(kept, grad):
    return (grad,)

def back_keep(v):
    return (v, None)

def back_low(kept, grad):
    return (low(grad),)
low.defvjp(low_keep, low_pass)
low_back.defvjp(back_keep, back_low)

def layer_norm(values, gain, bias):
    centre = values - lax.optimization_barrier(jnp.mean(values, -1, keepdims=True))
    spread = lax.optimization_barrier(jnp.mean(centre * centre, -1, keepdims=True))
    return centre * lax.rsqrt(spread + epsilon) * gain + bias

def rope_tables(places):
    half_size = HEAD // 2
    frequency = 10000.0 ** (-jnp.arange(half_size).astype(jnp.float32) / half_size)
    angles = places.reshape(-1).astype(jnp.float32)[:, None] * frequency[None, :]
    return (jnp.cos(angles)[:, None, :], jnp.sin(angles)[:, None, :])

def rotate(values, cosine, sine):
    half_size = values.shape[-1] // 2
    leading = values[..., :half_size]
    trailing = values[..., half_size:]
    return jnp.concatenate([leading * cosine - trailing * sine, trailing * cosine + leading * sine], -1)

def project(stream, layer_gains, attn_mat, cosine, sine):
    normed = low(layer_norm(stream, layer_gains[0, 0], layer_gains[0, 1]))
    projected = low_back(jnp.einsum('nd,dce->nce', normed, attn_mat, precision=highest))
    shaped = projected.reshape(S, 3, HEADS, HEAD)
    queries = low(rotate(shaped[:, 0], cosine, sine))
    keys_out = low(rotate(shaped[:, 1], cosine, sine))
    values_out = low(shaped[:, 2])
    return (queries, keys_out, values_out)

def attend(queries, keys_in, values_in, allowed):
    raw = low_back(jnp.einsum('qhd,khd->hqk', queries, keys_in, precision=highest) * HEAD ** (-0.5))
    masked = jnp.where(allowed[None], raw, far_below)
    row_top = lax.optimization_barrier(jnp.max(masked, -1, keepdims=True))
    expos = jnp.exp(masked - row_top)
    probs = expos / lax.optimization_barrier(jnp.sum(expos, -1, keepdims=True))
    mixed = jnp.einsum('hqk,khd->qhd', low(probs), values_in, precision=highest)
    return mixed.reshape(S, D)

def finish(stream, mixed, layer_gains, proj_mat, upper_mat, lower_mat):
    mixed_low = low(low_back(mixed))
    stream = stream + low_back(jnp.dot(mixed_low, proj_mat, precision=highest))
    normed = low(layer_norm(stream, layer_gains[1, 0], layer_gains[1, 1]))
    hidden = low_back(jnp.dot(normed, upper_mat, precision=highest))
    active = low(jax.nn.gelu(hidden))
    return stream + low_back(jnp.dot(active, lower_mat, precision=highest))

def row_loss(low_weights, norm_gains, clean_ids, target_ids, clean_pos, masked_pos, clean_len, masked_len):
    embedding, qkv_w, out_w, up_w, down_w = low_weights
    clean_x = low_back(embedding[clean_ids])
    masked_x = low_back(jnp.broadcast_to(embedding[V - 1], (S, D)))
    key_ids = jnp.arange(S)
    clean_keys = jnp.broadcast_to((key_ids < clean_len)[None, :], (S, S))
    clean_mask = clean_keys
    masked_mask = jnp.concatenate([clean_keys, jnp.eye(S, dtype=bool)], 1)
    cos_clean, sin_clean = rope_tables(clean_pos)
    cos_masked, sin_masked = rope_tables(masked_pos)
    for layer_index in range(L):
        layer_gains = norm_gains[2 * layer_index:2 * layer_index + 2]
        q_clean, k_clean, v_clean = project(clean_x, layer_gains, qkv_w[layer_index], cos_clean, sin_clean)
        q_masked, k_masked, v_masked = project(masked_x, layer_gains, qkv_w[layer_index], cos_masked, sin_masked)
        mixed_clean = attend(q_clean, k_clean, v_clean, clean_mask)
        mixed_masked = attend(q_masked, jnp.concatenate([k_clean, k_masked], 0), jnp.concatenate([v_clean, v_masked], 0), masked_mask)
        clean_x = finish(clean_x, mixed_clean, layer_gains, out_w[layer_index], up_w[layer_index], down_w[layer_index])
        masked_x = finish(masked_x, mixed_masked, layer_gains, out_w[layer_index], up_w[layer_index], down_w[layer_index])
    final = low(layer_norm(masked_x, norm_gains[2 * L, 0], norm_gains[2 * L, 1]))
    logits = low_back(jnp.dot(final, embedding.T, precision=highest))
    row_top = lax.optimization_barrier(jnp.max(logits, -1, keepdims=True))
    log_total = row_top[:, 0] + jnp.log(lax.optimization_barrier(jnp.sum(jnp.exp(logits - row_top), -1)))
    picked = jnp.take_along_axis(logits, target_ids[:, None], 1)[:, 0]
    return jnp.sum(jnp.where(key_ids < masked_len, log_total - picked, 0.0))

def total_loss(weights, norm_gains, tokens, positions, lengths):
    low_weights = tuple((low(part) for part in weights))
    row_total = tokens.shape[0] * tokens.shape[2]
    streams = (tokens[:, 0].reshape(row_total, S), tokens[:, 1].reshape(row_total, S), positions[:, 0].reshape(row_total, S), positions[:, 1].reshape(row_total, S), lengths[:, 0].reshape(row_total), lengths[:, 1].reshape(row_total))

    def row_step(carried, row_data):
        return (carried + row_loss(low_weights, norm_gains, *row_data), None)
    summed, unused = lax.scan(jax.checkpoint(row_step), jnp.zeros((), jnp.float32), streams)
    return summed

def update(weight, moment, average, grad, rate):
    fresh_mom = momentum * moment + grad
    fresh_w = weight - rate * (grad + momentum * fresh_mom)
    fresh_avg = average_decay * average + (1.0 - average_decay) * fresh_w
    return (fresh_mom, fresh_w, fresh_avg)

def reference(tokens, positions, lengths, embedding, embedding_mom, embedding_avg, qkv_w, qkv_mom, qkv_avg, out_w, out_mom, out_avg, up_w, up_mom, up_avg, down_w, down_mom, down_avg, norm_gains, gains_mom, gains_avg):

    def objective(matrices, gain_table):
        return total_loss(matrices, gain_table, tokens, positions, lengths)
    loss_sum, pullback = jax.vjp(objective, (embedding, qkv_w, out_w, up_w, down_w), norm_gains)
    grad_mats, grad_gains = pullback(jnp.ones_like(loss_sum))
    mask_count = jnp.sum(lengths[:, 1]).astype(jnp.float32)
    squares = jnp.sum(grad_gains * grad_gains)
    for part in grad_mats:
        squares = squares + jnp.sum(part * part)
    grad_norm = jnp.sqrt(squares) / mask_count
    factor = jnp.minimum(1.0, threshold / grad_norm) / mask_count
    e_mom, e_new, e_avg = update(embedding, embedding_mom, embedding_avg, grad_mats[0] * factor, rate_matrix)
    q_mom, q_new, q_avg = update(qkv_w, qkv_mom, qkv_avg, grad_mats[1] * factor, rate_matrix)
    o_mom, o_new, o_avg = update(out_w, out_mom, out_avg, grad_mats[2] * factor, rate_matrix)
    u_mom, u_new, u_avg = update(up_w, up_mom, up_avg, grad_mats[3] * factor, rate_matrix)
    d_mom, d_new, d_avg = update(down_w, down_mom, down_avg, grad_mats[4] * factor, rate_matrix)
    g_mom, g_new, g_avg = update(norm_gains, gains_mom, gains_avg, grad_gains * factor, rate_gains)
    return (loss_sum, mask_count, grad_norm, e_mom, e_new, e_avg, q_mom, q_new, q_avg, o_mom, o_new, o_avg, u_mom, u_new, u_avg, d_mom, d_new, d_avg, g_mom, g_new, g_avg)
```

```python
import jax
import jax.numpy as jnp
from jax import lax
from jax.sharding import Mesh
from jax.sharding import PartitionSpec as P

HEAD = 64
CAPACITY = 16

epsilon = 1e-05
threshold = 0.05
momentum = 0.9
average_decay = 0.75
rate_matrix = 2000.0
rate_gains = 5000.0
far_below = -1e30
bf16 = jnp.bfloat16
f32 = jnp.float32
ALL = ("grp", "y", "core", "tensor")
OWNERS = ("tensor", "grp", "y", "core")


def layer_norm(values, gain, bias):
    centre = values - jnp.mean(values, -1, keepdims=True)
    spread = jnp.mean(centre * centre, -1, keepdims=True)
    return centre * lax.rsqrt(spread + epsilon) * gain + bias


def norm_back(values, gain, bias, upstream):
    unused, pullback = jax.vjp(layer_norm, values, gain, bias)
    return pullback(upstream)


def rope_tables(places):
    half_size = HEAD // 2
    frequency = 10000.0 ** (-jnp.arange(half_size).astype(f32) / half_size)
    angles = places.reshape(-1).astype(f32)[:, None] * frequency[None, :]
    return (jnp.cos(angles)[:, None, :], jnp.sin(angles)[:, None, :])


def rotate(values, cosine, sine):
    half_size = values.shape[-1] // 2
    leading = values[..., :half_size]
    trailing = values[..., half_size:]
    return jnp.concatenate(
        [leading * cosine - trailing * sine, trailing * cosine + leading * sine], -1
    )


def dot(form, left, right):
    return jnp.einsum(form, left, right, preferred_element_type=f32)


def gather_weights(shards):
    everything = lax.all_gather(shards, OWNERS, axis=0, tiled=False)
    count = lax.axis_size("tensor")
    kinds, rows, width = shards.shape
    everything = everything.reshape(count, -1, kinds, rows, width)
    return everything.transpose(2, 0, 1, 3, 4).reshape(kinds, count, -1, width)


def flip(values, axis, bit):
    size = lax.axis_size(axis)
    return lax.ppermute(values, axis, [(i, i ^ bit) for i in range(size)])


def halve(values, axis, dim):
    mine = lax.axis_index(axis)
    keep = lax.dynamic_index_in_dim(values, mine, dim, keepdims=False)
    send = lax.dynamic_index_in_dim(values, 1 - mine, dim, keepdims=False)
    return (keep.astype(f32) + flip(send, axis, 1).astype(f32)).astype(bf16)


def scatter_grads(grads):
    kinds, count, width, unused = grads.shape
    if lax.axis_size("grp") != 2 or lax.axis_size("y") != 2:
        owners = lax.axis_size(("grp", "y", "core"))
        blocks = grads.reshape(kinds, count, owners, width // owners, width).transpose(1, 2, 0, 3, 4)
        return lax.psum_scatter(blocks, OWNERS, scatter_dimension=0, tiled=False) if False else (
            lax.psum_scatter(
                blocks.reshape((count * owners,) + blocks.shape[2:]),
                OWNERS, scatter_dimension=0, tiled=False,
            ).astype(f32)
        )
    rows = width // 8
    blocks = grads.reshape(kinds, count, 2, 2, 2, rows, width)
    blocks = halve(blocks, "core", 4)
    first, second = blocks[:, : count // 2], blocks[:, count // 2 :]
    first, second = halve(first, "grp", 2), halve(second, "y", 3)
    first, second = halve(first, "y", 2), halve(second, "grp", 2)
    blocks = jnp.concatenate([first, second], 1)
    parts = lax.all_to_all(blocks.transpose(1, 0, 2, 3), "tensor", 0, 0, tiled=True)
    return jnp.sum(parts.astype(f32), 0)


def head_shape(values):
    return values.reshape(values.shape[0], -1, HEAD)


def layer_forward(x, weights, gains, context):
    attn, upper, lower = weights
    cosine, sine, clean_len = context
    width = x.shape[1]
    part = width // attn.shape[0]
    clean = x.shape[0] // 2
    h = layer_norm(x, gains[0, 0], gains[0, 1]).astype(bf16)
    z = dot("nd,tdf->ntf", h, attn[:, :, : 3 * part])
    q = rotate(head_shape(z[:, :, :part]), cosine, sine).astype(bf16)
    k = rotate(head_shape(z[:, :, part : 2 * part]), cosine, sine).astype(bf16)
    v = head_shape(z[:, :, 2 * part :]).astype(bf16)
    both = lax.all_gather(
        jnp.stack([k[:clean], v[:clean]], 1), ("grp", "core"), axis=0, tiled=True
    )
    keys, values = both[:, 0], both[:, 1]
    state = (q, k, v, keys, values)
    score, alone = scores(state, clean_len)
    top = jnp.maximum(jnp.max(score, -1), alone)
    total = jnp.sum(jnp.exp(score - top[..., None]), -1) + jnp.exp(alone - top)
    log_total = top + jnp.log(total)
    prob = jnp.exp(score - log_total[..., None]).astype(bf16)
    prob_alone = jnp.exp(alone - log_total).astype(bf16)
    o = dot("hqk,khd->qhd", prob, values)
    o = o + (prob_alone.T.astype(f32))[..., None] * v.astype(f32)
    o = o.astype(bf16).reshape(x.shape[0], attn.shape[0], part)
    mid = x + dot("nte,tde->nd", o, attn[:, :, 3 * part :])
    h2 = layer_norm(mid, gains[1, 0], gains[1, 1]).astype(bf16)
    u = dot("nd,tdf->ntf", h2, upper)
    a = jax.nn.gelu(u).astype(bf16)
    out = mid + dot("ntf,tdf->nd", a, lower)
    return out, (x, h, state, log_total, o, mid, h2, u, a)


def scores(state, clean_len):
    q, k, v, keys, values = state
    scale = HEAD ** (-0.5)
    seen = jnp.arange(keys.shape[0]) < clean_len
    score = jnp.where(seen, dot("qhd,khd->hqk", q, keys) * scale, far_below)
    alone = jnp.sum(q.astype(f32) * k.astype(f32), -1).T * scale
    masked = jnp.arange(q.shape[0]) >= q.shape[0] // 2
    return score, jnp.where(masked, alone, far_below)


def layer_backward(grad_out, saved, weights, gains, context):
    x, h, state, log_total, o, mid, h2, u, a = saved
    q, k, v, keys, values = state
    attn, upper, lower = weights
    cosine, sine, clean_len = context
    width = x.shape[1]
    part = width // attn.shape[0]
    clean = x.shape[0] // 2
    scale = HEAD ** (-0.5)
    grad_low = grad_out.astype(bf16)
    grad_lower = dot("nd,ntf->tdf", grad_low, a)
    grad_a = dot("nd,tdf->ntf", grad_low, lower)
    unused, gelu_pull = jax.vjp(jax.nn.gelu, u)
    grad_u = gelu_pull(grad_a)[0].astype(bf16)
    grad_upper = dot("nd,ntf->tdf", h2, grad_u)
    back, gain_mid, bias_mid = norm_back(
        mid, gains[1, 0], gains[1, 1], dot("ntf,tdf->nd", grad_u, upper)
    )
    grad_mid = grad_out + back
    mid_low = grad_mid.astype(bf16)
    grad_proj = dot("nd,nte->tde", mid_low, o)
    grad_o = head_shape(dot("nd,tde->nte", mid_low, attn[:, :, 3 * part :])).astype(bf16)
    score, alone = scores(state, clean_len)
    prob = jnp.exp(score - log_total[..., None])
    prob_alone = jnp.exp(alone - log_total)
    dprob = dot("qhd,khd->hqk", grad_o, values)
    dalone = jnp.sum(grad_o.astype(f32) * v.astype(f32), -1).T
    delta = jnp.sum(dprob * prob, -1) + dalone * prob_alone
    dscore = (prob * (dprob - delta[..., None])).astype(bf16)
    dself = (prob_alone * (dalone - delta)).astype(bf16).astype(f32).T[..., None] * scale
    grad_q = dot("hqk,khd->qhd", dscore, keys) * scale + dself * k.astype(f32)
    grad_keys = dot("hqk,qhd->khd", dscore, q) * scale
    grad_values = dot("hqk,qhd->khd", prob.astype(bf16), grad_o)
    own_k = dself * q.astype(f32)
    own_v = prob_alone.astype(bf16).astype(f32).T[..., None] * grad_o.astype(f32)
    both = lax.psum_scatter(
        jnp.stack([grad_keys, grad_values], 1).astype(bf16),
        ("grp", "core"), scatter_dimension=0, tiled=True,
    ).astype(f32)
    grad_k = own_k.at[:clean].add(both[:, 0])
    grad_v = own_v.at[:clean].add(both[:, 1])

    def flat(values):
        return values.reshape(x.shape[0], attn.shape[0], part)

    grad_z = jnp.concatenate(
        [
            flat(rotate(grad_q, cosine, -sine)),
            flat(rotate(grad_k, cosine, -sine)),
            flat(grad_v),
        ],
        2,
    ).astype(bf16)
    grad_attn = dot("nd,ntf->tdf", h, grad_z)
    grad_h = dot("ntf,tdf->nd", grad_z, attn[:, :, : 3 * part])
    back, gain_in, bias_in = norm_back(x, gains[0, 0], gains[0, 1], grad_h)
    gain_grad = jnp.stack([jnp.stack([gain_in, bias_in]), jnp.stack([gain_mid, bias_mid])])
    grads = jnp.stack(
        [
            jnp.concatenate([grad_attn, grad_proj], 2).astype(bf16),
            grad_upper.astype(bf16),
            grad_lower.astype(bf16),
        ]
    )
    return grad_mid + back, grads, gain_grad


def update(weight, moment, average, grad, rate):
    fresh_mom = momentum * moment + grad
    fresh_w = weight - rate * (grad + momentum * fresh_mom)
    fresh_avg = average_decay * average + (1.0 - average_decay) * fresh_w
    return (fresh_mom, fresh_w, fresh_avg)


def lookup_plan(ids, block_rows):
    slots = ids.shape[1]
    owner = ids // block_rows
    order = jnp.arange(slots)
    same = ids[:, :, None] == ids[:, None, :]
    lead = jnp.min(jnp.where(same, order[None, None, :], slots), -1)
    first = lead == order
    ahead = jnp.logical_and(
        jnp.logical_and(first[:, None, :], owner[:, :, None] == owner[:, None, :]),
        order[None, None, :] < lead[:, :, None],
    )
    place = jnp.sum(ahead.astype(jnp.int32), -1)
    return owner, place, first


def per_device(
    tokens, positions, lengths,
    embedding, embedding_mom, embedding_avg,
    qkv_w, qkv_mom, qkv_avg,
    out_w, out_mom, out_avg,
    up_w, up_mom, up_avg,
    down_w, down_mom, down_avg,
    norm_gains, gains_mom, gains_avg,
):
    n_grp, n_y, n_t = lax.axis_size("grp"), lax.axis_size("y"), lax.axis_size("tensor")
    devices = 2 * n_grp * n_y * n_t
    at_grp, at_y, at_core, at_t = (lax.axis_index(name) for name in ALL)
    me = lax.axis_index(ALL)
    block_rows, width = embedding.shape
    layers = qkv_w.shape[0]
    micros, unused, rows_here, seq = tokens.shape
    rows = rows_here * 2 * n_y
    span = seq // (2 * n_grp)
    my_row = at_y * n_t + at_t
    my_part = at_grp * 2 + at_core

    packed = jnp.concatenate(
        [tokens, positions, jnp.broadcast_to(lengths[..., None], lengths.shape + (128,))], -1
    )
    packed = lax.all_gather(packed, ("y", "core"), axis=2, tiled=True)
    packed = packed.transpose(1, 0, 2, 3).reshape(2, micros * rows, -1)
    ids_all, places_all, lens_all = packed[..., :seq], packed[..., seq : 2 * seq], packed[..., -1]

    def by_device(table):
        split = table.reshape(n_y, n_t, n_grp, 2, span)
        return split.transpose(2, 0, 3, 1, 4).reshape(devices, span)

    lens = lax.dynamic_index_in_dim(lens_all, my_row, 1, keepdims=False)
    clean_len, masked_len = lens[0], lens[1]
    places = lax.dynamic_slice(places_all, (0, my_row, my_part * span), (2, 1, span))
    cosine, sine = rope_tables(places)
    context = (cosine, sine, clean_len)

    shards = []
    for layer in range(layers):
        shards += [
            jnp.concatenate([qkv_w[layer].reshape(qkv_w.shape[1], -1), out_w[layer].T], 1),
            up_w[layer],
            down_w[layer].T,
        ]
    gathered = gather_weights(jnp.stack(shards).astype(bf16))
    weights = [tuple(gathered[3 * layer + kind] for kind in range(3)) for layer in range(layers)]
    table = embedding.astype(bf16)

    mask_id = block_rows * devices - 1
    wanted = jnp.concatenate(
        [by_device(ids_all[0]), jnp.full((devices, 1), mask_id, jnp.int32)], 1
    )
    owner, place, first = lookup_plan(wanted, block_rows)
    rounds = jnp.max(place) // CAPACITY + 1
    mine = jnp.logical_and(first, owner == me)
    local = wanted - me * block_rows
    my_owner = lax.dynamic_index_in_dim(owner, me, 0, keepdims=False)
    my_place = lax.dynamic_index_in_dim(place, me, 0, keepdims=False)
    my_slot = my_owner * CAPACITY + my_place
    my_slot = jnp.concatenate([my_slot[:span], jnp.broadcast_to(my_slot[span:], (span,))])
    my_place = jnp.concatenate([my_place[:span], jnp.broadcast_to(my_place[span:], (span,))])

    def sent_rows(step):
        at = place - step * CAPACITY
        hit = jnp.logical_and(mine[:, None, :], at[:, None, :] == jnp.arange(CAPACITY)[None, :, None])
        row = jnp.sum(jnp.where(hit, local[:, None, :] + 1, 0), -1).reshape(-1) - 1
        return (row[:, None] == jnp.arange(block_rows)[None, :]).astype(bf16)

    def used_rows(step):
        slot = my_slot - step * CAPACITY
        inside = jnp.logical_and(my_place >= step * CAPACITY, my_place < (step + 1) * CAPACITY)
        slot = jnp.where(inside, slot, -1)
        return (slot[:, None] == jnp.arange(devices * CAPACITY)[None, :]).astype(bf16)

    def swap(values):
        return lax.all_to_all(values, ALL, 0, 0, tiled=True)

    def look(step):
        sent = dot("kv,vd->kd", sent_rows(step), table).astype(bf16)
        return dot("nk,kd->nd", used_rows(step), swap(sent))

    def look_back(step, grad):
        sent = dot("nk,nd->kd", used_rows(step), grad).astype(bf16)
        return dot("kv,kd->vd", sent_rows(step), swap(sent))

    def more(step_fn, begin):
        return lax.while_loop(
            lambda carry: carry[0] < rounds,
            lambda carry: (carry[0] + 1, carry[1] + step_fn(carry[0])),
            (jnp.int32(1), begin),
        )[1]

    x = more(look, look(0))

    kept = []
    for layer in range(layers):
        x, saved = layer_forward(x, weights[layer], norm_gains[2 * layer : 2 * layer + 2], context)
        kept.append(saved)

    last = x[span:]
    f_mine = layer_norm(last, norm_gains[2 * layers, 0], norm_gains[2 * layers, 1]).astype(bf16)
    f_all = lax.all_gather(f_mine, ALL, axis=0, tiled=True)
    targets = by_device(ids_all[1]).reshape(-1) - me * block_rows
    valid_all = by_device(
        (jnp.arange(seq)[None, :] < lens_all[1][:, None]).astype(jnp.int32)
    ).reshape(-1) > 0
    logits = dot("nd,vd->nv", f_all, table)
    top = jnp.max(logits, -1)
    part_total = top + jnp.log(jnp.sum(jnp.exp(logits - top[:, None]), -1))
    parts = lax.all_to_all(
        jnp.broadcast_to(part_total, (devices,) + part_total.shape), ALL, 0, 0, tiled=True
    )
    top = jnp.max(parts, 0)
    log_total = top + jnp.log(jnp.sum(jnp.exp(parts - top), 0))
    onehot = targets[:, None] == jnp.arange(block_rows)[None, :]
    target_part = jnp.sum(jnp.where(jnp.logical_and(onehot, valid_all[:, None]), logits, 0.0))
    own_total = lax.dynamic_slice(log_total, (me * span,), (span,))
    own_valid = my_part * span + jnp.arange(span) < masked_len
    loss_part = jnp.sum(jnp.where(own_valid, own_total, 0.0)) - target_part
    grad_logits = jnp.where(
        valid_all[:, None], jnp.exp(logits - log_total[:, None]) - onehot, 0.0
    ).astype(bf16)
    grad_f = dot("nv,vd->nd", grad_logits, table).astype(bf16)
    grad_f = lax.psum_scatter(grad_f, ALL, scatter_dimension=0, tiled=True).astype(f32)
    grad_table = dot("nv,nd->vd", grad_logits, f_all)

    back, gain_final, bias_final = norm_back(
        last, norm_gains[2 * layers, 0], norm_gains[2 * layers, 1], grad_f
    )
    grad_x = jnp.concatenate([jnp.zeros_like(back), back], 0)
    gain_parts, owned = [None] * layers, [None] * layers
    for layer in reversed(range(layers)):
        grad_x, grads, gain_parts[layer] = layer_backward(
            grad_x, kept[layer], weights[layer], norm_gains[2 * layer : 2 * layer + 2], context
        )
        owned[layer] = scatter_grads(grads)

    grad_low = grad_x.astype(bf16)
    grad_table = more(lambda step: look_back(step, grad_low), grad_table + look_back(0, grad_low))

    gains_grad = jnp.concatenate(gain_parts + [jnp.stack([gain_final, bias_final])[None]], 0)
    loss_sum, gains_total = lax.psum((loss_part, gains_grad), ALL)
    mask_count = jnp.sum(lens_all[1]).astype(f32)
    squares = jnp.sum(grad_table * grad_table)
    for part in owned:
        squares = squares + jnp.sum(part * part)
    squares = lax.psum(squares, ALL) + jnp.sum(gains_total * gains_total)
    grad_norm = jnp.sqrt(squares) / mask_count
    factor = jnp.minimum(1.0, threshold / grad_norm) / mask_count

    third = 3 * out_w.shape[1]
    qkv_grad = jnp.stack([part[0, :, :third].reshape(qkv_w.shape[1:]) for part in owned])
    out_grad = jnp.stack([part[0, :, third:].T for part in owned])
    up_grad = jnp.stack([part[1] for part in owned])
    down_grad = jnp.stack([part[2].T for part in owned])
    results = [loss_sum, mask_count, grad_norm]
    for weight, moment, average, grad, rate in (
        (embedding, embedding_mom, embedding_avg, grad_table, rate_matrix),
        (qkv_w, qkv_mom, qkv_avg, qkv_grad, rate_matrix),
        (out_w, out_mom, out_avg, out_grad, rate_matrix),
        (up_w, up_mom, up_avg, up_grad, rate_matrix),
        (down_w, down_mom, down_avg, down_grad, rate_matrix),
        (norm_gains, gains_mom, gains_avg, gains_total, rate_gains),
    ):
        results += update(weight, moment, average, grad * factor, rate)
    return tuple(results)


def solution(mesh):
    n_grp, n_dp, n_t = mesh.devices.shape
    split = Mesh(mesh.devices.reshape(n_grp, n_dp // 2, 2, n_t), ALL)
    dp = ("y", "core")
    owners = ("grp", "y", "core")
    rows = P(None, None, dp, None)
    table = P(ALL, None)
    wide = P(None, owners, None, "tensor")
    tall = P(None, "tensor", owners)
    flat = P(None, owners, "tensor")
    return jax.shard_map(
        per_device,
        mesh=split,
        in_specs=(rows, rows, P(None, None, dp))
        + (table,) * 3 + (wide,) * 3 + (tall,) * 3 + (flat,) * 3 + (tall,) * 3 + (P(),) * 3,
        out_specs=(P(),) * 3
        + (table,) * 3 + (wide,) * 3 + (tall,) * 3 + (flat,) * 3 + (tall,) * 3 + (P(),) * 3,
        check_vma=False,
    )
```

```python
import functools

import jax
import jax.numpy as jnp
from jax import lax
from jax.experimental import pallas as pl
from jax.experimental.pallas import tpu as pltpu
from jax.sharding import Mesh
from jax.sharding import PartitionSpec as P

HEAD = 64
CAPACITY = 16

epsilon = 1e-05
threshold = 0.05
momentum = 0.9
average_decay = 0.75
rate_matrix = 2000.0
rate_gains = 5000.0
far_below = -1e30
bf16 = jnp.bfloat16
f32 = jnp.float32
TENSOR = ("th", "tl")
ALL = ("grp", "y", "core", "th", "tl")
OWNERS = ("th", "tl", "grp", "y", "core")
HEAD_GROUP = ("grp", "y", "core", "th")


def layer_norm(values, gain, bias):
    centre = values - jnp.mean(values, -1, keepdims=True)
    spread = jnp.mean(centre * centre, -1, keepdims=True)
    return centre * lax.rsqrt(spread + epsilon) * gain + bias


def norm_back(values, gain, bias, upstream):
    unused, pullback = jax.vjp(layer_norm, values, gain, bias)
    return pullback(upstream)


def rope_tables(places):
    half_size = HEAD // 2
    lane = jnp.arange(TILE)
    frequency = 10000.0 ** (-(lane % half_size).astype(f32) / half_size)
    sign = jnp.where(lane % HEAD < half_size, -1.0, 1.0)
    angles = places.reshape(-1).astype(f32)[:, None] * frequency[None, :]
    return jnp.cos(angles), jnp.sin(angles) * sign


def dot(form, left, right):
    return jnp.einsum(form, left, right, preferred_element_type=f32)


def flip(values, axis):
    return lax.ppermute(values, axis, [(0, 1), (1, 0)])


def square_plane():
    return lax.axis_size("grp") == 2 and lax.axis_size("y") == 2


def coordinates():
    return jnp.stack([lax.axis_index("grp"), lax.axis_index("y"), lax.axis_index("core")])


def fence(*groups):
    return lax.optimization_barrier(groups)


def gather_whole(shards):
    kinds, rows, width = shards.shape
    everything = lax.all_gather(shards, OWNERS, axis=0, tiled=False)
    count = lax.axis_size(TENSOR)
    everything = everything.reshape(count, -1, kinds, rows, width)
    if rows % 16 == 0:
        return everything
    return everything.transpose(0, 2, 1, 3, 4).reshape(count, 1, kinds, -1, width)


def weight_grad_kernel(inputs, extra, at, *refs):
    xs, ys = refs[:inputs], refs[inputs : 2 * inputs]
    keep_ref, send_ref, turned, tile = refs[2 * inputs :]
    blocks, rows, width = tile.shape

    @pl.when(pl.program_id(0) == 0)
    def begin():
        for i in range(inputs):
            turned[i] = xs[i][...].T

    for kind in range(inputs - extra):
        grad = nn(turned[kind], ys[kind][...])
        if extra:
            more = nn(turned[1], ys[1][0])
            split = width - more.shape[1]
            grad = jnp.concatenate([grad[:, :split], grad[:, split:] + more], 1)
        tile[...] = grad.astype(bf16).reshape(blocks, rows, width)
        for by_x in range(2):
            for by_y in range(2):
                for core, ref in enumerate((keep_ref, send_ref)):
                    block = ((at[0] ^ by_x) * 2 + (at[1] ^ by_y)) * 2 + (at[2] ^ core)
                    ref[0, kind, by_x, by_y] = tile[block]


def weight_grads(pairs, extra=None):
    kinds = len(pairs)
    slots, width = pairs[0][0].shape
    count = pairs[0][1].shape[1] // width
    rows = width // 8
    if not square_plane():
        whole = [dot("nd,ntf->tdf", x, y.reshape(slots, count, width)) for x, y in pairs]
        if extra:
            more = dot("nd,tnf->tdf", *extra)
            whole[0] += jnp.pad(more, ((0, 0), (0, 0), (width - more.shape[2], 0)))
        return jnp.stack([part.astype(bf16) for part in whole], 1)
    part = pl.BlockSpec((1, kinds, 2, 2, rows, width), lambda t, at: (t, 0, 0, 0, 0, 0))
    shape = jax.ShapeDtypeStruct((count, kinds, 2, 2, rows, width), bf16)
    x_spec = pl.BlockSpec((slots, width), lambda t, at: (0, 0))
    x_specs = [x_spec] * kinds
    y_specs = [pl.BlockSpec((slots, width), lambda t, at: (0, t))] * kinds
    xs = [x for x, unused in pairs]
    ys = [y for unused, y in pairs]
    if extra:
        xs.append(extra[0])
        ys.append(extra[1])
        x_specs.append(x_spec)
        y_specs.append(pl.BlockSpec((1,) + extra[1].shape[1:], lambda t, at: (t, 0, 0)))
    return pl.pallas_call(
        functools.partial(weight_grad_kernel, len(xs), bool(extra)),
        grid_spec=pltpu.PrefetchScalarGridSpec(
            num_scalar_prefetch=1,
            grid=(count,),
            in_specs=x_specs + y_specs,
            out_specs=[part, part],
            scratch_shapes=[
                pltpu.VMEM((len(xs), width, slots), bf16),
                pltpu.VMEM((8, rows, width), bf16),
            ],
        ),
        out_shape=[shape, shape],
        compiler_params=pltpu.CompilerParams(vmem_limit_bytes=40 * 2**20),
        cost_estimate=pl.CostEstimate(
            flops=2 * slots * width * width * count * kinds,
            bytes_accessed=2 * count * kinds * width * (slots + width),
            transcendentals=0,
        ),
        name="weight_grads",
    )(coordinates(), *xs, *ys)


def plus(left, right):
    return (left.astype(f32) + right.astype(f32)).astype(bf16)


def add_first_kernel(own_low, own_high, got_low, got_high, low_keep, low_send, high_keep, high_send):
    low_keep[0] = plus(own_low[0, :, 0], got_low[0, :, 0])
    low_send[0] = plus(own_low[0, :, 1], got_low[0, :, 1])
    high_keep[0] = plus(own_high[0, :, :, 0], got_high[0, :, :, 0])
    high_send[0] = plus(own_high[0, :, :, 1], got_high[0, :, :, 1])


def add_first(own, got):
    count, kinds, unused, unused, rows, width = own.shape
    half = count // 2
    low = pl.BlockSpec((1, kinds, 2, 2, rows, width), lambda t: (t, 0, 0, 0, 0, 0))
    high = pl.BlockSpec((1, kinds, 2, 2, rows, width), lambda t: (t + half, 0, 0, 0, 0, 0))
    part = pl.BlockSpec((1, kinds, 2, rows, width), lambda t: (t, 0, 0, 0, 0))
    return pl.pallas_call(
        add_first_kernel,
        grid=(half,),
        in_specs=[low, high, low, high],
        out_specs=[part] * 4,
        out_shape=[jax.ShapeDtypeStruct((half, kinds, 2, rows, width), bf16)] * 4,
        compiler_params=pltpu.CompilerParams(vmem_limit_bytes=40 * 2**20),
        cost_estimate=pl.CostEstimate(flops=own.size, bytes_accessed=6 * own.size, transcendentals=0),
        name="add_first",
    )(own, own, got, got)


def add_second_kernel(low, low_got, high, high_got, low_keep, low_send, high_keep, high_send):
    low_keep[0] = plus(low[0, :, 0], low_got[0, :, 0])
    low_send[0] = plus(low[0, :, 1], low_got[0, :, 1])
    high_keep[0] = plus(high[0, :, 0], high_got[0, :, 0])
    high_send[0] = plus(high[0, :, 1], high_got[0, :, 1])


def add_second(low, low_got, high, high_got):
    half, kinds, unused, rows, width = low.shape
    part = pl.BlockSpec((1, kinds, 2, rows, width), lambda t: (t, 0, 0, 0, 0))
    out = pl.BlockSpec((1, kinds, rows, width), lambda t: (t, 0, 0, 0))
    return pl.pallas_call(
        add_second_kernel,
        grid=(half,),
        in_specs=[part] * 4,
        out_specs=[out] * 4,
        out_shape=[jax.ShapeDtypeStruct((half, kinds, rows, width), bf16)] * 4,
        compiler_params=pltpu.CompilerParams(vmem_limit_bytes=40 * 2**20),
        cost_estimate=pl.CostEstimate(flops=2 * low.size, bytes_accessed=12 * low.size, transcendentals=0),
        name="add_second",
    )(low, low_got, high, high_got)


def add_third_kernel(low, low_got, high, high_got, out):
    out[0, 0] = plus(low[0], low_got[0])
    out[1, 0] = plus(high[0], high_got[0])


def add_third(low, low_got, high, high_got):
    half, kinds, rows, width = low.shape
    part = pl.BlockSpec((1, kinds, rows, width), lambda t: (t, 0, 0, 0))
    out = pl.pallas_call(
        add_third_kernel,
        grid=(half,),
        in_specs=[part] * 4,
        out_specs=pl.BlockSpec((2, 1, kinds, rows, width), lambda t: (0, t, 0, 0, 0)),
        out_shape=jax.ShapeDtypeStruct((2, half, kinds, rows, width), bf16),
        compiler_params=pltpu.CompilerParams(vmem_limit_bytes=40 * 2**20),
        cost_estimate=pl.CostEstimate(flops=2 * low.size, bytes_accessed=12 * low.size, transcendentals=0),
        name="add_third",
    )(low, low_got, high, high_got)
    return out.reshape(2 * half, kinds, rows, width)


class Scatter:
    def __init__(self, grads=None):
        self.plane = square_plane() and grads is not None
        self.keep = self.sent = self.line = ()
        self.moving = () if grads is None else grads
        if self.plane:
            self.keep, send = grads
            self.moving = flip(send, "core")

    def first(self):
        if self.plane:
            low, low_send, high, high_send = add_first(self.keep, self.moving)
            self.keep, self.sent = (low, high), (low_send, high_send)

    def start(self):
        if self.plane:
            self.moving = (flip(self.sent[0], "grp"), flip(self.sent[1], "y"))

    def second(self):
        if self.plane:
            (low, high), (low_got, high_got) = self.keep, self.moving
            low, low_send, high, high_send = add_second(low, low_got, high, high_got)
            self.keep, self.sent = (low, high), (low_send, high_send)

    def restart(self):
        if self.plane:
            self.moving = (flip(self.sent[0], "y"), flip(self.sent[1], "grp"))

    def third(self, swapped=False):
        if self.plane:
            (low, high), (low_got, high_got) = self.keep, self.moving
            self.line = add_third(low, low_got, high, high_got)
            if swapped:
                parts = lax.all_to_all(self.line, TENSOR, 0, 0, tiled=True)
                self.moving = jnp.sum(parts.astype(f32), 0)
            else:
                self.moving = lax.psum_scatter(self.line, TENSOR, scatter_dimension=0, tiled=False)
        elif not isinstance(self.moving, tuple):
            count, kinds, width, unused = self.moving.shape
            owners = lax.axis_size(("grp", "y", "core"))
            blocks = self.moving.reshape(count, kinds, owners, width // owners, width)
            blocks = blocks.transpose(0, 2, 1, 3, 4).reshape(count * owners, kinds, -1, width)
            self.moving = lax.psum_scatter(blocks, OWNERS, scatter_dimension=0, tiled=False)

    def sums(self):
        return self.moving.astype(f32)


def table_grads(grad_logits, rows, split):
    whole = dot("nv,nd->vd", grad_logits, rows)
    return whole[:split], whole[split:].astype(bf16)


def gather_keys(own):
    far = flip(own, "grp")
    near = flip(own, "core")
    return own, near, far, flip(far, "core")


def gather_head(own):
    if not square_plane():
        return lax.all_gather(own, HEAD_GROUP, axis=0, tiled=True)
    half = own.shape[0] // 2
    line = jnp.stack([own, flip(own, "th")])
    low, high = line[:, :half], line[:, half:]
    low = jnp.stack([low, flip(low, "grp")])
    high = jnp.stack([high, flip(high, "y")])
    low = jnp.stack([low, flip(low, "y")])
    high = jnp.stack([high, flip(high, "grp")])
    plane = jnp.stack([low, high])
    return jnp.stack([plane, flip(plane, "core")]).reshape(-1, own.shape[1])


def scatter_head(grad):
    if not square_plane():
        return lax.psum_scatter(grad, HEAD_GROUP, scatter_dimension=0, tiled=True).astype(f32)
    width = grad.shape[1]
    blocks = grad.reshape(2, 2, 2, 2, 2, -1, width)
    got = flip(blocks[1], "core")
    low_got = flip(plus(blocks[0, 0, 1], got[0, 1]), "y")
    high_got = flip(plus(blocks[0, 1, 1], got[1, 1]), "grp")
    low, high = plus(blocks[0, 0, 0], got[0, 0]), plus(blocks[0, 1, 0], got[1, 0])
    low_next = flip(plus(low[1], low_got[1]), "grp")
    high_next = flip(plus(high[1], high_got[1]), "y")
    low = plus(plus(low[0], low_got[0]), low_next)
    high = plus(plus(high[0], high_got[0]), high_next)
    line = jnp.concatenate([low, high], 1)
    return line[0].astype(f32) + flip(line[1], "th").astype(f32)


def turned(table):
    for dim, axis in enumerate(HEAD_GROUP):
        table = jnp.where(lax.axis_index(axis) == 1, jnp.flip(table, dim), table)
    return table


def head_order(table):
    if not square_plane():
        return table.reshape(-1)
    table = turned(table)
    half = table.shape[-1] // 2
    low = table[..., :half].transpose(2, 1, 0, 3, 4)
    high = table[..., half:].transpose(2, 0, 1, 3, 4)
    return jnp.stack([low, high], 1).reshape(-1)


def head_table(flat, shape):
    if not square_plane():
        return flat.reshape(shape)
    halves = flat.reshape(2, 2, 2, 2, 2, -1)
    low = halves[:, 0].transpose(2, 1, 0, 3, 4)
    high = halves[:, 1].transpose(1, 2, 0, 3, 4)
    return turned(jnp.concatenate([low, high], -1))


def nn(left, right):
    return lax.dot_general(left, right, (((1,), (0,)), ((), ())), preferred_element_type=f32)


def nt(left, right):
    return lax.dot_general(left, right, (((1,), (1,)), ((), ())), preferred_element_type=f32)


def tn(left, right):
    return lax.dot_general(left, right, (((0,), (0,)), ((), ())), preferred_element_type=f32)


def norm_rows(values, gains):
    centre = values - jnp.mean(values, -1, keepdims=True)
    spread = jnp.mean(centre * centre, -1, keepdims=True)
    return centre * lax.rsqrt(spread + epsilon) * gains[0:1] + gains[1:2]


def norm_rows_back(values, gains, upstream):
    centre = values - jnp.mean(values, -1, keepdims=True)
    inverse = lax.rsqrt(jnp.mean(centre * centre, -1, keepdims=True) + epsilon)
    unit = centre * inverse
    inner = upstream * gains[0:1]
    back = inverse * (
        inner
        - jnp.mean(inner, -1, keepdims=True)
        - unit * jnp.mean(inner * unit, -1, keepdims=True)
    )
    gain = jnp.sum(upstream * unit, 0, keepdims=True)
    bias = jnp.sum(upstream, 0, keepdims=True)
    return back, jnp.concatenate([gain, bias], 0)


TILE = 128


def lanes(rows):
    return lax.broadcasted_iota(jnp.int32, (rows, TILE), 1)


def turn(values, cosine, sine, part):
    half = HEAD // 2
    where = lanes(values.shape[0])
    swapped = jnp.where(
        where % HEAD < half,
        pltpu.roll(values, TILE - half, 1),
        pltpu.roll(values, half, 1),
    )
    turned = values * cosine + swapped * sine
    return turned if part == TILE else jnp.where(where < part, turned, values)


def weight_spec(weight, index):
    array, kind = weight
    unused, blocks, unused, rows, width = array.shape
    return pl.BlockSpec((1, blocks, 1, rows, width), lambda s, *at: (index(s), 0, kind, 0, 0))


def matrix(ref):
    blocks, rows, width = ref.shape[1], ref.shape[3], ref.shape[4]
    return ref[0, :, 0].reshape(blocks * rows, width)


def whole_spec(array):
    zeros = (0,) * array.ndim
    return pl.BlockSpec(array.shape, lambda s: zeros)


def spec(shape, index):
    return pl.BlockSpec(shape, index)


def params(limit=48):
    return pltpu.CompilerParams(vmem_limit_bytes=limit * 2**20)


def cost(flops, moved):
    return pl.CostEstimate(flops=int(flops), bytes_accessed=int(moved), transcendentals=0)


def project_kernel(x, gains, cosine, sine, w, h, q, clean, masked, h_now):
    @pl.when(pl.program_id(0) == 0)
    def begin():
        h_now[...] = norm_rows(x[...], gains[...]).astype(bf16)
        h[...] = h_now[...]

    z = nn(h_now[...], matrix(w)[:, : 5 * TILE])
    cos, sin = cosine[...], sine[...]
    tiles = [z[:, TILE * i : TILE * (i + 1)] for i in range(5)]
    rows = z.shape[0]
    low = lanes(rows) < HEAD
    q[0, :, :TILE] = turn(tiles[0], cos, sin, TILE).astype(bf16)
    q[0, :, TILE:] = jnp.where(low, turn(tiles[4], cos, sin, TILE), 0.0).astype(bf16)
    triple = jnp.concatenate(
        [turn(tiles[1], cos, sin, TILE), tiles[2], turn(tiles[3], cos, sin, HEAD)], 1
    ).astype(bf16)
    span = rows // 2
    clean[...] = triple[:span]
    masked[...] = triple[span:]


def project(x, gains, tables, w):
    rows, width = x.shape
    count = w[0].shape[0]
    span = rows // 2
    triple = spec((span, 3 * TILE), lambda t: (0, t))
    return pl.pallas_call(
        project_kernel,
        grid=(count,),
        in_specs=[whole_spec(x), whole_spec(gains)]
        + [whole_spec(table) for table in tables]
        + [weight_spec(w, lambda t: t)],
        out_specs=[
            spec((rows, width), lambda t: (0, 0)),
            spec((1, rows, 2 * TILE), lambda t: (t, 0, 0)),
            triple,
            triple,
        ],
        out_shape=[
            jax.ShapeDtypeStruct((rows, width), bf16),
            jax.ShapeDtypeStruct((count, rows, 2 * TILE), bf16),
            jax.ShapeDtypeStruct((span, count * 3 * TILE), bf16),
            jax.ShapeDtypeStruct((span, count * 3 * TILE), bf16),
        ],
        scratch_shapes=[pltpu.VMEM((rows, width), bf16)],
        compiler_params=params(),
        cost_estimate=cost(2 * rows * width * width * count, 2 * count * width * width),
        name="project",
    )(x, gains, *tables, w[0])


def head_operands(pair, triple, own, j):
    rows = pair.shape[0]
    low = lanes(rows) < HEAD
    if j == 2:
        query, key, value = pair[:, TILE:], triple[:, 2 * TILE :], triple[:, 2 * TILE :]
        own_key, own_value = own[:, 2 * TILE :], own[:, 2 * TILE :]
    else:
        keep = low if j == 0 else jnp.logical_not(low)
        query = jnp.where(keep, pair[:, :TILE], jnp.zeros((), pair.dtype))
        key, value = triple[:, :TILE], triple[:, TILE : 2 * TILE]
        own_key, own_value = own[:, :TILE], own[:, TILE : 2 * TILE]
    return query, key, value, own_key, own_value


def head_scores(query, key, own_key, seen):
    scale = HEAD ** (-0.5)
    span = own_key.shape[0]
    score = jnp.where(seen > 0.0, nt(query, key) * scale, far_below)
    alone = jnp.sum(query[span:].astype(f32) * own_key.astype(f32), -1, keepdims=True) * scale
    return score, jnp.concatenate([jnp.full((query.shape[0] - span, 1), far_below, f32), alone], 0)


def attend_kernel(x, q, k0, k1, k2, k3, own, seen, w, mid, o, log_total):
    rows = x.shape[0]
    span = own.shape[0]

    @pl.when(pl.program_id(0) == 0)
    def begin():
        mid[...] = x[...]

    pair = q[0]
    triple = jnp.concatenate([k0[...], k1[...], k2[...], k3[...]], 0)
    lane = lanes(rows)
    low = lane < HEAD
    outs, logs = [], jnp.zeros((rows, TILE), f32)
    for j in range(3):
        query, key, value, own_key, own_value = head_operands(pair, triple, own[...], j)
        score, alone = head_scores(query, key, own_key, seen[...])
        top = jnp.maximum(jnp.max(score, -1, keepdims=True), alone)
        part = jnp.exp(score - top)
        part_alone = jnp.exp(alone - top)
        total = jnp.sum(part, -1, keepdims=True) + part_alone
        inverse = 1.0 / total
        logs = jnp.where(lane == j, top + jnp.log(total), logs)
        out = nn((part * inverse).astype(bf16), value)
        weight = (part_alone * inverse).astype(bf16).astype(f32)[span:]
        out = jnp.concatenate([out[:span], out[span:] + weight * own_value.astype(f32)], 0)
        outs.append(out)
    both = jnp.concatenate(
        [jnp.where(low, 0.0, outs[2]), jnp.where(low, outs[0], outs[1])], 1
    ).astype(bf16)
    o[0] = both
    log_total[0] = logs
    mid[...] += nt(both, matrix(w)[:, 4 * TILE :])


def attend(x, q, keys, own, seen, w):
    rows, width = x.shape
    count = w[0].shape[0]
    span = own.shape[0]
    triple = spec((span, 3 * TILE), lambda t: (0, t))
    return pl.pallas_call(
        attend_kernel,
        grid=(count,),
        in_specs=[
            whole_spec(x),
            spec((1, rows, 2 * TILE), lambda t: (t, 0, 0)),
            triple, triple, triple, triple, triple,
            whole_spec(seen),
            weight_spec(w, lambda t: t),
        ],
        out_specs=[
            spec((rows, width), lambda t: (0, 0)),
            spec((1, rows, 2 * TILE), lambda t: (t, 0, 0)),
            spec((1, rows, TILE), lambda t: (t, 0, 0)),
        ],
        out_shape=[
            jax.ShapeDtypeStruct((rows, width), f32),
            jax.ShapeDtypeStruct((count, rows, 2 * TILE), bf16),
            jax.ShapeDtypeStruct((count, rows, TILE), f32),
        ],
        compiler_params=params(),
        cost_estimate=cost(16 * rows * 4 * span * HEAD * count, 2 * count * width * width),
        name="attend",
    )(x, q, *keys, own, seen, w[0])


def gelu_parts(u):
    root = 0.7978845608028654
    square = u * u
    th = jnp.tanh(root * (u + 0.044715 * square * u))
    value = 0.5 * u * (1.0 + th)
    slope = 0.5 * (1.0 + th) + 0.5 * u * (1.0 - th * th) * (root * (1.0 + 3 * 0.044715 * square))
    return value, slope


def feed_kernel(mid, gains, up, down, h2, out):
    @pl.when(pl.program_id(0) == 0)
    def begin():
        h2[...] = norm_rows(mid[...], gains[...]).astype(bf16)
        out[...] = mid[...]

    u = nn(h2[...], matrix(up))
    out[...] += nt(gelu_parts(u)[0].astype(bf16), matrix(down))


def feed(mid, gains, up, down):
    rows, width = mid.shape
    count = up[0].shape[0]
    return pl.pallas_call(
        feed_kernel,
        grid=(count,),
        in_specs=[
            whole_spec(mid), whole_spec(gains),
            weight_spec(up, lambda t: t), weight_spec(down, lambda t: t),
        ],
        out_specs=[spec((rows, width), lambda t: (0, 0))] * 2,
        out_shape=[
            jax.ShapeDtypeStruct((rows, width), bf16),
            jax.ShapeDtypeStruct((rows, width), f32),
        ],
        compiler_params=params(),
        cost_estimate=cost(4 * rows * width * width * count, 4 * count * width * width),
        name="feed",
    )(mid, gains, up[0], down[0])


def feed_back_kernel(
    grad, mid, h2, gains, up, down, grad_low, a, grad_u, grad_mid, mid_low, gain_grad, total
):
    step = pl.program_id(0)

    @pl.when(step == 0)
    def begin():
        grad_low[...] = grad[...].astype(bf16)
        total[...] = jnp.zeros_like(total)

    value, slope = gelu_parts(nn(h2[...], matrix(up)))
    a[...] = value.astype(bf16)
    grad_hidden = (nn(grad_low[...], matrix(down)) * slope).astype(bf16)
    grad_u[...] = grad_hidden
    total[...] += nt(grad_hidden, matrix(up))

    @pl.when(step == pl.num_programs(0) - 1)
    def norm():
        back, gain_grad[...] = norm_rows_back(mid[...], gains[...], total[...])
        back = back + grad[...]
        grad_mid[...] = back
        mid_low[...] = back.astype(bf16)


def feed_back(grad, mid, h2, gains, up, down):
    rows, width = grad.shape
    count = up[0].shape[0]
    hidden = spec((rows, width), lambda t: (0, t))
    plain = spec((rows, width), lambda t: (0, 0))

    def rows_of(kind, columns=width):
        return jax.ShapeDtypeStruct((rows, columns), kind)

    return pl.pallas_call(
        feed_back_kernel,
        grid=(count,),
        in_specs=[plain, plain, plain, whole_spec(gains)]
        + [weight_spec(up, lambda t: t), weight_spec(down, lambda t: t)],
        out_specs=[plain, hidden, hidden, plain, plain, whole_spec(gains)],
        out_shape=[
            rows_of(bf16), rows_of(bf16, count * width), rows_of(bf16, count * width),
            rows_of(f32), rows_of(bf16), jax.ShapeDtypeStruct(gains.shape, f32),
        ],
        scratch_shapes=[pltpu.VMEM((rows, width), f32)],
        compiler_params=params(),
        cost_estimate=cost(6 * rows * width * width * count, 4 * count * width * width),
        name="feed_back",
    )(grad, mid, h2, gains, up[0], down[0])


def attend_back_kernel(
    mid_low, q, k0, k1, k2, k3, own, seen, log_total, cosine, sine, w, grad_q, keep, send, grad_own
):
    rows = mid_low.shape[0]
    span = own.shape[0]
    scale = HEAD ** (-0.5)
    grad_o = nn(mid_low[...], matrix(w)[:, 4 * TILE :]).astype(bf16)
    pair = q[0]
    triple = jnp.concatenate([k0[...], k1[...], k2[...], k3[...]], 0)
    lane = lanes(rows)
    low = lane < HEAD
    zero = jnp.zeros((), bf16)
    query_grads, key_grads, value_grads, own_keys, own_values = [], [], [], [], []
    for j in range(3):
        query, key, value, own_key, own_value = head_operands(pair, triple, own[...], j)
        if j == 2:
            upstream = jnp.where(low, zero, grad_o[:, :TILE])
        else:
            keep_lane = low if j == 0 else jnp.logical_not(low)
            upstream = jnp.where(keep_lane, grad_o[:, TILE:], zero)
        score, alone = head_scores(query, key, own_key, seen[...])
        logs = log_total[0][:, j : j + 1]
        prob = jnp.exp(score - logs)
        prob_alone = jnp.exp(alone - logs)
        dprob = nt(upstream, value)
        lone = upstream[span:].astype(f32)
        dalone = jnp.sum(lone * own_value.astype(f32), -1, keepdims=True)
        dalone = jnp.concatenate([jnp.zeros((rows - span, 1), f32), dalone], 0)
        delta = jnp.sum(dprob * prob, -1, keepdims=True) + dalone * prob_alone
        dscore = (prob * (dprob - delta)).astype(bf16)
        dself = (prob_alone * (dalone - delta)).astype(bf16).astype(f32)[span:] * scale
        query_grad = nn(dscore, key) * scale
        query_grads.append(
            jnp.concatenate(
                [query_grad[:span], query_grad[span:] + dself * own_key.astype(f32)], 0
            )
        )
        key_grads.append(tn(dscore, query) * scale)
        value_grads.append(tn(prob.astype(bf16), upstream))
        own_keys.append(dself * query[span:].astype(f32))
        own_values.append(prob_alone.astype(bf16).astype(f32)[span:] * lone)
    cos, sin = cosine[...], -sine[...]
    first = jnp.where(low, query_grads[0], query_grads[1])
    grad_q[0, :, :TILE] = turn(first, cos, sin, TILE).astype(bf16)
    grad_q[0, :, TILE:] = jnp.where(low, turn(query_grads[2], cos, sin, TILE), 0.0).astype(bf16)
    grads = jnp.concatenate(
        [
            key_grads[0] + key_grads[1],
            value_grads[0] + value_grads[1],
            key_grads[2] + value_grads[2],
        ],
        1,
    ).astype(bf16)
    keep[0] = grads[:span]
    send[0] = grads[span : 2 * span]
    keep[1] = grads[2 * span : 3 * span]
    send[1] = grads[3 * span :]
    grad_own[...] = jnp.concatenate(
        [own_keys[0] + own_keys[1], own_values[0] + own_values[1], own_keys[2] + own_values[2]], 1
    )


def attend_back(mid_low, q, keys, own, seen, log_total, tables, w):
    rows, width = mid_low.shape
    count = w[0].shape[0]
    span = own.shape[0]
    triple = spec((span, 3 * TILE), lambda t: (0, t))
    pair = spec((1, rows, 2 * TILE), lambda t: (t, 0, 0))
    couple = spec((2, span, 3 * TILE), lambda t: (0, 0, t))
    couple_shape = jax.ShapeDtypeStruct((2, span, count * 3 * TILE), bf16)
    return pl.pallas_call(
        attend_back_kernel,
        grid=(count,),
        in_specs=[spec((rows, width), lambda t: (0, 0)), pair]
        + [triple] * 5
        + [whole_spec(seen), spec((1, rows, TILE), lambda t: (t, 0, 0))]
        + [whole_spec(table) for table in tables]
        + [weight_spec(w, lambda t: t)],
        out_specs=[pair, couple, couple, triple],
        out_shape=[
            jax.ShapeDtypeStruct((count, rows, 2 * TILE), bf16),
            couple_shape, couple_shape,
            jax.ShapeDtypeStruct((span, count * 3 * TILE), f32),
        ],
        compiler_params=params(),
        cost_estimate=cost(32 * rows * 4 * span * HEAD * count, 2 * count * width * width),
        name="attend_back",
    )(mid_low, q, *keys, own, seen, log_total, *tables, w[0])


def back_second_kernel(
    keep, got, far, grad_own, grad_q, cosine, sine, x, grad_mid, gains, w, dz, out, gain_grad, total
):
    step = pl.program_id(0)

    @pl.when(step == 0)
    def begin():
        total[...] = jnp.zeros_like(total)

    clean = keep[0].astype(f32) + got[0].astype(f32) + far[...].astype(f32)
    triple = jnp.concatenate([clean, grad_own[...]], 0)
    cos, sin = cosine[...], -sine[...]
    pair = grad_q[0]
    grads = jnp.concatenate(
        [
            pair[:, :TILE],
            turn(triple[:, :TILE], cos, sin, TILE).astype(bf16),
            triple[:, TILE : 2 * TILE].astype(bf16),
            turn(triple[:, 2 * TILE :], cos, sin, HEAD).astype(bf16),
            pair[:, TILE:],
        ],
        1,
    )
    dz[:, : 5 * TILE] = grads
    dz[:, 5 * TILE :] = jnp.zeros_like(pair[:, TILE:])
    total[...] += nt(grads, matrix(w)[:, : 5 * TILE])

    @pl.when(step == pl.num_programs(0) - 1)
    def norm():
        back, gain_grad[...] = norm_rows_back(x[...], gains[...], total[...])
        out[...] = grad_mid[...] + back


def back_second(keep, got, far, grad_own, grad_q, tables, x, grad_mid, gains, w):
    rows, width = x.shape
    count = w[0].shape[0]
    span = rows // 2
    triple = spec((span, 3 * TILE), lambda t: (0, t))
    couple = spec((1, span, 3 * TILE), lambda t: (0, 0, t))
    plain = spec((rows, width), lambda t: (0, 0))
    return pl.pallas_call(
        back_second_kernel,
        grid=(count,),
        in_specs=[couple, couple, triple, triple, spec((1, rows, 2 * TILE), lambda t: (t, 0, 0))]
        + [whole_spec(table) for table in tables]
        + [plain, plain, whole_spec(gains), weight_spec(w, lambda t: t)],
        out_specs=[spec((rows, width), lambda t: (0, t)), plain, whole_spec(gains)],
        out_shape=[
            jax.ShapeDtypeStruct((rows, count * width), bf16),
            jax.ShapeDtypeStruct((rows, width), f32),
            jax.ShapeDtypeStruct(gains.shape, f32),
        ],
        scratch_shapes=[pltpu.VMEM((rows, width), f32)],
        compiler_params=params(),
        cost_estimate=cost(2 * rows * width * width * count, 2 * count * width * width),
        name="back_second",
    )(keep, got, far, grad_own, grad_q, *tables, x, grad_mid, gains, w[0])


def update(weight, moment, average, grad, rate):
    fresh_mom = momentum * moment + grad
    fresh_w = weight - rate * (grad + momentum * fresh_mom)
    fresh_avg = average_decay * average + (1.0 - average_decay) * fresh_w
    return (fresh_mom, fresh_w, fresh_avg)


def lookup_plan(ids, block_rows):
    slots = ids.shape[1]
    owner = ids // block_rows
    order = jnp.arange(slots)
    same = ids[:, :, None] == ids[:, None, :]
    lead = jnp.min(jnp.where(same, order[None, None, :], slots), -1)
    first = lead == order
    ahead = jnp.logical_and(
        jnp.logical_and(first[:, None, :], owner[:, :, None] == owner[:, None, :]),
        order[None, None, :] < lead[:, :, None],
    )
    place = jnp.sum(ahead.astype(jnp.int32), -1)
    return owner, place, first


def per_device(
    tokens, positions, lengths,
    embedding, embedding_mom, embedding_avg,
    qkv_w, qkv_mom, qkv_avg,
    out_w, out_mom, out_avg,
    up_w, up_mom, up_avg,
    down_w, down_mom, down_avg,
    norm_gains, gains_mom, gains_avg,
):
    n_grp, n_y, n_t = lax.axis_size("grp"), lax.axis_size("y"), lax.axis_size(TENSOR)
    devices = 2 * n_grp * n_y * n_t
    at_grp, at_y, at_core = (lax.axis_index(name) for name in ALL[:3])
    at_t = lax.axis_index(TENSOR)
    me = lax.axis_index(ALL)
    block_rows, width = embedding.shape
    layers = qkv_w.shape[0]
    micros, unused, rows_here, seq = tokens.shape
    rows = rows_here * 2 * n_y
    span = seq // (2 * n_grp)
    my_row = at_y * n_t + at_t
    my_part = at_grp * 2 + at_core

    packed = jnp.concatenate(
        [tokens, positions, jnp.broadcast_to(lengths[..., None], lengths.shape + (128,))], -1
    )
    packed = lax.all_gather(packed, ("y", "core"), axis=2, tiled=True)
    packed = packed.transpose(1, 0, 2, 3).reshape(2, micros * rows, -1)
    ids_all, places_all, lens_all = packed[..., :seq], packed[..., seq : 2 * seq], packed[..., -1]

    def by_device(table):
        split = table.reshape(n_y, n_t, n_grp, 2, span)
        return split.transpose(2, 0, 3, 1, 4).reshape(devices, span)

    lens = lax.dynamic_index_in_dim(lens_all, my_row, 1, keepdims=False)
    clean_len, masked_len = lens[0], lens[1]
    places = lax.dynamic_slice(places_all, (0, my_row, my_part * span), (2, 1, span))
    tables = rope_tables(places)
    near = jnp.array([0, 1, 0, 1]) ^ at_core
    far = jnp.array([0, 0, 1, 1]) ^ at_grp
    slots = (far * 2 + near)[:, None] * span + jnp.arange(span)[None, :]
    seen = (slots.reshape(1, -1) < clean_len).astype(f32)

    shards = []
    for layer in range(layers):
        turned_out = out_w[layer].T
        q_part, k_part, v_part = (qkv_w[layer][:, i] for i in range(3))
        attn = [
            q_part[:, :TILE], k_part[:, :TILE], v_part[:, :TILE],
            k_part[:, TILE:], v_part[:, TILE:], q_part[:, TILE:], turned_out[:, TILE:],
            turned_out[:, :TILE],
        ]
        shards.append(
            jnp.stack([jnp.concatenate(attn, 1), up_w[layer], down_w[layer].T]).astype(bf16)
        )
    front = gather_whole(jnp.concatenate([shards[0], shards[1][:1]]))
    rest = gather_whole(shards[1][1:])
    weights = [
        ((front, 0), (front, 1), (front, 2)),
        ((front, 3), (rest, 0), (rest, 1)),
    ]
    table = embedding.astype(bf16)

    mask_id = block_rows * devices - 1
    wanted = jnp.concatenate(
        [by_device(ids_all[0]), jnp.full((devices, 1), mask_id, jnp.int32)], 1
    )
    owner, place, first = lookup_plan(wanted, block_rows)
    rounds = jnp.max(place) // CAPACITY + 1
    mine = jnp.logical_and(first, owner == me)
    local = wanted - me * block_rows
    my_owner = lax.dynamic_index_in_dim(owner, me, 0, keepdims=False)
    my_place = lax.dynamic_index_in_dim(place, me, 0, keepdims=False)
    my_slot = my_owner * CAPACITY + my_place
    my_slot = jnp.concatenate([my_slot[:span], jnp.broadcast_to(my_slot[span:], (span,))])
    my_place = jnp.concatenate([my_place[:span], jnp.broadcast_to(my_place[span:], (span,))])

    def sent_rows(step):
        at = place - step * CAPACITY
        hit = jnp.logical_and(mine[:, None, :], at[:, None, :] == jnp.arange(CAPACITY)[None, :, None])
        row = jnp.sum(jnp.where(hit, local[:, None, :] + 1, 0), -1).reshape(-1) - 1
        return (row[:, None] == jnp.arange(block_rows)[None, :]).astype(bf16)

    def used_rows(step):
        slot = my_slot - step * CAPACITY
        inside = jnp.logical_and(my_place >= step * CAPACITY, my_place < (step + 1) * CAPACITY)
        slot = jnp.where(inside, slot, -1)
        return (slot[:, None] == jnp.arange(devices * CAPACITY)[None, :]).astype(bf16)

    def swap(values):
        return lax.all_to_all(values, ALL, 0, 0, tiled=True)

    def look(step):
        sent = dot("kv,vd->kd", sent_rows(step), table).astype(bf16)
        return dot("nk,kd->nd", used_rows(step), swap(sent))

    def look_sent(step, grad):
        return dot("nk,nd->kd", used_rows(step), grad).astype(bf16)

    def look_back(step, grad):
        return dot("kv,kd->vd", sent_rows(step), swap(look_sent(step, grad)))

    def more(step_fn, begin):
        return lax.while_loop(
            lambda carry: carry[0] < rounds,
            lambda carry: (carry[0] + 1, carry[1] + step_fn(carry[0])),
            (jnp.int32(1), begin),
        )[1]

    x = more(look, look(0))

    kept = []
    for layer in range(layers):
        attn, upper, lower = weights[layer]
        h, q, clean, own = project(x, norm_gains[2 * layer], tables, attn)
        keys = gather_keys(clean)
        mid, o, log_total = attend(x, q, keys, own, seen, attn)
        h2, after = feed(mid, norm_gains[2 * layer + 1], upper, lower)
        kept.append((x, h, q, keys, own, o, log_total, mid, h2))
        x = after

    last = x[span:]
    f_mine = layer_norm(last, norm_gains[2 * layers, 0], norm_gains[2 * layers, 1]).astype(bf16)
    f_all = gather_head(f_mine)
    both_tables = jnp.concatenate([table, flip(table, "tl")])

    def my_group(by_dev):
        split = by_dev.reshape(n_grp, n_y, 2, n_t // 2, 2, span)
        return lax.dynamic_index_in_dim(split, at_t % 2, 4, keepdims=False)

    targets = head_order(my_group(by_device(ids_all[1])))
    target_block = targets // block_rows
    targets = targets % block_rows + jnp.where(target_block == me ^ 1, block_rows, 0)
    targets = jnp.where(target_block | 1 == me | 1, targets, -1)
    valid_all = head_order(
        my_group(by_device((jnp.arange(seq)[None, :] < lens_all[1][:, None]).astype(jnp.int32)))
    ) > 0
    logits = dot("nd,vd->nv", f_all, both_tables)
    top = jnp.max(logits, -1)
    part_total = head_table(
        top + jnp.log(jnp.sum(jnp.exp(logits - top[:, None]), -1)), (n_grp, n_y, 2, n_t // 2, span)
    )
    group = lax.axis_size(HEAD_GROUP)
    parts = lax.all_to_all(
        jnp.broadcast_to(part_total.reshape(1, -1), (group, group * span)),
        HEAD_GROUP, 0, 0, tiled=True,
    )
    top = jnp.max(parts, 0)
    log_total = top + jnp.log(jnp.sum(jnp.exp(parts - top), 0))
    own_total = lax.dynamic_slice(log_total, (lax.axis_index(HEAD_GROUP) * span,), (span,))
    log_total = head_order(log_total.reshape(part_total.shape))
    onehot = targets[:, None] == jnp.arange(2 * block_rows)[None, :]
    target_part = jnp.sum(jnp.where(jnp.logical_and(onehot, valid_all[:, None]), logits, 0.0))
    own_valid = my_part * span + jnp.arange(span) < masked_len
    loss_part = jnp.sum(jnp.where(own_valid, own_total, 0.0)) - target_part
    grad_logits = jnp.where(
        valid_all[:, None], jnp.exp(logits - log_total[:, None]) - onehot, 0.0
    ).astype(bf16)
    grad_f = dot("nv,vd->nd", grad_logits, both_tables).astype(bf16)
    grad_f = scatter_head(grad_f)

    back, gain_final, bias_final = norm_back(
        last, norm_gains[2 * layers, 0], norm_gains[2 * layers, 1], grad_f
    )
    grad_x = jnp.concatenate([jnp.zeros_like(back), back], 0)
    gain_parts = [None] * layers
    pieces, table_got = [[], [], []], []
    nothing = Scatter()
    outer = inner = nothing
    owned = []
    for layer in reversed(range(layers)):
        attn, upper, lower = weights[layer]
        before, h, q, keys, own, o, log_total, mid, h2 = kept[layer]

        outer.restart()
        beside = flip(pieces[0], "tl")
        grad_low, a, grad_u, grad_mid, mid_low, gain_mid = feed_back(
            grad_x, mid, h2, norm_gains[2 * layer + 1], upper, lower
        )
        grad_u, inner.moving, outer.moving, beside = fence(
            grad_u, inner.moving, outer.moving, beside
        )
        table_got += beside

        outer.third()
        inner.first()
        grads = weight_grads([(h2, grad_u), (grad_low, a)])
        mid_low, grads, inner.sent = fence(mid_low, grads, inner.sent)

        outer = Scatter(grads)
        inner.start()
        beside = flip(pieces[1], "tl")
        grad_q, keep, send, grad_own = attend_back(
            mid_low, q, keys, own, seen, log_total, tables, attn
        )
        keep, send, outer.moving, inner.moving, beside = fence(
            keep, send, outer.moving, inner.moving, beside
        )
        table_got += beside

        got = flip(send, "core")
        outer.first()
        inner.second()
        keep, got, outer.sent, inner.sent = fence(keep, got, outer.sent, inner.sent)

        far = plus(keep[1], got[1])
        far, outer.sent, inner.sent = fence(far, outer.sent, inner.sent)

        far = flip(far, "grp")
        inner.restart()
        far, outer.sent, inner.moving = fence(far, outer.sent, inner.moving)

        outer.start()
        beside = flip(pieces[2], "tl")
        dz, grad_x, gain_in = back_second(
            keep, got, far, grad_own, grad_q, tables, before, grad_mid, norm_gains[2 * layer], attn
        )
        gain_parts[layer] = jnp.stack([gain_in, gain_mid])
        grads = weight_grads([(h, dz)], (mid_low, o))
        if inner is nothing:
            grad_logits, dz = fence(grad_logits, dz)
            own_table, other_table = table_grads(grad_logits, f_all, block_rows)
            cuts = [-(-block_rows // 64) * 16 * i for i in range(1, 4)]
            first, second, *others = jnp.split(other_table, cuts)
            pieces = [[first], [second], others]
        grad_x, grads, pieces, outer.moving, beside = fence(
            grad_x, grads, pieces, outer.moving, beside
        )
        table_got += beside

        inner.third()
        outer.second()
        outer.sent, grads = fence(outer.sent, grads)
        owned.append(outer)
        inner = Scatter(grads)
        owned.append(inner)

    outer.restart()
    grad_low = grad_x.astype(bf16)
    sent = look_sent(0, grad_low)
    gains_grad = jnp.concatenate(gain_parts + [jnp.stack([gain_final, bias_final])[None]], 0)
    small = jnp.concatenate([gains_grad.reshape(-1), loss_part[None]])
    small = jnp.pad(small, (0, -small.size % (devices * 128))).reshape(devices, -1)
    sent, small, inner.moving, outer.moving = fence(sent, small, inner.moving, outer.moving)

    inner.first()
    outer.third()
    inner.sent, outer.line = fence(inner.sent, outer.line)

    inner.start()
    got_rows = swap(sent)
    inner.moving, got_rows = fence(inner.moving, got_rows)

    inner.second()
    inner.sent, small = fence(inner.sent, small)

    inner.restart()
    small = swap(small)
    inner.moving, small = fence(inner.moving, small)

    inner.third(True)
    grad_table = own_table + jnp.concatenate(table_got).astype(f32)
    grad_table = grad_table + dot("kv,kd->vd", sent_rows(0), got_rows)
    grad_table = more(lambda step: look_back(step, grad_low), grad_table)
    small = jnp.sum(small, 0)
    owned = [
        [owned[2 * i + 1].sums()[0], owned[2 * i].sums()[0], owned[2 * i].sums()[1]]
        for i in reversed(range(layers))
    ]

    mask_count = jnp.sum(lens_all[1]).astype(f32)
    squares = jnp.sum(grad_table * grad_table)
    for part in owned[0] + owned[1]:
        squares = squares + jnp.sum(part * part)
    shared = jnp.concatenate([small, jnp.broadcast_to(squares, (128,))])
    shared = swap(jnp.broadcast_to(shared[None], (devices, shared.size)))
    small = shared[:, : small.size].reshape(-1)
    gains_total = small[: gains_grad.size].reshape(gains_grad.shape)
    loss_sum = small[gains_grad.size]
    squares = jnp.sum(shared[:, -1]) + jnp.sum(gains_total * gains_total)
    grad_norm = jnp.sqrt(squares) / mask_count
    factor = jnp.minimum(1.0, threshold / grad_norm) / mask_count

    qkv_grads, out_grads = [], []
    for part in owned:
        tiles = jnp.split(part[0], 2 * width // TILE, 1)
        q_pair, k_pair, v_pair = (
            jnp.concatenate(tiles[2 * i : 2 * i + 2], 1) for i in range(3)
        )
        qkv_grads.append(
            jnp.stack(
                [
                    jnp.concatenate([q_pair, tiles[8]], 1),
                    jnp.concatenate([k_pair, tiles[6]], 1),
                    jnp.concatenate([v_pair, tiles[7]], 1),
                ],
                1,
            )
        )
        out_grads.append(jnp.concatenate([tiles[10], tiles[11], tiles[9]], 1).T)
    qkv_grad, out_grad = jnp.stack(qkv_grads), jnp.stack(out_grads)
    up_grad = jnp.stack([part[1] for part in owned])
    down_grad = jnp.stack([part[2].T for part in owned])
    results = [loss_sum, mask_count, grad_norm]
    for weight, moment, average, grad, rate in (
        (embedding, embedding_mom, embedding_avg, grad_table, rate_matrix),
        (qkv_w, qkv_mom, qkv_avg, qkv_grad, rate_matrix),
        (out_w, out_mom, out_avg, out_grad, rate_matrix),
        (up_w, up_mom, up_avg, up_grad, rate_matrix),
        (down_w, down_mom, down_avg, down_grad, rate_matrix),
        (norm_gains, gains_mom, gains_avg, gains_total, rate_gains),
    ):
        results += update(weight, moment, average, grad * factor, rate)
    return tuple(results)


def solution(mesh):
    n_grp, n_dp, n_t = mesh.devices.shape
    split = Mesh(mesh.devices.reshape(n_grp, n_dp // 2, 2, n_t // 2, 2), ALL)
    dp = ("y", "core")
    owners = ("grp", "y", "core")
    rows = P(None, None, dp, None)
    table = P(ALL, None)
    wide = P(None, owners, None, TENSOR)
    tall = P(None, TENSOR, owners)
    flat = P(None, owners, TENSOR)
    return jax.shard_map(
        per_device,
        mesh=split,
        in_specs=(rows, rows, P(None, None, dp))
        + (table,) * 3 + (wide,) * 3 + (tall,) * 3 + (flat,) * 3 + (tall,) * 3 + (P(),) * 3,
        out_specs=(P(),) * 3
        + (table,) * 3 + (wide,) * 3 + (tall,) * 3 + (flat,) * 3 + (tall,) * 3 + (P(),) * 3,
        check_vma=False,
    )
```

```python
import functools

import jax
import jax.numpy as jnp
from jax import lax
from jax.experimental import pallas as pl
from jax.experimental.pallas import tpu as pltpu
from jax.sharding import Mesh
from jax.sharding import PartitionSpec as P

HEAD = 64
CAPACITY = 15

epsilon = 1e-05
threshold = 0.05
momentum = 0.9
average_decay = 0.75
rate_matrix = 2000.0
rate_gains = 5000.0
far_below = -1e30
bf16 = jnp.bfloat16
f32 = jnp.float32
TENSOR = ("th", "tl")
ALL = ("grp", "y", "core", "th", "tl")
OWNERS = ("th", "tl", "grp", "y", "core")
HEAD_GROUP = ("grp", "y", "core", "th")


def layer_norm(values, gain, bias):
    centre = values - jnp.mean(values, -1, keepdims=True)
    spread = jnp.mean(centre * centre, -1, keepdims=True)
    return centre * lax.rsqrt(spread + epsilon) * gain + bias


def norm_back(values, gain, bias, upstream):
    unused, pullback = jax.vjp(layer_norm, values, gain, bias)
    return pullback(upstream)


def rope_tables(places):
    half_size = HEAD // 2
    lane = jnp.arange(TILE)
    frequency = 10000.0 ** (-(lane % half_size).astype(f32) / half_size)
    sign = jnp.where(lane % HEAD < half_size, -1.0, 1.0)
    angles = places.reshape(-1).astype(f32)[:, None] * frequency[None, :]
    return jnp.cos(angles), jnp.sin(angles) * sign


def dot(form, left, right):
    return jnp.einsum(form, left, right, preferred_element_type=f32)


def flip(values, axis):
    return lax.ppermute(values, axis, [(0, 1), (1, 0)])


def square_plane():
    return lax.axis_size("grp") == 2 and lax.axis_size("y") == 2


def coordinates():
    return jnp.stack([lax.axis_index("grp"), lax.axis_index("y"), lax.axis_index("core")])


def fence(*groups):
    return lax.optimization_barrier(groups)


def gather_whole(shards):
    kinds, rows, width = shards.shape
    everything = lax.all_gather(shards, OWNERS, axis=0, tiled=False)
    count = lax.axis_size(TENSOR)
    everything = everything.reshape(count, -1, kinds, rows, width)
    if rows % 16 == 0:
        return everything
    return everything.transpose(0, 2, 1, 3, 4).reshape(count, 1, kinds, -1, width)


def weight_grad_kernel(inputs, extra, at, *refs):
    xs, ys = refs[:inputs], refs[inputs : 2 * inputs]
    keep_ref, send_ref, turned, tile = refs[2 * inputs :]
    blocks, rows, width = tile.shape

    @pl.when(pl.program_id(0) == 0)
    def begin():
        for i in range(inputs):
            turned[i] = xs[i][...].T

    for kind in range(inputs - extra):
        grad = nn(turned[kind], ys[kind][...])
        if extra:
            more = nn(turned[1], ys[1][0])
            split = width - more.shape[1]
            grad = jnp.concatenate([grad[:, :split], grad[:, split:] + more], 1)
        tile[...] = grad.astype(bf16).reshape(blocks, rows, width)
        for by_x in range(2):
            for by_y in range(2):
                for core, ref in enumerate((keep_ref, send_ref)):
                    block = ((at[0] ^ by_x) * 2 + (at[1] ^ by_y)) * 2 + (at[2] ^ core)
                    ref[0, kind, by_x, by_y] = tile[block]


def weight_grads(pairs, extra=None):
    kinds = len(pairs)
    slots, width = pairs[0][0].shape
    count = pairs[0][1].shape[1] // width
    rows = width // 8
    if not square_plane():
        whole = [dot("nd,ntf->tdf", x, y.reshape(slots, count, width)) for x, y in pairs]
        if extra:
            more = dot("nd,tnf->tdf", *extra)
            whole[0] += jnp.pad(more, ((0, 0), (0, 0), (width - more.shape[2], 0)))
        return jnp.stack([part.astype(bf16) for part in whole], 1)
    part = pl.BlockSpec((1, kinds, 2, 2, rows, width), lambda t, at: (t, 0, 0, 0, 0, 0))
    shape = jax.ShapeDtypeStruct((count, kinds, 2, 2, rows, width), bf16)
    x_spec = pl.BlockSpec((slots, width), lambda t, at: (0, 0))
    x_specs = [x_spec] * kinds
    y_specs = [pl.BlockSpec((slots, width), lambda t, at: (0, t))] * kinds
    xs = [x for x, unused in pairs]
    ys = [y for unused, y in pairs]
    if extra:
        xs.append(extra[0])
        ys.append(extra[1])
        x_specs.append(x_spec)
        y_specs.append(pl.BlockSpec((1,) + extra[1].shape[1:], lambda t, at: (t, 0, 0)))
    return pl.pallas_call(
        functools.partial(weight_grad_kernel, len(xs), bool(extra)),
        grid_spec=pltpu.PrefetchScalarGridSpec(
            num_scalar_prefetch=1,
            grid=(count,),
            in_specs=x_specs + y_specs,
            out_specs=[part, part],
            scratch_shapes=[
                pltpu.VMEM((len(xs), width, slots), bf16),
                pltpu.VMEM((8, rows, width), bf16),
            ],
        ),
        out_shape=[shape, shape],
        compiler_params=pltpu.CompilerParams(vmem_limit_bytes=60 * 2**20),
        cost_estimate=pl.CostEstimate(
            flops=2 * slots * width * width * count * kinds,
            bytes_accessed=2 * count * kinds * width * (slots + width),
            transcendentals=0,
        ),
        name="weight_grads",
    )(coordinates(), *xs, *ys)


def plus(left, right):
    return (left.astype(f32) + right.astype(f32)).astype(bf16)


def add_first_kernel(kinds, own_low, own_high, got_low, got_high, low_keep, high_keep, *sends):
    low_keep[0] = plus(own_low[0, :, 0], got_low[0, :, 0])
    high_keep[0] = plus(own_high[0, :, :, 0], got_high[0, :, :, 0])
    for kind in range(kinds):
        low_send, high_send = sends[2 * kind : 2 * kind + 2]
        low_send[0] = plus(own_low[0, kind, 1], got_low[0, kind, 1])
        high_send[0] = plus(own_high[0, kind, :, 1], got_high[0, kind, :, 1])


def add_first(own, got):
    count, kinds, unused, unused, rows, width = own.shape
    half = count // 2
    low = pl.BlockSpec((1, kinds, 2, 2, rows, width), lambda t: (t, 0, 0, 0, 0, 0))
    high = pl.BlockSpec((1, kinds, 2, 2, rows, width), lambda t: (t + half, 0, 0, 0, 0, 0))
    part = pl.BlockSpec((1, kinds, 2, rows, width), lambda t: (t, 0, 0, 0, 0))
    send = pl.BlockSpec((1, 2, rows, width), lambda t: (t, 0, 0, 0))
    low_keep, high_keep, *sends = pl.pallas_call(
        functools.partial(add_first_kernel, kinds),
        grid=(half,),
        in_specs=[low, high, low, high],
        out_specs=[part] * 2 + [send] * (2 * kinds),
        out_shape=[jax.ShapeDtypeStruct((half, kinds, 2, rows, width), bf16)] * 2
        + [jax.ShapeDtypeStruct((half, 2, rows, width), bf16)] * (2 * kinds),
        compiler_params=pltpu.CompilerParams(vmem_limit_bytes=60 * 2**20),
        cost_estimate=pl.CostEstimate(flops=own.size, bytes_accessed=6 * own.size, transcendentals=0),
        name="add_first",
    )(own, own, got, got)
    return (low_keep, high_keep), tuple(zip(sends[::2], sends[1::2]))


def add_second_kernel(kinds, low, high, *refs):
    gots, (low_keep, low_send, high_keep, high_send) = refs[: 2 * kinds], refs[2 * kinds :]
    for kind in range(kinds):
        low_got, high_got = gots[2 * kind : 2 * kind + 2]
        low_keep[0, kind] = plus(low[0, kind, 0], low_got[0, 0])
        low_send[0, kind] = plus(low[0, kind, 1], low_got[0, 1])
        high_keep[0, kind] = plus(high[0, kind, 0], high_got[0, 0])
        high_send[0, kind] = plus(high[0, kind, 1], high_got[0, 1])


def add_second(low, high, gots):
    half, kinds, unused, rows, width = low.shape
    part = pl.BlockSpec((1, kinds, 2, rows, width), lambda t: (t, 0, 0, 0, 0))
    got = pl.BlockSpec((1, 2, rows, width), lambda t: (t, 0, 0, 0))
    out = pl.BlockSpec((1, kinds, rows, width), lambda t: (t, 0, 0, 0))
    return pl.pallas_call(
        functools.partial(add_second_kernel, kinds),
        grid=(half,),
        in_specs=[part] * 2 + [got] * (2 * kinds),
        out_specs=[out] * 4,
        out_shape=[jax.ShapeDtypeStruct((half, kinds, rows, width), bf16)] * 4,
        compiler_params=pltpu.CompilerParams(vmem_limit_bytes=60 * 2**20),
        cost_estimate=pl.CostEstimate(flops=2 * low.size, bytes_accessed=12 * low.size, transcendentals=0),
        name="add_second",
    )(low, high, *[part for pair in gots for part in pair])


def add_third_kernel(low, low_got, high, high_got, out):
    out[0, 0] = plus(low[0], low_got[0])
    out[1, 0] = plus(high[0], high_got[0])


def add_third(low, low_got, high, high_got):
    half, kinds, rows, width = low.shape
    part = pl.BlockSpec((1, kinds, rows, width), lambda t: (t, 0, 0, 0))
    out = pl.pallas_call(
        add_third_kernel,
        grid=(half,),
        in_specs=[part] * 4,
        out_specs=pl.BlockSpec((2, 1, kinds, rows, width), lambda t: (0, t, 0, 0, 0)),
        out_shape=jax.ShapeDtypeStruct((2, half, kinds, rows, width), bf16),
        compiler_params=pltpu.CompilerParams(vmem_limit_bytes=60 * 2**20),
        cost_estimate=pl.CostEstimate(flops=2 * low.size, bytes_accessed=12 * low.size, transcendentals=0),
        name="add_third",
    )(low, low_got, high, high_got)
    return out.reshape(2 * half, kinds, rows, width)


class Scatter:
    def __init__(self, grads=None):
        self.plane = square_plane() and grads is not None
        self.keep = self.sent = self.line = ()
        self.moving = () if grads is None else grads
        if self.plane:
            self.keep, send = grads
            self.moving = flip(send, "core")

    def first(self):
        if self.plane:
            self.keep, self.sent = add_first(self.keep, self.moving)
            self.moving = ()

    def start(self):
        if self.plane:
            low, high = self.sent[0]
            self.sent = self.sent[1:]
            self.moving += ((flip(low, "grp"), flip(high, "y")),)

    def second(self):
        if self.plane:
            low, low_send, high, high_send = add_second(*self.keep, self.moving)
            self.keep, self.sent = (low, high), (low_send, high_send)

    def restart(self):
        if self.plane:
            self.moving = (flip(self.sent[0], "y"), flip(self.sent[1], "grp"))

    def third(self):
        if self.plane:
            (low, high), (low_got, high_got) = self.keep, self.moving
            self.line = add_third(low, low_got, high, high_got)

    def finish(self, swapped=False):
        if self.plane and swapped:
            parts = lax.all_to_all(self.line, TENSOR, 0, 0, tiled=True)
            self.moving = jnp.sum(parts.astype(f32), 0)
        elif self.plane:
            self.moving = lax.psum_scatter(self.line, TENSOR, scatter_dimension=0, tiled=False)
        elif not isinstance(self.moving, tuple):
            count, kinds, width, unused = self.moving.shape
            owners = lax.axis_size(("grp", "y", "core"))
            blocks = self.moving.reshape(count, kinds, owners, width // owners, width)
            blocks = blocks.transpose(0, 2, 1, 3, 4).reshape(count * owners, kinds, -1, width)
            self.moving = lax.psum_scatter(blocks, OWNERS, scatter_dimension=0, tiled=False)

    def sums(self):
        return self.moving.astype(f32)


def gather_keys(own):
    far = flip(own, "grp")
    near = flip(own, "core")
    return own, near, far, flip(far, "core")


def gather_head(own, first, second):
    if not square_plane():
        return lax.all_gather(own, HEAD_GROUP, axis=0, tiled=True), flip(first + second, "tl")
    half = own.shape[0] // 2
    got, first = fence(flip(own, "th"), flip(first, "tl"))
    line = jnp.stack([own, got])
    low, high = line[:, :half], line[:, half:]
    low_got, high_got = flip(low, "grp"), flip(high, "y")
    low, high = jnp.stack([low, low_got]), jnp.stack([high, high_got])
    low_got, high_got = flip(low, "y"), flip(high, "grp")
    low_got, high_got, second = fence(low_got, high_got, flip(second, "tl"))
    low, high = jnp.stack([low, low_got]), jnp.stack([high, high_got])
    plane = jnp.stack([low, high])
    whole = jnp.stack([plane, flip(plane, "core")]).reshape(-1, own.shape[1])
    return whole, first + second


def scatter_head(grad):
    if not square_plane():
        return lax.psum_scatter(grad, HEAD_GROUP, scatter_dimension=0, tiled=True).astype(f32)
    width = grad.shape[1]
    blocks = grad.reshape(2, 2, 2, 2, 2, -1, width)
    got = flip(blocks[1], "core")
    low_got = flip(plus(blocks[0, 0, 1], got[0, 1]), "y")
    high_got = flip(plus(blocks[0, 1, 1], got[1, 1]), "grp")
    low, high = plus(blocks[0, 0, 0], got[0, 0]), plus(blocks[0, 1, 0], got[1, 0])
    low_next = flip(plus(low[1], low_got[1]), "grp")
    high_next = flip(plus(high[1], high_got[1]), "y")
    low = plus(plus(low[0], low_got[0]), low_next)
    high = plus(plus(high[0], high_got[0]), high_next)
    line = jnp.concatenate([low, high], 1)
    return line[0].astype(f32) + flip(line[1], "th").astype(f32)


def turned(table):
    for dim, axis in enumerate(HEAD_GROUP):
        table = jnp.where(lax.axis_index(axis) == 1, jnp.flip(table, dim), table)
    return table


def head_order(table):
    if not square_plane():
        return table.reshape(-1)
    table = turned(table)
    half = table.shape[-1] // 2
    low = table[..., :half].transpose(2, 1, 0, 3, 4)
    high = table[..., half:].transpose(2, 0, 1, 3, 4)
    return jnp.stack([low, high], 1).reshape(-1)


def head_table(flat, shape):
    if not square_plane():
        return flat.reshape(shape)
    halves = flat.reshape(2, 2, 2, 2, 2, -1)
    low = halves[:, 0].transpose(2, 1, 0, 3, 4)
    high = halves[:, 1].transpose(1, 2, 0, 3, 4)
    return turned(jnp.concatenate([low, high], -1))


def nn(left, right):
    return lax.dot_general(left, right, (((1,), (0,)), ((), ())), preferred_element_type=f32)


def nt(left, right):
    return lax.dot_general(left, right, (((1,), (1,)), ((), ())), preferred_element_type=f32)


def tn(left, right):
    return lax.dot_general(left, right, (((0,), (0,)), ((), ())), preferred_element_type=f32)


def norm_rows(values, gains):
    centre = values - jnp.mean(values, -1, keepdims=True)
    spread = jnp.mean(centre * centre, -1, keepdims=True)
    return centre * lax.rsqrt(spread + epsilon) * gains[0:1] + gains[1:2]


def norm_rows_back(values, gains, upstream):
    centre = values - jnp.mean(values, -1, keepdims=True)
    inverse = lax.rsqrt(jnp.mean(centre * centre, -1, keepdims=True) + epsilon)
    unit = centre * inverse
    inner = upstream * gains[0:1]
    back = inverse * (
        inner
        - jnp.mean(inner, -1, keepdims=True)
        - unit * jnp.mean(inner * unit, -1, keepdims=True)
    )
    gain = jnp.sum(upstream * unit, 0, keepdims=True)
    bias = jnp.sum(upstream, 0, keepdims=True)
    return back, jnp.concatenate([gain, bias], 0)


TILE = 128


def lanes(rows):
    return lax.broadcasted_iota(jnp.int32, (rows, TILE), 1)


def turn(values, cosine, sine, part):
    half = HEAD // 2
    where = lanes(values.shape[0])
    swapped = jnp.where(
        where % HEAD < half,
        pltpu.roll(values, TILE - half, 1),
        pltpu.roll(values, half, 1),
    )
    turned = values * cosine + swapped * sine
    return turned if part == TILE else jnp.where(where < part, turned, values)


def weight_spec(weight, index):
    array, kind = weight
    unused, blocks, unused, rows, width = array.shape
    return pl.BlockSpec((1, blocks, 1, rows, width), lambda s, *at: (index(s), 0, kind, 0, 0))


def matrix(ref):
    blocks, rows, width = ref.shape[1], ref.shape[3], ref.shape[4]
    return ref[0, :, 0].reshape(blocks * rows, width)


def whole_spec(array):
    zeros = (0,) * array.ndim
    return pl.BlockSpec(array.shape, lambda s: zeros)


def spec(shape, index):
    return pl.BlockSpec(shape, index)


def params(limit=60):
    return pltpu.CompilerParams(vmem_limit_bytes=limit * 2**20)


def cost(flops, moved):
    return pl.CostEstimate(flops=int(flops), bytes_accessed=int(moved), transcendentals=0)


def project_kernel(x, gains, cosine, sine, w, h, q, clean, masked, h_now):
    @pl.when(pl.program_id(0) == 0)
    def begin():
        h_now[...] = norm_rows(x[...], gains[...]).astype(bf16)
        h[...] = h_now[...]

    z = nn(h_now[...], matrix(w)[:, : 5 * TILE])
    cos, sin = cosine[...], sine[...]
    tiles = [z[:, TILE * i : TILE * (i + 1)] for i in range(5)]
    rows = z.shape[0]
    low = lanes(rows) < HEAD
    q[0, :, :TILE] = turn(tiles[0], cos, sin, TILE).astype(bf16)
    q[0, :, TILE:] = jnp.where(low, turn(tiles[4], cos, sin, TILE), 0.0).astype(bf16)
    triple = jnp.concatenate(
        [turn(tiles[1], cos, sin, TILE), tiles[2], turn(tiles[3], cos, sin, HEAD)], 1
    ).astype(bf16)
    span = rows // 2
    clean[...] = triple[:span]
    masked[...] = triple[span:]


def project(x, gains, tables, w):
    rows, width = x.shape
    count = w[0].shape[0]
    span = rows // 2
    triple = spec((span, 3 * TILE), lambda t: (0, t))
    return pl.pallas_call(
        project_kernel,
        grid=(count,),
        in_specs=[whole_spec(x), whole_spec(gains)]
        + [whole_spec(table) for table in tables]
        + [weight_spec(w, lambda t: t)],
        out_specs=[
            spec((rows, width), lambda t: (0, 0)),
            spec((1, rows, 2 * TILE), lambda t: (t, 0, 0)),
            triple,
            triple,
        ],
        out_shape=[
            jax.ShapeDtypeStruct((rows, width), bf16),
            jax.ShapeDtypeStruct((count, rows, 2 * TILE), bf16),
            jax.ShapeDtypeStruct((span, count * 3 * TILE), bf16),
            jax.ShapeDtypeStruct((span, count * 3 * TILE), bf16),
        ],
        scratch_shapes=[pltpu.VMEM((rows, width), bf16)],
        compiler_params=params(),
        cost_estimate=cost(2 * rows * width * width * count, 2 * count * width * width),
        name="project",
    )(x, gains, *tables, w[0])


def head_operands(pair, triple, own, j):
    low = lanes(pair.shape[0]) < HEAD
    if j == 2:
        return pair[:, TILE:], triple[:, 2 * TILE :], 2 * TILE, own[:, 2 * TILE :]
    keep = low if j == 0 else jnp.logical_not(low)
    query = jnp.where(keep, pair[:, :TILE], jnp.zeros((), pair.dtype))
    return query, triple[:, :TILE], TILE, own[:, :TILE]


def head_scores(query, key, own_key, seen):
    span = own_key.shape[0]
    query = query * jnp.asarray(HEAD ** (-0.5), query.dtype)
    score = nt(key, query) + seen
    alone = row_sums(query[span:].astype(f32) * own_key.astype(f32))
    return score, jnp.concatenate([jnp.full((1, query.shape[0] - span), far_below, f32), alone], 1)


def row_sums(values):
    return jnp.sum(values.T, 0, keepdims=True)


def attend_kernel(x, q, k0, k1, k2, k3, own, seen, w, mid, o, log_total):
    rows = x.shape[0]
    span = own.shape[0]

    @pl.when(pl.program_id(0) == 0)
    def begin():
        mid[...] = x[...]

    pair = q[0]
    triple = jnp.concatenate([k0[...], k1[...], k2[...], k3[...]], 0)
    low = lax.broadcasted_iota(jnp.int32, (TILE, rows), 0) < HEAD
    turned = {TILE: triple[:, TILE : 2 * TILE].T, 2 * TILE: triple[:, 2 * TILE :].T}
    own_turned = {start: own[:, start : start + TILE].astype(f32).T for start in turned}
    outs = []
    for j in range(3):
        query, key, value_start, own_key = head_operands(pair, triple, own[...], j)
        score, alone = head_scores(query, key, own_key, seen[...])
        top = jnp.maximum(jnp.max(score, 0, keepdims=True), alone)
        part = jnp.exp(score - top)
        part_alone = jnp.exp(alone - top)
        total = jnp.sum(part, 0, keepdims=True) + part_alone
        inverse = 1.0 / total
        log_total[0, j : j + 1, :] = top + jnp.log(total)
        out = nn(turned[value_start], part.astype(bf16)) * inverse
        weight = (part_alone * inverse).astype(bf16).astype(f32)[:, span:]
        out = jnp.concatenate([out[:, :span], out[:, span:] + weight * own_turned[value_start]], 1)
        outs.append(out)
    both = jnp.concatenate(
        [jnp.where(low, 0.0, outs[2]), jnp.where(low, outs[0], outs[1])], 0
    ).T.astype(bf16)
    o[0] = both
    mid[...] += nt(both, matrix(w)[:, 4 * TILE :])


def attend(x, q, keys, own, seen, w):
    rows, width = x.shape
    count = w[0].shape[0]
    span = own.shape[0]
    triple = spec((span, 3 * TILE), lambda t: (0, t))
    return pl.pallas_call(
        attend_kernel,
        grid=(count,),
        in_specs=[
            whole_spec(x),
            spec((1, rows, 2 * TILE), lambda t: (t, 0, 0)),
            triple, triple, triple, triple, triple,
            whole_spec(seen),
            weight_spec(w, lambda t: t),
        ],
        out_specs=[
            spec((rows, width), lambda t: (0, 0)),
            spec((1, rows, 2 * TILE), lambda t: (t, 0, 0)),
            spec((1, 8, rows), lambda t: (t, 0, 0)),
        ],
        out_shape=[
            jax.ShapeDtypeStruct((rows, width), f32),
            jax.ShapeDtypeStruct((count, rows, 2 * TILE), bf16),
            jax.ShapeDtypeStruct((count, 8, rows), f32),
        ],
        compiler_params=params(),
        cost_estimate=cost(16 * rows * 4 * span * HEAD * count, 2 * count * width * width),
        name="attend",
    )(x, q, *keys, own, seen, w[0])


def gelu_parts(u):
    root = 0.7978845608028654
    square = u * u
    th = jnp.tanh(root * (u + 0.044715 * square * u))
    value = 0.5 * u * (1.0 + th)
    slope = 0.5 * (1.0 + th) + 0.5 * u * (1.0 - th * th) * (root * (1.0 + 3 * 0.044715 * square))
    return value, slope


def feed_kernel(mid, gains, up, down, h2, out):
    @pl.when(pl.program_id(0) == 0)
    def begin():
        h2[...] = norm_rows(mid[...], gains[...]).astype(bf16)
        out[...] = mid[...]

    u = nn(h2[...], matrix(up))
    out[...] += nt(gelu_parts(u)[0].astype(bf16), matrix(down))


def feed(mid, gains, up, down):
    rows, width = mid.shape
    count = up[0].shape[0]
    return pl.pallas_call(
        feed_kernel,
        grid=(count,),
        in_specs=[
            whole_spec(mid), whole_spec(gains),
            weight_spec(up, lambda t: t), weight_spec(down, lambda t: t),
        ],
        out_specs=[spec((rows, width), lambda t: (0, 0))] * 2,
        out_shape=[
            jax.ShapeDtypeStruct((rows, width), bf16),
            jax.ShapeDtypeStruct((rows, width), f32),
        ],
        compiler_params=params(),
        cost_estimate=cost(4 * rows * width * width * count, 4 * count * width * width),
        name="feed",
    )(mid, gains, up[0], down[0])


def feed_back_kernel(
    grad, mid, h2, gains, up, down, grad_low, a, grad_u, grad_mid, mid_low, gain_grad, total
):
    step = pl.program_id(0)

    @pl.when(step == 0)
    def begin():
        grad_low[...] = grad[...].astype(bf16)
        total[...] = jnp.zeros_like(total)

    value, slope = gelu_parts(nn(h2[...], matrix(up)))
    a[...] = value.astype(bf16)
    grad_hidden = (nn(grad_low[...], matrix(down)) * slope).astype(bf16)
    grad_u[...] = grad_hidden
    total[...] += nt(grad_hidden, matrix(up))

    @pl.when(step == pl.num_programs(0) - 1)
    def norm():
        back, gain_grad[...] = norm_rows_back(mid[...], gains[...], total[...])
        back = back + grad[...]
        grad_mid[...] = back
        mid_low[...] = back.astype(bf16)


def feed_back(grad, mid, h2, gains, up, down):
    rows, width = grad.shape
    count = up[0].shape[0]
    hidden = spec((rows, width), lambda t: (0, t))
    plain = spec((rows, width), lambda t: (0, 0))

    def rows_of(kind, columns=width):
        return jax.ShapeDtypeStruct((rows, columns), kind)

    return pl.pallas_call(
        feed_back_kernel,
        grid=(count,),
        in_specs=[plain, plain, plain, whole_spec(gains)]
        + [weight_spec(up, lambda t: t), weight_spec(down, lambda t: t)],
        out_specs=[plain, hidden, hidden, plain, plain, whole_spec(gains)],
        out_shape=[
            rows_of(bf16), rows_of(bf16, count * width), rows_of(bf16, count * width),
            rows_of(f32), rows_of(bf16), jax.ShapeDtypeStruct(gains.shape, f32),
        ],
        scratch_shapes=[pltpu.VMEM((rows, width), f32)],
        compiler_params=params(),
        cost_estimate=cost(6 * rows * width * width * count, 4 * count * width * width),
        name="feed_back",
    )(grad, mid, h2, gains, up[0], down[0])


def attend_back_kernel(
    mid_low, q, k0, k1, k2, k3, own, seen, log_total, cosine, sine, w, grad_q, keep, send, grad_own
):
    rows = mid_low.shape[0]
    span = own.shape[0]
    scale = HEAD ** (-0.5)
    grad_o = nn(mid_low[...], matrix(w)[:, 4 * TILE :]).astype(bf16)
    pair = q[0]
    triple = jnp.concatenate([k0[...], k1[...], k2[...], k3[...]], 0)
    low = lanes(rows) < HEAD
    low_rows = lax.broadcasted_iota(jnp.int32, (TILE, rows), 0) < HEAD
    zero = jnp.zeros((), bf16)
    turned = {0: triple[:, :TILE].T, 2 * TILE: triple[:, 2 * TILE :].T}
    own_turned = {start: own[:, start : start + TILE].astype(f32).T for start in turned}
    query_grads, key_grads, value_grads, own_keys, own_values = [], [], [], [], []
    for j in range(3):
        query, key, value_start, own_key = head_operands(pair, triple, own[...], j)
        key_start = 2 * TILE if j == 2 else 0
        value = triple[:, value_start : value_start + TILE]
        own_value = own[:, value_start : value_start + TILE]
        if j == 2:
            upstream = jnp.where(low, zero, grad_o[:, :TILE])
        else:
            keep_lane = low if j == 0 else jnp.logical_not(low)
            upstream = jnp.where(keep_lane, grad_o[:, TILE:], zero)
        score, alone = head_scores(query, key, own_key, seen[...])
        logs = log_total[0, j : j + 1, :]
        prob = jnp.exp(score - logs)
        prob_alone = jnp.exp(alone - logs)
        dprob = nt(value, upstream)
        lone = upstream[span:].astype(f32)
        dalone = row_sums(lone * own_value.astype(f32))
        dalone = jnp.concatenate([jnp.zeros((1, rows - span), f32), dalone], 1)
        delta = jnp.sum(dprob * prob, 0, keepdims=True) + dalone * prob_alone
        dscore = (prob * (dprob - delta)).astype(bf16)
        dself = (prob_alone * (dalone - delta)).astype(bf16).astype(f32)[:, span:]
        lone_weight = prob_alone.astype(bf16).astype(f32)[:, span:]
        query_grad = nn(turned[key_start], dscore)
        query_grads.append(
            jnp.concatenate(
                [
                    query_grad[:, :span],
                    query_grad[:, span:] + dself * own_turned[key_start],
                ],
                1,
            )
        )
        key_grads.append(nn(dscore, query))
        value_grads.append(nn(prob.astype(bf16), upstream))
        own_keys.append(dself * query[span:].astype(f32).T)
        own_values.append(lone_weight * lone.T)
    cos, sin = cosine[...], -sine[...]
    first = (jnp.where(low_rows, query_grads[0], query_grads[1]) * scale).T
    second = (jnp.where(low_rows, query_grads[2], 0.0) * scale).T
    grad_q[0, :, :TILE] = turn(first, cos, sin, TILE).astype(bf16)
    grad_q[0, :, TILE:] = turn(second, cos, sin, TILE).astype(bf16)
    grads = jnp.concatenate(
        [
            (key_grads[0] + key_grads[1]) * scale,
            value_grads[0] + value_grads[1],
            key_grads[2] * scale + value_grads[2],
        ],
        1,
    ).astype(bf16)
    keep[0] = grads[:span]
    send[0] = grads[span : 2 * span]
    keep[1] = grads[2 * span : 3 * span]
    send[1] = grads[3 * span :]
    grad_own[...] = jnp.concatenate(
        [
            (own_keys[0] + own_keys[1]) * scale,
            own_values[0] + own_values[1],
            own_keys[2] * scale + own_values[2],
        ],
        0,
    ).T


def attend_back(mid_low, q, keys, own, seen, log_total, tables, w):
    rows, width = mid_low.shape
    count = w[0].shape[0]
    span = own.shape[0]
    triple = spec((span, 3 * TILE), lambda t: (0, t))
    pair = spec((1, rows, 2 * TILE), lambda t: (t, 0, 0))
    couple = spec((2, span, 3 * TILE), lambda t: (0, 0, t))
    couple_shape = jax.ShapeDtypeStruct((2, span, count * 3 * TILE), bf16)
    return pl.pallas_call(
        attend_back_kernel,
        grid=(count,),
        in_specs=[spec((rows, width), lambda t: (0, 0)), pair]
        + [triple] * 5
        + [whole_spec(seen), spec((1, 8, rows), lambda t: (t, 0, 0))]
        + [whole_spec(table) for table in tables]
        + [weight_spec(w, lambda t: t)],
        out_specs=[pair, couple, couple, triple],
        out_shape=[
            jax.ShapeDtypeStruct((count, rows, 2 * TILE), bf16),
            couple_shape, couple_shape,
            jax.ShapeDtypeStruct((span, count * 3 * TILE), f32),
        ],
        compiler_params=params(),
        cost_estimate=cost(32 * rows * 4 * span * HEAD * count, 2 * count * width * width),
        name="attend_back",
    )(mid_low, q, *keys, own, seen, log_total, *tables, w[0])


def back_second_kernel(
    keep, got, far, grad_own, grad_q, cosine, sine, x, grad_mid, gains, w, dz, out, gain_grad, total
):
    step = pl.program_id(0)

    @pl.when(step == 0)
    def begin():
        total[...] = jnp.zeros_like(total)

    clean = keep[0].astype(f32) + got[0].astype(f32) + far[...].astype(f32)
    triple = jnp.concatenate([clean, grad_own[...]], 0)
    cos, sin = cosine[...], -sine[...]
    pair = grad_q[0]
    grads = jnp.concatenate(
        [
            pair[:, :TILE],
            turn(triple[:, :TILE], cos, sin, TILE).astype(bf16),
            triple[:, TILE : 2 * TILE].astype(bf16),
            turn(triple[:, 2 * TILE :], cos, sin, HEAD).astype(bf16),
            pair[:, TILE:],
        ],
        1,
    )
    dz[:, : 5 * TILE] = grads
    dz[:, 5 * TILE :] = jnp.zeros_like(pair[:, TILE:])
    total[...] += nt(grads, matrix(w)[:, : 5 * TILE])

    @pl.when(step == pl.num_programs(0) - 1)
    def norm():
        back, gain_grad[...] = norm_rows_back(x[...], gains[...], total[...])
        out[...] = grad_mid[...] + back


def back_second(keep, got, far, grad_own, grad_q, tables, x, grad_mid, gains, w):
    rows, width = x.shape
    count = w[0].shape[0]
    span = rows // 2
    triple = spec((span, 3 * TILE), lambda t: (0, t))
    couple = spec((1, span, 3 * TILE), lambda t: (0, 0, t))
    plain = spec((rows, width), lambda t: (0, 0))
    return pl.pallas_call(
        back_second_kernel,
        grid=(count,),
        in_specs=[couple, couple, triple, triple, spec((1, rows, 2 * TILE), lambda t: (t, 0, 0))]
        + [whole_spec(table) for table in tables]
        + [plain, plain, whole_spec(gains), weight_spec(w, lambda t: t)],
        out_specs=[spec((rows, width), lambda t: (0, t)), plain, whole_spec(gains)],
        out_shape=[
            jax.ShapeDtypeStruct((rows, count * width), bf16),
            jax.ShapeDtypeStruct((rows, width), f32),
            jax.ShapeDtypeStruct(gains.shape, f32),
        ],
        scratch_shapes=[pltpu.VMEM((rows, width), f32)],
        compiler_params=params(),
        cost_estimate=cost(2 * rows * width * width * count, 2 * count * width * width),
        name="back_second",
    )(keep, got, far, grad_own, grad_q, *tables, x, grad_mid, gains, w[0])


def logits_kernel(f, table, *refs):
    target, *parts, stats, other = refs[-5:]
    whole_table(refs[:-5], other)
    block = table.shape[0]
    logits = [nt(f[...], half[...]) for half in (table, other)]
    top = jnp.maximum(*(jnp.max(half, -1, keepdims=True) for half in logits))
    column = lax.broadcasted_iota(jnp.int32, logits[0].shape, 1)
    total, picked = 0.0, 0.0
    for i in range(2):
        part = jnp.exp(logits[i] - top)
        parts[i][...] = part.astype(bf16)
        total = total + jnp.sum(part, -1, keepdims=True)
        chosen = jnp.where(column == target[:, :1] - i * block, logits[i], 0.0)
        picked = picked + jnp.sum(chosen, -1, keepdims=True)
    lane = lanes(f.shape[0])
    stats[...] = jnp.where(lane == 0, top, jnp.where(lane == 1, top + jnp.log(total), picked))


def whole_table(pieces, other):
    @pl.when(pl.program_id(0) == 0)
    def lay():
        start = 0
        for piece in pieces:
            other[start : start + piece.shape[0]] = piece[...]
            start += piece.shape[0]


def head_logits(f, table, pieces, target):
    rows, width = f.shape
    columns = table.shape[0]
    block = 256
    wide = spec((block, columns), lambda i: (i, 0))
    narrow = spec((block, TILE), lambda i: (i, 0))
    *parts, stats = pl.pallas_call(
        logits_kernel,
        grid=(rows // block,),
        in_specs=[spec((block, width), lambda i: (i, 0)), whole_spec(table)]
        + [whole_spec(piece) for piece in pieces]
        + [narrow],
        out_specs=[wide, wide, narrow],
        out_shape=[jax.ShapeDtypeStruct((rows, columns), bf16)] * 2
        + [jax.ShapeDtypeStruct((rows, TILE), f32)],
        scratch_shapes=[pltpu.VMEM(table.shape, bf16)],
        compiler_params=params(60),
        cost_estimate=cost(4 * rows * width * columns, 4 * rows * columns),
        name="head_logits",
    )(f, table, *pieces, target)
    return parts, stats


def logits_back_kernel(first, second, table, *refs):
    target, stats, log_total, *grads, grad_f, other = refs[-7:]
    whole_table(refs[:-7], other)
    block = table.shape[0]
    scale = jnp.exp(stats[:, :1] - log_total[:, :1])
    column = lax.broadcasted_iota(jnp.int32, first.shape, 1)
    total = 0.0
    for i, (part, half) in enumerate(((first, table), (second, other))):
        prob = part[...].astype(f32) * scale
        hit = column == target[:, :1] - i * block
        grads[i][...] = jnp.where(hit, prob - 1.0, prob).astype(bf16)
        total = total + nn(grads[i][...], half[...])
    grad_f[...] = total.astype(bf16)


def head_back(parts, table, pieces, target, stats, log_total):
    rows, columns = parts[0].shape
    width = table.shape[1]
    block = 256
    wide = spec((block, columns), lambda i: (i, 0))
    narrow = spec((block, TILE), lambda i: (i, 0))
    *grads, grad_f = pl.pallas_call(
        logits_back_kernel,
        grid=(rows // block,),
        in_specs=[wide, wide, whole_spec(table)]
        + [whole_spec(piece) for piece in pieces]
        + [narrow] * 3,
        out_specs=[wide, wide, spec((block, width), lambda i: (i, 0))],
        out_shape=[jax.ShapeDtypeStruct((rows, columns), bf16)] * 2
        + [jax.ShapeDtypeStruct((rows, width), bf16)],
        scratch_shapes=[pltpu.VMEM(table.shape, bf16)],
        compiler_params=params(60),
        cost_estimate=cost(4 * rows * width * columns, 8 * rows * columns),
        name="head_back",
    )(
        *parts, table, *pieces, target, stats,
        jnp.broadcast_to(log_total[:, None], (rows, TILE)),
    )
    return grads, grad_f


def update(weight, moment, average, grad, rate):
    fresh_mom = momentum * moment + grad
    fresh_w = weight - rate * (grad + momentum * fresh_mom)
    fresh_avg = average_decay * average + (1.0 - average_decay) * fresh_w
    return (fresh_mom, fresh_w, fresh_avg)


def lookup_plan(ids, block_rows):
    slots = ids.shape[1]
    owner = ids // block_rows
    order = jnp.arange(slots)
    same = ids[:, :, None] == ids[:, None, :]
    lead = jnp.min(jnp.where(same, order[None, None, :], slots), -1)
    first = lead == order
    ahead = jnp.logical_and(
        jnp.logical_and(first[:, None, :], owner[:, :, None] == owner[:, None, :]),
        order[None, None, :] < lead[:, :, None],
    )
    place = jnp.sum(ahead.astype(jnp.int32), -1)
    return owner, place, first


def per_device(
    tokens, positions, lengths,
    embedding, embedding_mom, embedding_avg,
    qkv_w, qkv_mom, qkv_avg,
    out_w, out_mom, out_avg,
    up_w, up_mom, up_avg,
    down_w, down_mom, down_avg,
    norm_gains, gains_mom, gains_avg,
):
    n_grp, n_y, n_t = lax.axis_size("grp"), lax.axis_size("y"), lax.axis_size(TENSOR)
    devices = 2 * n_grp * n_y * n_t
    at_grp, at_y, at_core = (lax.axis_index(name) for name in ALL[:3])
    at_t = lax.axis_index(TENSOR)
    me = lax.axis_index(ALL)
    block_rows, width = embedding.shape
    layers = qkv_w.shape[0]
    micros, unused, rows_here, seq = tokens.shape
    rows = rows_here * 2 * n_y
    span = seq // (2 * n_grp)
    my_row = at_y * n_t + at_t
    my_part = at_grp * 2 + at_core

    packed = jnp.concatenate(
        [tokens, positions, jnp.broadcast_to(lengths[..., None], lengths.shape + (128,))], -1
    )
    packed = lax.all_gather(packed, ("y", "core"), axis=2, tiled=True)
    packed = packed.transpose(1, 0, 2, 3).reshape(2, micros * rows, -1)
    ids_all, places_all, lens_all = packed[..., :seq], packed[..., seq : 2 * seq], packed[..., -1]

    def by_device(table):
        split = table.reshape(n_y, n_t, n_grp, 2, span)
        return split.transpose(2, 0, 3, 1, 4).reshape(devices, span)

    lens = lax.dynamic_index_in_dim(lens_all, my_row, 1, keepdims=False)
    clean_len, masked_len = lens[0], lens[1]
    places = lax.dynamic_slice(places_all, (0, my_row, my_part * span), (2, 1, span))
    tables = rope_tables(places)
    near = jnp.array([0, 1, 0, 1]) ^ at_core
    far = jnp.array([0, 0, 1, 1]) ^ at_grp
    slots = (far * 2 + near)[:, None] * span + jnp.arange(span)[None, :]
    seen = jnp.where(slots.reshape(-1, 1) < clean_len, 0.0, far_below)
    seen = jnp.broadcast_to(seen, (seen.shape[0], 2 * span))

    shards = []
    for layer in range(layers):
        turned_out = out_w[layer].T
        q_part, k_part, v_part = (qkv_w[layer][:, i] for i in range(3))
        attn = [
            q_part[:, :TILE], k_part[:, :TILE], v_part[:, :TILE],
            k_part[:, TILE:], v_part[:, TILE:], q_part[:, TILE:], turned_out[:, TILE:],
            turned_out[:, :TILE],
        ]
        shards.append(
            jnp.stack([jnp.concatenate(attn, 1), up_w[layer], down_w[layer].T]).astype(bf16)
        )
    front = gather_whole(jnp.concatenate([shards[0], shards[1][:2]]))
    rest = gather_whole(shards[1][2:])
    weights = [
        ((front, 0), (front, 1), (front, 2)),
        ((front, 3), (front, 4), (rest, 0)),
    ]
    table = embedding.astype(bf16)

    def my_group(by_dev):
        split = by_dev.reshape(n_grp, n_y, 2, n_t // 2, 2, span)
        return lax.dynamic_index_in_dim(split, at_t % 2, 4, keepdims=False)

    targets = head_order(my_group(by_device(ids_all[1])))
    target_block = targets // block_rows
    targets = targets % block_rows + jnp.where(target_block == me ^ 1, block_rows, 0)
    valid_all = head_order(
        my_group(by_device((jnp.arange(seq)[None, :] < lens_all[1][:, None]).astype(jnp.int32)))
    ) > 0
    targets = jnp.where(jnp.logical_and(target_block | 1 == me | 1, valid_all), targets, -1)
    targets = jnp.broadcast_to(targets[:, None], targets.shape + (TILE,))
    valid_all = valid_all.astype(f32)

    mask_id = block_rows * devices - 1
    wanted = jnp.concatenate(
        [by_device(ids_all[0]), jnp.full((devices, 1), mask_id, jnp.int32)], 1
    )
    owner, place, first = lookup_plan(wanted, block_rows)
    rounds = jnp.max(place) // CAPACITY + 1
    mine = jnp.logical_and(first, owner == me)
    local = wanted - me * block_rows
    my_owner = lax.dynamic_index_in_dim(owner, me, 0, keepdims=False)
    my_place = lax.dynamic_index_in_dim(place, me, 0, keepdims=False)
    my_slot = my_owner * CAPACITY + my_place
    my_slot = jnp.concatenate([my_slot[:span], jnp.broadcast_to(my_slot[span:], (span,))])
    my_place = jnp.concatenate([my_place[:span], jnp.broadcast_to(my_place[span:], (span,))])

    def sent_rows(step):
        at = place - step * CAPACITY
        hit = jnp.logical_and(mine[:, None, :], at[:, None, :] == jnp.arange(CAPACITY)[None, :, None])
        row = jnp.sum(jnp.where(hit, local[:, None, :] + 1, 0), -1).reshape(-1) - 1
        return (row[:, None] == jnp.arange(block_rows)[None, :]).astype(bf16)

    def used_rows(step):
        slot = my_slot - step * CAPACITY
        inside = jnp.logical_and(my_place >= step * CAPACITY, my_place < (step + 1) * CAPACITY)
        slot = jnp.where(inside, slot, -1)
        return (slot[:, None] == jnp.arange(devices * CAPACITY)[None, :]).astype(bf16)

    def swap(values):
        return lax.all_to_all(values, ALL, 0, 0, tiled=True)

    def look(step):
        sent = dot("kv,vd->kd", sent_rows(step), table).astype(bf16)
        return dot("nk,kd->nd", used_rows(step), exchange(sent))

    def exchange(values):
        return take_small(swap(add_small(values, jnp.zeros((devices, width // 2), f32))))[0]

    def add_small(values, small):
        high = small.astype(bf16)
        pair = [high, (small - high.astype(f32)).astype(bf16)]
        pair = [jnp.pad(part, ((0, 0), (0, width // 2 - part.shape[1]))) for part in pair]
        row = jnp.concatenate(pair, 1)[:, None]
        return jnp.concatenate([values.reshape(devices, CAPACITY, width), row], 1)

    def take_small(both):
        row = both[:, CAPACITY].astype(f32)
        return (
            both[:, :CAPACITY].reshape(devices * CAPACITY, width),
            jnp.sum(row[:, : width // 2] + row[:, width // 2 :], 0),
        )

    def look_sent(step, grad):
        return dot("nk,nd->kd", used_rows(step), grad).astype(bf16)

    def look_back(step, grad):
        return dot("kv,kd->vd", sent_rows(step), exchange(look_sent(step, grad)))

    def more(step_fn, begin):
        return lax.while_loop(
            lambda carry: carry[0] < rounds,
            lambda carry: (carry[0] + 1, carry[1] + step_fn(carry[0])),
            (jnp.int32(1), begin),
        )[1]

    x, targets, valid_all = fence(more(look, look(0)), targets, valid_all)

    kept = []
    cuts = [-(-block_rows // 64) * 16 * i for i in range(1, 4)]
    table_parts = [[part] for part in jnp.split(table, cuts)]
    for layer in range(layers):
        attn, upper, lower = weights[layer]
        h, q, clean, own = project(x, norm_gains[2 * layer], tables, attn)
        keys = gather_keys(clean)
        if layer == layers - 1:
            q, table_parts = fence(q, table_parts)
        arriving = table_parts if layer == layers - 1 else [(), (), (), ()]
        got = flip(arriving[0], "tl")
        mid, o, log_total = attend(x, q, keys, own, seen, attn)
        mid, got = fence(mid, got)
        other_table = got
        got = flip(arriving[1], "tl")
        h2, after = feed(mid, norm_gains[2 * layer + 1], upper, lower)
        after, got = fence(after, got)
        other_table += got
        kept.append((x, h, q, keys, own, o, log_total, mid, h2))
        x = after

    last = x[span:]
    f_mine = layer_norm(last, norm_gains[2 * layers, 0], norm_gains[2 * layers, 1]).astype(bf16)
    f_all, got = gather_head(f_mine, *table_parts[2:])
    other_table += got

    parts_low, stats = head_logits(f_all, table, other_table, targets)
    part_total = head_table(stats[:, 1], (n_grp, n_y, 2, n_t // 2, span))
    group = lax.axis_size(HEAD_GROUP)
    parts = lax.all_to_all(
        jnp.broadcast_to(part_total.reshape(1, -1), (group, group * span)),
        HEAD_GROUP, 0, 0, tiled=True,
    )
    top = jnp.max(parts, 0)
    log_total = top + jnp.log(jnp.sum(jnp.exp(parts - top), 0))
    own_total = lax.dynamic_slice(log_total, (lax.axis_index(HEAD_GROUP) * span,), (span,))
    log_total = head_order(log_total.reshape(part_total.shape))
    target_part = jnp.sum(jnp.where(valid_all > 0.0, stats[:, 2], 0.0))
    own_valid = my_part * span + jnp.arange(span) < masked_len
    loss_part = jnp.sum(jnp.where(own_valid, own_total, 0.0)) - target_part
    log_total = jnp.where(valid_all > 0.0, log_total, -far_below)
    grad_logits, grad_f = head_back(parts_low, table, other_table, targets, stats, log_total)
    grad_f = scatter_head(grad_f)

    back, gain_final, bias_final = norm_back(
        last, norm_gains[2 * layers, 0], norm_gains[2 * layers, 1], grad_f
    )
    grad_x = jnp.concatenate([jnp.zeros_like(back), back], 0)
    last_gains = jnp.stack([gain_final, bias_final])[None]
    grad_x, last_gains, loss_part = fence(grad_x, last_gains, loss_part)
    gain_parts = [None] * layers
    pieces, table_got = [[], [], [], []], []
    nothing = Scatter()
    outer = inner = nothing
    owned = []
    for layer in reversed(range(layers)):
        attn, upper, lower = weights[layer]
        before, h, q, keys, own, o, log_total, mid, h2 = kept[layer]
        first_step = inner is nothing

        outer.restart()
        beside = flip(pieces[0], "tl")
        fed = feed_back(grad_x, mid, h2, norm_gains[2 * layer + 1], upper, lower)
        fed, inner.moving, outer.moving, beside = fence(fed, inner.moving, outer.moving, beside)
        grad_low, a, grad_u, grad_mid, mid_low, gain_mid = fed
        table_got += beside

        outer.third()
        inner.first()
        inner.sent, outer.line = fence(inner.sent, outer.line)
        outer.finish()
        grads = weight_grads([(h2, grad_u), (grad_low, a)])
        mid_low, grads, inner.sent = fence(mid_low, grads, inner.sent)

        outer = Scatter(grads)
        inner.start()
        beside = flip(pieces[1], "tl")
        passed = attend_back(mid_low, q, keys, own, seen, log_total, tables, attn)
        passed, outer.moving, inner.moving, beside = fence(
            passed, outer.moving, inner.moving, beside
        )
        grad_q, keep, send, grad_own = passed
        table_got += beside

        got = flip(send, "core")
        inner.second()
        keep, got, inner.sent = fence(keep, got, inner.sent)

        far = plus(keep[1], got[1])
        far, outer.moving = fence(far, outer.moving)

        far = flip(far, "grp")
        outer.first()
        far, outer.sent, inner.sent = fence(far, outer.sent, inner.sent)

        inner.restart()
        if not first_step:
            outer.start()
        backed = back_second(
            keep, got, far, grad_own, grad_q, tables, before, grad_mid, norm_gains[2 * layer], attn
        )
        backed, outer.sent, outer.moving, inner.moving = fence(
            backed, outer.sent, outer.moving, inner.moving
        )
        dz, grad_x, gain_in = backed
        gain_parts[layer] = jnp.stack([gain_in, gain_mid])

        if first_step:
            outer.start()
        outer.start()
        beside = flip(pieces[2], "tl")
        grads = weight_grads([(h, dz)], (mid_low, o))
        sent = ()
        if first_step:
            grad_logits, dz = fence(grad_logits, dz)
            own_table, beside_table = (dot("nv,nd->vd", part, f_all) for part in grad_logits)
            pieces = [[piece] for piece in jnp.split(beside_table.astype(bf16), cuts)]
        if layer == 0:
            grad_low = grad_x.astype(bf16)
            gains_grad = jnp.concatenate(gain_parts + [last_gains], 0)
            small = jnp.concatenate([gains_grad.reshape(-1), loss_part[None]])
            small = jnp.pad(small, (0, -small.size % (devices * 128))).reshape(devices, -1)
            sent = add_small(look_sent(0, grad_low), small)
        grad_x, grads, pieces, outer.moving, beside, sent = fence(
            grad_x, grads, pieces, outer.moving, beside, sent
        )
        table_got += beside

        owned.append(outer)
        last, inner = inner, Scatter(grads)
        owned.append(inner)
        outer.second()
        if layer == 0:
            inner.moving, last.moving, outer.sent = fence(inner.moving, last.moving, outer.sent)
            inner.first()
        outer.sent, inner.moving, last.moving, inner.sent = fence(
            outer.sent, inner.moving, last.moving, inner.sent
        )
        last.third()
        last.finish()

    outer.restart()
    inner.start()
    got_rows = swap(sent)
    beside = flip(pieces[3], "tl")
    inner.moving, outer.moving, got_rows, beside = fence(
        inner.moving, outer.moving, got_rows, beside
    )
    table_got += beside

    inner.second()
    inner.sent, outer.moving = fence(inner.sent, outer.moving)

    inner.restart()
    outer.third()
    inner.moving, outer.line = fence(inner.moving, outer.line)
    outer.finish()

    inner.third()
    got_rows, inner.line, own_table, table_got = fence(
        got_rows, inner.line, own_table, table_got
    )
    inner.finish(True)
    got_rows, small = take_small(got_rows)
    grad_table = own_table + jnp.concatenate(table_got).astype(f32)
    grad_table = grad_table + dot("kv,kd->vd", sent_rows(0), got_rows)
    grad_table = more(lambda step: look_back(step, grad_low), grad_table)
    owned = [
        [owned[2 * i + 1].sums()[0], owned[2 * i].sums()[0], owned[2 * i].sums()[1]]
        for i in reversed(range(layers))
    ]

    mask_count = jnp.sum(lens_all[1]).astype(f32)
    squares = jnp.sum(grad_table * grad_table, 0)
    for part in owned[0] + owned[1]:
        squares = squares + jnp.sum(part * part, 0)
    small = small[: -(-(gains_grad.size + 1) // (devices * 128)) * 128]
    shared = jnp.concatenate([small, squares])
    shared = swap(jnp.broadcast_to(shared[None], (devices, shared.size)))
    squares = jnp.sum(shared[:, small.size :])
    small = shared[:, : small.size].reshape(-1)
    gains_total = small[: gains_grad.size].reshape(gains_grad.shape)
    loss_sum = small[gains_grad.size]
    squares = squares + jnp.sum(gains_total * gains_total)
    grad_norm = jnp.sqrt(squares) / mask_count
    factor = jnp.minimum(1.0, threshold / grad_norm) / mask_count

    qkv_grads, out_grads = [], []
    for part in owned:
        tiles = jnp.split(part[0], 2 * width // TILE, 1)
        q_pair, k_pair, v_pair = (
            jnp.concatenate(tiles[2 * i : 2 * i + 2], 1) for i in range(3)
        )
        qkv_grads.append(
            jnp.stack(
                [
                    jnp.concatenate([q_pair, tiles[8]], 1),
                    jnp.concatenate([k_pair, tiles[6]], 1),
                    jnp.concatenate([v_pair, tiles[7]], 1),
                ],
                1,
            )
        )
        out_grads.append(jnp.concatenate([tiles[10], tiles[11], tiles[9]], 1).T)
    qkv_grad, out_grad = jnp.stack(qkv_grads), jnp.stack(out_grads)
    up_grad = jnp.stack([part[1] for part in owned])
    down_grad = jnp.stack([part[2].T for part in owned])
    results = [loss_sum, mask_count, grad_norm]
    for weight, moment, average, grad, rate in (
        (embedding, embedding_mom, embedding_avg, grad_table, rate_matrix),
        (qkv_w, qkv_mom, qkv_avg, qkv_grad, rate_matrix),
        (out_w, out_mom, out_avg, out_grad, rate_matrix),
        (up_w, up_mom, up_avg, up_grad, rate_matrix),
        (down_w, down_mom, down_avg, down_grad, rate_matrix),
        (norm_gains, gains_mom, gains_avg, gains_total, rate_gains),
    ):
        results += update(weight, moment, average, grad * factor, rate)
    return tuple(results)


def solution(mesh):
    n_grp, n_dp, n_t = mesh.devices.shape
    split = Mesh(mesh.devices.reshape(n_grp, n_dp // 2, 2, n_t // 2, 2), ALL)
    dp = ("y", "core")
    owners = ("grp", "y", "core")
    rows = P(None, None, dp, None)
    table = P(ALL, None)
    wide = P(None, owners, None, TENSOR)
    tall = P(None, TENSOR, owners)
    flat = P(None, owners, TENSOR)
    return jax.shard_map(
        per_device,
        mesh=split,
        in_specs=(rows, rows, P(None, None, dp))
        + (table,) * 3 + (wide,) * 3 + (tall,) * 3 + (flat,) * 3 + (tall,) * 3 + (P(),) * 3,
        out_specs=(P(),) * 3
        + (table,) * 3 + (wide,) * 3 + (tall,) * 3 + (flat,) * 3 + (tall,) * 3 + (P(),) * 3,
        check_vma=False,
    )
```

```python
import functools

import jax
import jax.numpy as jnp
from jax import lax
from jax.experimental import pallas as pl
from jax.experimental.pallas import tpu as pltpu
from jax.sharding import Mesh
from jax.sharding import PartitionSpec as P

HEAD = 64
CAPACITY = 15

epsilon = 1e-05
threshold = 0.05
momentum = 0.9
average_decay = 0.75
rate_matrix = 2000.0
rate_gains = 5000.0
far_below = -1e30
bf16 = jnp.bfloat16
f32 = jnp.float32
TENSOR = ("th", "tl")
ALL = ("grp", "y", "core", "th", "tl")
OWNERS = ("th", "tl", "grp", "y", "core")
HEAD_GROUP = ("grp", "y", "core", "th")


def layer_norm(values, gain, bias):
    centre = values - jnp.mean(values, -1, keepdims=True)
    spread = jnp.mean(centre * centre, -1, keepdims=True)
    return centre * lax.rsqrt(spread + epsilon) * gain + bias


def norm_back(values, gain, bias, upstream):
    unused, pullback = jax.vjp(layer_norm, values, gain, bias)
    return pullback(upstream)


def rope_tables(places):
    half_size = HEAD // 2
    lane = jnp.arange(TILE)
    frequency = 10000.0 ** (-(lane % half_size).astype(f32) / half_size)
    sign = jnp.where(lane % HEAD < half_size, -1.0, 1.0)
    angles = places.reshape(-1).astype(f32)[:, None] * frequency[None, :]
    return jnp.cos(angles), jnp.sin(angles) * sign


def dot(form, left, right):
    return jnp.einsum(form, left, right, preferred_element_type=f32)


def flip(values, axis):
    return lax.ppermute(values, axis, [(0, 1), (1, 0)])


def square_plane():
    return lax.axis_size("grp") == 2 and lax.axis_size("y") == 2


def coordinates():
    return jnp.stack([lax.axis_index("grp"), lax.axis_index("y"), lax.axis_index("core")])


def fence(*groups):
    return lax.optimization_barrier(groups)


def gather_whole(shards):
    kinds, rows, width = shards.shape
    everything = lax.all_gather(shards, OWNERS, axis=0, tiled=False)
    count = lax.axis_size(TENSOR)
    everything = everything.reshape(count, -1, kinds, rows, width)
    if rows % 16 == 0:
        return everything
    return everything.transpose(0, 2, 1, 3, 4).reshape(count, 1, kinds, -1, width)


def weight_grad_kernel(inputs, extra, at, *refs):
    xs, ys = refs[:inputs], refs[inputs : 2 * inputs]
    keep_ref, send_ref, turned, tile = refs[2 * inputs :]
    blocks, rows, width = tile.shape

    @pl.when(pl.program_id(0) == 0)
    def begin():
        for i in range(inputs):
            turned[i] = xs[i][...].T

    for kind in range(inputs - extra):
        grad = nn(turned[kind], ys[kind][...])
        if extra:
            more = nn(turned[1], ys[1][0])
            split = width - more.shape[1]
            grad = jnp.concatenate([grad[:, :split], grad[:, split:] + more], 1)
        tile[...] = grad.astype(bf16).reshape(blocks, rows, width)
        for by_x in range(2):
            for by_y in range(2):
                for core, ref in enumerate((keep_ref, send_ref)):
                    block = ((at[0] ^ by_x) * 2 + (at[1] ^ by_y)) * 2 + (at[2] ^ core)
                    ref[0, kind, by_x, by_y] = tile[block]


def weight_grads(pairs, extra=None):
    kinds = len(pairs)
    slots, width = pairs[0][0].shape
    count = pairs[0][1].shape[1] // width
    rows = width // 8
    if not square_plane():
        whole = [dot("nd,ntf->tdf", x, y.reshape(slots, count, width)) for x, y in pairs]
        if extra:
            more = dot("nd,tnf->tdf", *extra)
            whole[0] += jnp.pad(more, ((0, 0), (0, 0), (width - more.shape[2], 0)))
        return jnp.stack([part.astype(bf16) for part in whole], 1)
    part = pl.BlockSpec((1, kinds, 2, 2, rows, width), lambda t, at: (t, 0, 0, 0, 0, 0))
    shape = jax.ShapeDtypeStruct((count, kinds, 2, 2, rows, width), bf16)
    x_spec = pl.BlockSpec((slots, width), lambda t, at: (0, 0))
    x_specs = [x_spec] * kinds
    y_specs = [pl.BlockSpec((slots, width), lambda t, at: (0, t))] * kinds
    xs = [x for x, unused in pairs]
    ys = [y for unused, y in pairs]
    if extra:
        xs.append(extra[0])
        ys.append(extra[1])
        x_specs.append(x_spec)
        y_specs.append(pl.BlockSpec((1,) + extra[1].shape[1:], lambda t, at: (t, 0, 0)))
    return pl.pallas_call(
        functools.partial(weight_grad_kernel, len(xs), bool(extra)),
        grid_spec=pltpu.PrefetchScalarGridSpec(
            num_scalar_prefetch=1,
            grid=(count,),
            in_specs=x_specs + y_specs,
            out_specs=[part, part],
            scratch_shapes=[
                pltpu.VMEM((len(xs), width, slots), bf16),
                pltpu.VMEM((8, rows, width), bf16),
            ],
        ),
        out_shape=[shape, shape],
        compiler_params=pltpu.CompilerParams(vmem_limit_bytes=60 * 2**20),
        cost_estimate=pl.CostEstimate(
            flops=2 * slots * width * width * count * kinds,
            bytes_accessed=2 * count * kinds * width * (slots + width),
            transcendentals=0,
        ),
        name="weight_grads",
    )(coordinates(), *xs, *ys)


def plus(left, right):
    return (left.astype(f32) + right.astype(f32)).astype(bf16)


def add_first_kernel(kinds, own_low, own_high, got_low, got_high, low_keep, high_keep, *sends):
    low_keep[0] = plus(own_low[0, :, 0], got_low[0, :, 0])
    high_keep[0] = plus(own_high[0, :, :, 0], got_high[0, :, :, 0])
    for kind in range(kinds):
        low_send, high_send = sends[2 * kind : 2 * kind + 2]
        low_send[0] = plus(own_low[0, kind, 1], got_low[0, kind, 1])
        high_send[0] = plus(own_high[0, kind, :, 1], got_high[0, kind, :, 1])


def add_first(own, got):
    count, kinds, unused, unused, rows, width = own.shape
    half = count // 2
    low = pl.BlockSpec((1, kinds, 2, 2, rows, width), lambda t: (t, 0, 0, 0, 0, 0))
    high = pl.BlockSpec((1, kinds, 2, 2, rows, width), lambda t: (t + half, 0, 0, 0, 0, 0))
    part = pl.BlockSpec((1, kinds, 2, rows, width), lambda t: (t, 0, 0, 0, 0))
    send = pl.BlockSpec((1, 2, rows, width), lambda t: (t, 0, 0, 0))
    low_keep, high_keep, *sends = pl.pallas_call(
        functools.partial(add_first_kernel, kinds),
        grid=(half,),
        in_specs=[low, high, low, high],
        out_specs=[part] * 2 + [send] * (2 * kinds),
        out_shape=[jax.ShapeDtypeStruct((half, kinds, 2, rows, width), bf16)] * 2
        + [jax.ShapeDtypeStruct((half, 2, rows, width), bf16)] * (2 * kinds),
        compiler_params=pltpu.CompilerParams(vmem_limit_bytes=60 * 2**20),
        cost_estimate=pl.CostEstimate(flops=own.size, bytes_accessed=6 * own.size, transcendentals=0),
        name="add_first",
    )(own, own, got, got)
    return (low_keep, high_keep), tuple(zip(sends[::2], sends[1::2]))


def add_second_kernel(kinds, low, high, *refs):
    gots, (low_keep, low_send, high_keep, high_send) = refs[: 2 * kinds], refs[2 * kinds :]
    for kind in range(kinds):
        low_got, high_got = gots[2 * kind : 2 * kind + 2]
        low_keep[0, kind] = plus(low[0, kind, 0], low_got[0, 0])
        low_send[0, kind] = plus(low[0, kind, 1], low_got[0, 1])
        high_keep[0, kind] = plus(high[0, kind, 0], high_got[0, 0])
        high_send[0, kind] = plus(high[0, kind, 1], high_got[0, 1])


def add_second(low, high, gots):
    half, kinds, unused, rows, width = low.shape
    part = pl.BlockSpec((1, kinds, 2, rows, width), lambda t: (t, 0, 0, 0, 0))
    got = pl.BlockSpec((1, 2, rows, width), lambda t: (t, 0, 0, 0))
    out = pl.BlockSpec((1, kinds, rows, width), lambda t: (t, 0, 0, 0))
    return pl.pallas_call(
        functools.partial(add_second_kernel, kinds),
        grid=(half,),
        in_specs=[part] * 2 + [got] * (2 * kinds),
        out_specs=[out] * 4,
        out_shape=[jax.ShapeDtypeStruct((half, kinds, rows, width), bf16)] * 4,
        compiler_params=pltpu.CompilerParams(vmem_limit_bytes=60 * 2**20),
        cost_estimate=pl.CostEstimate(flops=2 * low.size, bytes_accessed=12 * low.size, transcendentals=0),
        name="add_second",
    )(low, high, *[part for pair in gots for part in pair])


def add_third_kernel(low, low_got, high, high_got, out):
    out[0, 0] = plus(low[0], low_got[0])
    out[1, 0] = plus(high[0], high_got[0])


def add_third(low, low_got, high, high_got):
    half, kinds, rows, width = low.shape
    part = pl.BlockSpec((1, kinds, rows, width), lambda t: (t, 0, 0, 0))
    out = pl.pallas_call(
        add_third_kernel,
        grid=(half,),
        in_specs=[part] * 4,
        out_specs=pl.BlockSpec((2, 1, kinds, rows, width), lambda t: (0, t, 0, 0, 0)),
        out_shape=jax.ShapeDtypeStruct((2, half, kinds, rows, width), bf16),
        compiler_params=pltpu.CompilerParams(vmem_limit_bytes=60 * 2**20),
        cost_estimate=pl.CostEstimate(flops=2 * low.size, bytes_accessed=12 * low.size, transcendentals=0),
        name="add_third",
    )(low, low_got, high, high_got)
    return out.reshape(2 * half, kinds, rows, width)


class Scatter:
    def __init__(self, grads=None):
        self.plane = square_plane() and grads is not None
        self.keep = self.sent = self.line = ()
        self.moving = () if grads is None else grads
        if self.plane:
            self.keep, send = grads
            self.moving = flip(send, "core")

    def first(self):
        if self.plane:
            self.keep, self.sent = add_first(self.keep, self.moving)
            self.moving = ()

    def start(self):
        if self.plane:
            low, high = self.sent[0]
            self.sent = self.sent[1:]
            self.moving += ((flip(low, "grp"), flip(high, "y")),)

    def second(self):
        if self.plane:
            low, low_send, high, high_send = add_second(*self.keep, self.moving)
            self.keep, self.sent = (low, high), (low_send, high_send)

    def restart(self):
        if self.plane:
            self.moving = (flip(self.sent[0], "y"), flip(self.sent[1], "grp"))

    def third(self):
        if self.plane:
            (low, high), (low_got, high_got) = self.keep, self.moving
            self.line = add_third(low, low_got, high, high_got)

    def finish(self, swapped=False):
        if self.plane and swapped:
            parts = lax.all_to_all(self.line, TENSOR, 0, 0, tiled=True)
            self.moving = jnp.sum(parts.astype(f32), 0)
        elif self.plane:
            self.moving = lax.psum_scatter(self.line, TENSOR, scatter_dimension=0, tiled=False)
        elif not isinstance(self.moving, tuple):
            count, kinds, width, unused = self.moving.shape
            owners = lax.axis_size(("grp", "y", "core"))
            blocks = self.moving.reshape(count, kinds, owners, width // owners, width)
            blocks = blocks.transpose(0, 2, 1, 3, 4).reshape(count * owners, kinds, -1, width)
            self.moving = lax.psum_scatter(blocks, OWNERS, scatter_dimension=0, tiled=False)

    def sums(self):
        return self.moving.astype(f32)


def gather_keys(own):
    far = flip(own, "grp")
    near = flip(own, "core")
    return own, near, far, flip(far, "core")


def gather_head(own, first, second):
    if not square_plane():
        return lax.all_gather(own, HEAD_GROUP, axis=0, tiled=True), flip(first + second, "tl")
    half = own.shape[0] // 2
    got, first = fence(flip(own, "th"), flip(first, "tl"))
    line = jnp.stack([own, got])
    low, high = line[:, :half], line[:, half:]
    low_got, high_got = flip(low, "grp"), flip(high, "y")
    low, high = jnp.stack([low, low_got]), jnp.stack([high, high_got])
    low_got, high_got = flip(low, "y"), flip(high, "grp")
    low_got, high_got, second = fence(low_got, high_got, flip(second, "tl"))
    low, high = jnp.stack([low, low_got]), jnp.stack([high, high_got])
    plane = jnp.stack([low, high])
    whole = jnp.stack([plane, flip(plane, "core")]).reshape(-1, own.shape[1])
    return whole, first + second


def scatter_head(send, keep, work):
    if not square_plane():
        grad = jnp.concatenate([keep, send])
        return lax.psum_scatter(grad, HEAD_GROUP, scatter_dimension=0, tiled=True).astype(f32), work()
    width = keep.shape[1]
    got = flip(send, "core").reshape(2, 2, 2, 2, -1, width)
    blocks = keep.reshape(2, 2, 2, 2, -1, width)
    low_send, high_send = plus(blocks[0, 1], got[0, 1]), plus(blocks[1, 1], got[1, 1])
    low, high = plus(blocks[0, 0], got[0, 0]), plus(blocks[1, 0], got[1, 0])
    low, high, low_send, high_send = fence(low, high, low_send, high_send)
    low_got, high_got = flip(low_send, "y"), flip(high_send, "grp")
    low_got, high_got, low, high, done = fence(low_got, high_got, low, high, work())
    low_next = flip(plus(low[1], low_got[1]), "grp")
    high_next = flip(plus(high[1], high_got[1]), "y")
    low = plus(plus(low[0], low_got[0]), low_next)
    high = plus(plus(high[0], high_got[0]), high_next)
    line = jnp.concatenate([low, high], 1)
    return line[0].astype(f32) + flip(line[1], "th").astype(f32), done


def turned(table):
    for dim, axis in enumerate(HEAD_GROUP):
        table = jnp.where(lax.axis_index(axis) == 1, jnp.flip(table, dim), table)
    return table


def head_order(table):
    if not square_plane():
        return table.reshape(-1)
    table = turned(table)
    half = table.shape[-1] // 2
    low = table[..., :half].transpose(2, 1, 0, 3, 4)
    high = table[..., half:].transpose(2, 0, 1, 3, 4)
    return jnp.stack([low, high], 1).reshape(-1)


def head_table(flat, shape):
    if not square_plane():
        return flat.reshape(shape)
    halves = flat.reshape(2, 2, 2, 2, 2, -1)
    low = halves[:, 0].transpose(2, 1, 0, 3, 4)
    high = halves[:, 1].transpose(1, 2, 0, 3, 4)
    return turned(jnp.concatenate([low, high], -1))


def nn(left, right):
    return lax.dot_general(left, right, (((1,), (0,)), ((), ())), preferred_element_type=f32)


def nt(left, right):
    return lax.dot_general(left, right, (((1,), (1,)), ((), ())), preferred_element_type=f32)


def tn(left, right):
    return lax.dot_general(left, right, (((0,), (0,)), ((), ())), preferred_element_type=f32)


def norm_rows(values, gains):
    centre = values - jnp.mean(values, -1, keepdims=True)
    spread = jnp.mean(centre * centre, -1, keepdims=True)
    return centre * lax.rsqrt(spread + epsilon) * gains[0:1] + gains[1:2]


def norm_rows_back(values, gains, upstream):
    centre = values - jnp.mean(values, -1, keepdims=True)
    inverse = lax.rsqrt(jnp.mean(centre * centre, -1, keepdims=True) + epsilon)
    unit = centre * inverse
    inner = upstream * gains[0:1]
    back = inverse * (
        inner
        - jnp.mean(inner, -1, keepdims=True)
        - unit * jnp.mean(inner * unit, -1, keepdims=True)
    )
    gain = jnp.sum(upstream * unit, 0, keepdims=True)
    bias = jnp.sum(upstream, 0, keepdims=True)
    return back, jnp.concatenate([gain, bias], 0)


TILE = 128


def lanes(rows):
    return lax.broadcasted_iota(jnp.int32, (rows, TILE), 1)


def turn(values, cosine, sine, part):
    half = HEAD // 2
    where = lanes(values.shape[0])
    swapped = jnp.where(
        where % HEAD < half,
        pltpu.roll(values, TILE - half, 1),
        pltpu.roll(values, half, 1),
    )
    turned = values * cosine + swapped * sine
    return turned if part == TILE else jnp.where(where < part, turned, values)


def weight_spec(weight, index):
    array, kind = weight
    unused, blocks, unused, rows, width = array.shape
    return pl.BlockSpec((1, blocks, 1, rows, width), lambda s, *at: (index(s), 0, kind, 0, 0))


def matrix(ref):
    blocks, rows, width = ref.shape[1], ref.shape[3], ref.shape[4]
    return ref[0, :, 0].reshape(blocks * rows, width)


def whole_spec(array):
    zeros = (0,) * array.ndim
    return pl.BlockSpec(array.shape, lambda s: zeros)


def spec(shape, index):
    return pl.BlockSpec(shape, index)


def params(limit=60):
    return pltpu.CompilerParams(vmem_limit_bytes=limit * 2**20)


def cost(flops, moved):
    return pl.CostEstimate(flops=int(flops), bytes_accessed=int(moved), transcendentals=0)


def project_kernel(x, gains, cosine, sine, w, h, q, clean, masked, h_now):
    @pl.when(pl.program_id(0) == 0)
    def begin():
        h_now[...] = norm_rows(x[...], gains[...]).astype(bf16)
        h[...] = h_now[...]

    z = nn(h_now[...], matrix(w)[:, : 5 * TILE])
    cos, sin = cosine[...], sine[...]
    tiles = [z[:, TILE * i : TILE * (i + 1)] for i in range(5)]
    rows = z.shape[0]
    low = lanes(rows) < HEAD
    q[0, :, :TILE] = turn(tiles[0], cos, sin, TILE).astype(bf16)
    q[0, :, TILE:] = jnp.where(low, turn(tiles[4], cos, sin, TILE), 0.0).astype(bf16)
    triple = jnp.concatenate(
        [turn(tiles[1], cos, sin, TILE), tiles[2], turn(tiles[3], cos, sin, HEAD)], 1
    ).astype(bf16)
    span = rows // 2
    clean[...] = triple[:span]
    masked[...] = triple[span:]


def project(x, gains, tables, w):
    rows, width = x.shape
    count = w[0].shape[0]
    span = rows // 2
    triple = spec((span, 3 * TILE), lambda t: (0, t))
    return pl.pallas_call(
        project_kernel,
        grid=(count,),
        in_specs=[whole_spec(x), whole_spec(gains)]
        + [whole_spec(table) for table in tables]
        + [weight_spec(w, lambda t: t)],
        out_specs=[
            spec((rows, width), lambda t: (0, 0)),
            spec((1, rows, 2 * TILE), lambda t: (t, 0, 0)),
            triple,
            triple,
        ],
        out_shape=[
            jax.ShapeDtypeStruct((rows, width), bf16),
            jax.ShapeDtypeStruct((count, rows, 2 * TILE), bf16),
            jax.ShapeDtypeStruct((span, count * 3 * TILE), bf16),
            jax.ShapeDtypeStruct((span, count * 3 * TILE), bf16),
        ],
        scratch_shapes=[pltpu.VMEM((rows, width), bf16)],
        compiler_params=params(),
        cost_estimate=cost(2 * rows * width * width * count, 2 * count * width * width),
        name="project",
    )(x, gains, *tables, w[0])


def head_operands(pair, triple, own, j):
    low = lanes(pair.shape[0]) < HEAD
    if j == 2:
        return pair[:, TILE:], triple[:, 2 * TILE :], 2 * TILE, own[:, 2 * TILE :]
    keep = low if j == 0 else jnp.logical_not(low)
    query = jnp.where(keep, pair[:, :TILE], jnp.zeros((), pair.dtype))
    return query, triple[:, :TILE], TILE, own[:, :TILE]


def head_scores(query, key, own_key, seen):
    span = own_key.shape[0]
    query = query * jnp.asarray(HEAD ** (-0.5), query.dtype)
    score = nt(key, query) + seen
    alone = row_sums(query[span:].astype(f32) * own_key.astype(f32))
    return score, jnp.concatenate([jnp.full((1, query.shape[0] - span), far_below, f32), alone], 1)


def row_sums(values):
    return jnp.sum(values.T, 0, keepdims=True)


def attend_kernel(x, q, k0, k1, k2, k3, own, seen, w, mid, o, log_total):
    rows = x.shape[0]
    span = own.shape[0]

    @pl.when(pl.program_id(0) == 0)
    def begin():
        mid[...] = x[...]

    pair = q[0]
    triple = jnp.concatenate([k0[...], k1[...], k2[...], k3[...]], 0)
    low = lax.broadcasted_iota(jnp.int32, (TILE, rows), 0) < HEAD
    turned = {TILE: triple[:, TILE : 2 * TILE].T, 2 * TILE: triple[:, 2 * TILE :].T}
    own_turned = {start: own[:, start : start + TILE].astype(f32).T for start in turned}
    outs = []
    for j in range(3):
        query, key, value_start, own_key = head_operands(pair, triple, own[...], j)
        score, alone = head_scores(query, key, own_key, seen[...])
        top = jnp.maximum(jnp.max(score, 0, keepdims=True), alone)
        part = jnp.exp(score - top)
        part_alone = jnp.exp(alone - top)
        total = jnp.sum(part, 0, keepdims=True) + part_alone
        inverse = 1.0 / total
        log_total[0, j : j + 1, :] = top + jnp.log(total)
        out = nn(turned[value_start], part.astype(bf16)) * inverse
        weight = (part_alone * inverse).astype(bf16).astype(f32)[:, span:]
        out = jnp.concatenate([out[:, :span], out[:, span:] + weight * own_turned[value_start]], 1)
        outs.append(out)
    both = jnp.concatenate(
        [jnp.where(low, 0.0, outs[2]), jnp.where(low, outs[0], outs[1])], 0
    ).T.astype(bf16)
    o[0] = both
    mid[...] += nt(both, matrix(w)[:, 4 * TILE :])


def attend(x, q, keys, own, seen, w):
    rows, width = x.shape
    count = w[0].shape[0]
    span = own.shape[0]
    triple = spec((span, 3 * TILE), lambda t: (0, t))
    return pl.pallas_call(
        attend_kernel,
        grid=(count,),
        in_specs=[
            whole_spec(x),
            spec((1, rows, 2 * TILE), lambda t: (t, 0, 0)),
            triple, triple, triple, triple, triple,
            whole_spec(seen),
            weight_spec(w, lambda t: t),
        ],
        out_specs=[
            spec((rows, width), lambda t: (0, 0)),
            spec((1, rows, 2 * TILE), lambda t: (t, 0, 0)),
            spec((1, 8, rows), lambda t: (t, 0, 0)),
        ],
        out_shape=[
            jax.ShapeDtypeStruct((rows, width), f32),
            jax.ShapeDtypeStruct((count, rows, 2 * TILE), bf16),
            jax.ShapeDtypeStruct((count, 8, rows), f32),
        ],
        compiler_params=params(),
        cost_estimate=cost(16 * rows * 4 * span * HEAD * count, 2 * count * width * width),
        name="attend",
    )(x, q, *keys, own, seen, w[0])


def gelu_parts(u):
    root = 0.7978845608028654
    square = u * u
    th = jnp.tanh(root * (u + 0.044715 * square * u))
    value = 0.5 * u * (1.0 + th)
    slope = 0.5 * (1.0 + th) + 0.5 * u * (1.0 - th * th) * (root * (1.0 + 3 * 0.044715 * square))
    return value, slope


def feed_kernel(mid, gains, up, down, *refs):
    *last, h2, out = refs

    @pl.when(pl.program_id(0) == 0)
    def begin():
        h2[...] = norm_rows(mid[...], gains[...]).astype(bf16)
        out[...] = mid[...]

    u = nn(h2[...], matrix(up))
    out[...] += nt(gelu_parts(u)[0].astype(bf16), matrix(down))
    if last:
        last_gains, final = last

        @pl.when(pl.program_id(0) == pl.num_programs(0) - 1)
        def end():
            final[...] = norm_rows(out[final.shape[0] :], last_gains[...]).astype(bf16)


def feed(mid, gains, up, down, last_gains=None):
    rows, width = mid.shape
    count = up[0].shape[0]
    plain = spec((rows, width), lambda t: (0, 0))
    last = last_gains is not None

    def call(*operands):
        specs = [whole_spec(mid), whole_spec(gains)]
        specs += [weight_spec(up, lambda t: t), weight_spec(down, lambda t: t)]
        shapes = [
            jax.ShapeDtypeStruct((rows, width), bf16),
            jax.ShapeDtypeStruct((rows, width), f32),
        ]
        outs = [plain, plain]
        if last:
            specs.append(whole_spec(last_gains))
            shapes.insert(0, jax.ShapeDtypeStruct((rows // 2, width), bf16))
            outs.insert(0, spec((rows // 2, width), lambda t: (0, 0)))
        return pl.pallas_call(
            feed_kernel,
            grid=(count,),
            in_specs=specs,
            out_specs=outs,
            out_shape=shapes,
            compiler_params=params(),
            cost_estimate=cost(4 * rows * width * width * count, 4 * count * width * width),
            name="feed",
        )(*operands)

    return call(mid, gains, up[0], down[0], *([last_gains] if last else []))


def feed_back_kernel(
    grad, mid, h2, gains, up, down, grad_low, a, grad_u, grad_mid, mid_low, gain_grad, total
):
    step = pl.program_id(0)

    @pl.when(step == 0)
    def begin():
        grad_low[...] = grad[...].astype(bf16)
        total[...] = jnp.zeros_like(total)

    value, slope = gelu_parts(nn(h2[...], matrix(up)))
    a[...] = value.astype(bf16)
    grad_hidden = (nn(grad_low[...], matrix(down)) * slope).astype(bf16)
    grad_u[...] = grad_hidden
    total[...] += nt(grad_hidden, matrix(up))

    @pl.when(step == pl.num_programs(0) - 1)
    def norm():
        back, gain_grad[...] = norm_rows_back(mid[...], gains[...], total[...])
        back = back + grad[...]
        grad_mid[...] = back
        mid_low[...] = back.astype(bf16)


def feed_back(grad, mid, h2, gains, up, down):
    rows, width = grad.shape
    count = up[0].shape[0]
    hidden = spec((rows, width), lambda t: (0, t))
    plain = spec((rows, width), lambda t: (0, 0))

    def rows_of(kind, columns=width):
        return jax.ShapeDtypeStruct((rows, columns), kind)

    return pl.pallas_call(
        feed_back_kernel,
        grid=(count,),
        in_specs=[plain, plain, plain, whole_spec(gains)]
        + [weight_spec(up, lambda t: t), weight_spec(down, lambda t: t)],
        out_specs=[plain, hidden, hidden, plain, plain, whole_spec(gains)],
        out_shape=[
            rows_of(bf16), rows_of(bf16, count * width), rows_of(bf16, count * width),
            rows_of(f32), rows_of(bf16), jax.ShapeDtypeStruct(gains.shape, f32),
        ],
        scratch_shapes=[pltpu.VMEM((rows, width), f32)],
        compiler_params=params(),
        cost_estimate=cost(6 * rows * width * width * count, 4 * count * width * width),
        name="feed_back",
    )(grad, mid, h2, gains, up[0], down[0])


def attend_back_kernel(
    mid_low, q, k0, k1, k2, k3, own, seen, log_total, cosine, sine, w, grad_q, keep, send, grad_own
):
    rows = mid_low.shape[0]
    span = own.shape[0]
    scale = HEAD ** (-0.5)
    grad_o = nn(mid_low[...], matrix(w)[:, 4 * TILE :]).astype(bf16)
    pair = q[0]
    triple = jnp.concatenate([k0[...], k1[...], k2[...], k3[...]], 0)
    low = lanes(rows) < HEAD
    low_rows = lax.broadcasted_iota(jnp.int32, (TILE, rows), 0) < HEAD
    zero = jnp.zeros((), bf16)
    turned = {0: triple[:, :TILE].T, 2 * TILE: triple[:, 2 * TILE :].T}
    own_turned = {start: own[:, start : start + TILE].astype(f32).T for start in turned}
    query_grads, key_grads, value_grads, own_keys, own_values = [], [], [], [], []
    for j in range(3):
        query, key, value_start, own_key = head_operands(pair, triple, own[...], j)
        key_start = 2 * TILE if j == 2 else 0
        value = triple[:, value_start : value_start + TILE]
        own_value = own[:, value_start : value_start + TILE]
        if j == 2:
            upstream = jnp.where(low, zero, grad_o[:, :TILE])
        else:
            keep_lane = low if j == 0 else jnp.logical_not(low)
            upstream = jnp.where(keep_lane, grad_o[:, TILE:], zero)
        score, alone = head_scores(query, key, own_key, seen[...])
        logs = log_total[0, j : j + 1, :]
        prob = jnp.exp(score - logs)
        prob_alone = jnp.exp(alone - logs)
        dprob = nt(value, upstream)
        lone = upstream[span:].astype(f32)
        dalone = row_sums(lone * own_value.astype(f32))
        dalone = jnp.concatenate([jnp.zeros((1, rows - span), f32), dalone], 1)
        delta = jnp.sum(dprob * prob, 0, keepdims=True) + dalone * prob_alone
        dscore = (prob * (dprob - delta)).astype(bf16)
        dself = (prob_alone * (dalone - delta)).astype(bf16).astype(f32)[:, span:]
        lone_weight = prob_alone.astype(bf16).astype(f32)[:, span:]
        query_grad = nn(turned[key_start], dscore)
        query_grads.append(
            jnp.concatenate(
                [
                    query_grad[:, :span],
                    query_grad[:, span:] + dself * own_turned[key_start],
                ],
                1,
            )
        )
        key_grads.append(nn(dscore, query))
        value_grads.append(nn(prob.astype(bf16), upstream))
        own_keys.append(dself * query[span:].astype(f32).T)
        own_values.append(lone_weight * lone.T)
    cos, sin = cosine[...], -sine[...]
    first = (jnp.where(low_rows, query_grads[0], query_grads[1]) * scale).T
    second = (jnp.where(low_rows, query_grads[2], 0.0) * scale).T
    grad_q[0, :, :TILE] = turn(first, cos, sin, TILE).astype(bf16)
    grad_q[0, :, TILE:] = turn(second, cos, sin, TILE).astype(bf16)
    grads = jnp.concatenate(
        [
            (key_grads[0] + key_grads[1]) * scale,
            value_grads[0] + value_grads[1],
            key_grads[2] * scale + value_grads[2],
        ],
        1,
    ).astype(bf16)
    keep[0] = grads[:span]
    send[0] = grads[span : 2 * span]
    keep[1] = grads[2 * span : 3 * span]
    send[1] = grads[3 * span :]
    grad_own[...] = jnp.concatenate(
        [
            (own_keys[0] + own_keys[1]) * scale,
            own_values[0] + own_values[1],
            own_keys[2] * scale + own_values[2],
        ],
        0,
    ).T


def attend_back(mid_low, q, keys, own, seen, log_total, tables, w):
    rows, width = mid_low.shape
    count = w[0].shape[0]
    span = own.shape[0]
    triple = spec((span, 3 * TILE), lambda t: (0, t))
    pair = spec((1, rows, 2 * TILE), lambda t: (t, 0, 0))
    couple = spec((2, span, 3 * TILE), lambda t: (0, 0, t))
    couple_shape = jax.ShapeDtypeStruct((2, span, count * 3 * TILE), bf16)
    return pl.pallas_call(
        attend_back_kernel,
        grid=(count,),
        in_specs=[spec((rows, width), lambda t: (0, 0)), pair]
        + [triple] * 5
        + [whole_spec(seen), spec((1, 8, rows), lambda t: (t, 0, 0))]
        + [whole_spec(table) for table in tables]
        + [weight_spec(w, lambda t: t)],
        out_specs=[pair, couple, couple, triple],
        out_shape=[
            jax.ShapeDtypeStruct((count, rows, 2 * TILE), bf16),
            couple_shape, couple_shape,
            jax.ShapeDtypeStruct((span, count * 3 * TILE), f32),
        ],
        compiler_params=params(),
        cost_estimate=cost(32 * rows * 4 * span * HEAD * count, 2 * count * width * width),
        name="attend_back",
    )(mid_low, q, *keys, own, seen, log_total, *tables, w[0])


def back_second_kernel(
    keep, got, far, grad_own, grad_q, cosine, sine, x, grad_mid, gains, w, dz, out, gain_grad, total
):
    step = pl.program_id(0)

    @pl.when(step == 0)
    def begin():
        total[...] = jnp.zeros_like(total)

    clean = keep[0].astype(f32) + got[0].astype(f32) + far[...].astype(f32)
    triple = jnp.concatenate([clean, grad_own[...]], 0)
    cos, sin = cosine[...], -sine[...]
    pair = grad_q[0]
    grads = jnp.concatenate(
        [
            pair[:, :TILE],
            turn(triple[:, :TILE], cos, sin, TILE).astype(bf16),
            triple[:, TILE : 2 * TILE].astype(bf16),
            turn(triple[:, 2 * TILE :], cos, sin, HEAD).astype(bf16),
            pair[:, TILE:],
        ],
        1,
    )
    dz[:, : 5 * TILE] = grads
    dz[:, 5 * TILE :] = jnp.zeros_like(pair[:, TILE:])
    total[...] += nt(grads, matrix(w)[:, : 5 * TILE])

    @pl.when(step == pl.num_programs(0) - 1)
    def norm():
        back, gain_grad[...] = norm_rows_back(x[...], gains[...], total[...])
        out[...] = grad_mid[...] + back


def back_second(keep, got, far, grad_own, grad_q, tables, x, grad_mid, gains, w):
    rows, width = x.shape
    count = w[0].shape[0]
    span = rows // 2
    triple = spec((span, 3 * TILE), lambda t: (0, t))
    couple = spec((1, span, 3 * TILE), lambda t: (0, 0, t))
    plain = spec((rows, width), lambda t: (0, 0))
    return pl.pallas_call(
        back_second_kernel,
        grid=(count,),
        in_specs=[couple, couple, triple, triple, spec((1, rows, 2 * TILE), lambda t: (t, 0, 0))]
        + [whole_spec(table) for table in tables]
        + [plain, plain, whole_spec(gains), weight_spec(w, lambda t: t)],
        out_specs=[spec((rows, width), lambda t: (0, t)), plain, whole_spec(gains)],
        out_shape=[
            jax.ShapeDtypeStruct((rows, count * width), bf16),
            jax.ShapeDtypeStruct((rows, width), f32),
            jax.ShapeDtypeStruct(gains.shape, f32),
        ],
        scratch_shapes=[pltpu.VMEM((rows, width), f32)],
        compiler_params=params(),
        cost_estimate=cost(2 * rows * width * width * count, 2 * count * width * width),
        name="back_second",
    )(keep, got, far, grad_own, grad_q, *tables, x, grad_mid, gains, w[0])


def logits_kernel(f, table, *refs):
    target, *parts, stats, other = refs[-5:]
    whole_table(refs[:-5], other)
    block = table.shape[0]
    column = lax.broadcasted_iota(jnp.int32, (f.shape[0], block), 1)
    tops, totals, picked = [], [], 0.0
    for i, half in enumerate((table, other)):
        logits = nt(f[...], half[...])
        top = jnp.max(logits, -1, keepdims=True)
        part = jnp.exp(logits - top)
        parts[i][...] = part.astype(bf16)
        tops.append(top)
        totals.append(jnp.sum(part, -1, keepdims=True))
        chosen = jnp.where(column == target[:, :1] - i * block, logits, 0.0)
        picked = picked + jnp.sum(chosen, -1, keepdims=True)
    top = jnp.maximum(*tops)
    total = sum(totals[i] * jnp.exp(tops[i] - top) for i in range(2))
    lane = lanes(f.shape[0])
    columns = jnp.where(lane == 0, tops[0], jnp.where(lane == 3, tops[1], picked))
    columns = jnp.where(lane == 1, top + jnp.log(total), columns)
    stats[0] = columns.T[: stats.shape[1]]


def whole_table(pieces, other):
    @pl.when(pl.program_id(0) == 0)
    def lay():
        start = 0
        for piece in pieces:
            other[start : start + piece.shape[0]] = piece[...]
            start += piece.shape[0]


def head_logits(f, table, pieces, target):
    rows, width = f.shape
    columns = table.shape[0]
    block = 256
    wide = spec((block, columns), lambda i: (i, 0))
    narrow = spec((block, TILE), lambda i: (i, 0))
    *parts, stats = pl.pallas_call(
        logits_kernel,
        grid=(rows // block,),
        in_specs=[spec((block, width), lambda i: (i, 0)), whole_spec(table)]
        + [whole_spec(piece) for piece in pieces]
        + [narrow],
        out_specs=[wide, wide, spec((1, 8, block), lambda i: (i, 0, 0))],
        out_shape=[jax.ShapeDtypeStruct((rows, columns), bf16)] * 2
        + [jax.ShapeDtypeStruct((rows // block, 8, block), f32)],
        scratch_shapes=[pltpu.VMEM(table.shape, bf16)],
        compiler_params=params(60),
        cost_estimate=cost(4 * rows * width * columns, 4 * rows * columns),
        name="head_logits",
    )(f, table, *pieces, target)
    return parts, stats


def logits_back_kernel(first, second, table, *refs):
    target, top, log_total, *grads, send, keep, other = refs[-8:]
    whole_table(refs[:-8], other)
    block = table.shape[0]
    scales = jnp.exp(top[0] - log_total[0])
    scales = jnp.concatenate([scales] * (TILE // scales.shape[0]), 0).T
    column = lax.broadcasted_iota(jnp.int32, first.shape, 1)
    total = 0.0
    for i, (part, half) in enumerate(((first, table), (second, other))):
        prob = part[...].astype(f32) * scales[:, 3 * i : 3 * i + 1]
        hit = column == target[:, :1] - i * block
        grads[i][...] = jnp.where(hit, prob - 1.0, prob).astype(bf16)
        total = total + nn(grads[i][...], half[...])
    total = total.astype(bf16)
    early = pl.program_id(0) < pl.num_programs(0) // 2

    @pl.when(early)
    def to_keep():
        keep[...] = total

    @pl.when(jnp.logical_not(early))
    def to_send():
        send[...] = total


def head_back(parts, table, pieces, target, stats, log_total):
    rows, columns = parts[0].shape
    width = table.shape[1]
    block = stats.shape[2]
    half = rows // block // 2
    wide = spec((block, columns), lambda i: (i, 0))
    *grads, send, keep = pl.pallas_call(
        logits_back_kernel,
        grid=(rows // block,),
        in_specs=[wide, wide, whole_spec(table)]
        + [whole_spec(piece) for piece in pieces]
        + [
            spec((block, TILE), lambda i: (i, 0)),
            spec((1, 8, block), lambda i: (i, 0, 0)),
            spec((1, 1, block), lambda i: (i, 0, 0)),
        ],
        out_specs=[
            wide, wide,
            spec((block, width), lambda i: (jnp.maximum(i - half, 0), 0)),
            spec((block, width), lambda i: (jnp.minimum(i, half - 1), 0)),
        ],
        out_shape=[jax.ShapeDtypeStruct((rows, columns), bf16)] * 2
        + [jax.ShapeDtypeStruct((rows // 2, width), bf16)] * 2,
        scratch_shapes=[pltpu.VMEM(table.shape, bf16)],
        compiler_params=params(60),
        cost_estimate=cost(4 * rows * width * columns, 8 * rows * columns),
        name="head_back",
    )(*parts, table, *pieces, target, stats, log_total)
    return grads, send, keep


def update(weight, moment, average, grad, rate):
    fresh_mom = momentum * moment + grad
    fresh_w = weight - rate * (grad + momentum * fresh_mom)
    fresh_avg = average_decay * average + (1.0 - average_decay) * fresh_w
    return (fresh_mom, fresh_w, fresh_avg)


def update_turned_kernel(factor, weight, moment, average, *refs):
    *grads, new_moment, new_weight, new_average = refs
    for layer, grad in enumerate(grads):
        turned = grad[...].T * factor[0, 0]
        new_moment[layer], new_weight[layer], new_average[layer] = update(
            weight[layer], moment[layer], average[layer], turned, rate_matrix
        )


def update_turned(weight, moment, average, grads, factor):
    if not square_plane():
        turned = jnp.stack([grad.T for grad in grads])
        return update(weight, moment, average, turned * factor, rate_matrix)
    return pl.pallas_call(
        update_turned_kernel,
        in_specs=[pl.BlockSpec(memory_space=pltpu.SMEM)]
        + [pl.BlockSpec(memory_space=pltpu.VMEM)] * (3 + len(grads)),
        out_specs=[pl.BlockSpec(memory_space=pltpu.VMEM)] * 3,
        out_shape=[jax.ShapeDtypeStruct(weight.shape, f32)] * 3,
        compiler_params=params(),
        name="update_turned",
    )(factor.reshape(1, 1), weight, moment, average, *grads)


def lookup_plan(ids, block_rows):
    slots = ids.shape[1]
    owner = ids // block_rows
    order = jnp.arange(slots)
    same = ids[:, :, None] == ids[:, None, :]
    lead = jnp.min(jnp.where(same, order[None, None, :], slots), -1)
    first = lead == order
    ahead = jnp.logical_and(
        jnp.logical_and(first[:, None, :], owner[:, :, None] == owner[:, None, :]),
        order[None, None, :] < lead[:, :, None],
    )
    place = jnp.sum(ahead.astype(jnp.int32), -1)
    return owner, place, first


def per_device(
    tokens, positions, lengths,
    embedding, embedding_mom, embedding_avg,
    qkv_w, qkv_mom, qkv_avg,
    out_w, out_mom, out_avg,
    up_w, up_mom, up_avg,
    down_w, down_mom, down_avg,
    norm_gains, gains_mom, gains_avg,
):
    n_grp, n_y, n_t = lax.axis_size("grp"), lax.axis_size("y"), lax.axis_size(TENSOR)
    devices = 2 * n_grp * n_y * n_t
    at_grp, at_y, at_core = (lax.axis_index(name) for name in ALL[:3])
    at_t = lax.axis_index(TENSOR)
    me = lax.axis_index(ALL)
    block_rows, width = embedding.shape
    layers = qkv_w.shape[0]
    micros, unused, rows_here, seq = tokens.shape
    rows = rows_here * 2 * n_y
    span = seq // (2 * n_grp)
    my_row = at_y * n_t + at_t
    my_part = at_grp * 2 + at_core

    packed = jnp.concatenate(
        [tokens, positions, jnp.broadcast_to(lengths[..., None], lengths.shape + (128,))], -1
    )
    packed = lax.all_gather(packed, ("y", "core"), axis=2, tiled=True)
    packed = packed.transpose(1, 0, 2, 3).reshape(2, micros * rows, -1)
    ids_all, places_all, lens_all = packed[..., :seq], packed[..., seq : 2 * seq], packed[..., -1]

    def by_device(table):
        split = table.reshape(n_y, n_t, n_grp, 2, span)
        return split.transpose(2, 0, 3, 1, 4).reshape(devices, span)

    shards = []
    for layer in range(layers):
        turned_out = out_w[layer].T
        q_part, k_part, v_part = (qkv_w[layer][:, i] for i in range(3))
        attn = [
            q_part[:, :TILE], k_part[:, :TILE], v_part[:, :TILE],
            k_part[:, TILE:], v_part[:, TILE:], q_part[:, TILE:], turned_out[:, TILE:],
            turned_out[:, :TILE],
        ]
        shards.append(
            jnp.stack([jnp.concatenate(attn, 1), up_w[layer], down_w[layer].T]).astype(bf16)
        )
    front = gather_whole(jnp.concatenate([shards[0], shards[1][:2]]))
    rest = gather_whole(shards[1][2:])
    weights = [
        ((front, 0), (front, 1), (front, 2)),
        ((front, 3), (front, 4), (rest, 0)),
    ]
    table = embedding.astype(bf16)

    def my_group(by_dev):
        split = by_dev.reshape(n_grp, n_y, 2, n_t // 2, 2, span)
        return lax.dynamic_index_in_dim(split, at_t % 2, 4, keepdims=False)

    mask_id = block_rows * devices - 1
    wanted = jnp.concatenate(
        [by_device(ids_all[0]), jnp.full((devices, 1), mask_id, jnp.int32)], 1
    )
    owner, place, first = lookup_plan(wanted, block_rows)
    rounds = jnp.max(place) // CAPACITY + 1
    mine = jnp.logical_and(first, owner == me)
    local = wanted - me * block_rows
    my_owner = lax.dynamic_index_in_dim(owner, me, 0, keepdims=False)
    my_place = lax.dynamic_index_in_dim(place, me, 0, keepdims=False)
    my_slot = my_owner * CAPACITY + my_place
    my_slot = jnp.concatenate([my_slot[:span], jnp.broadcast_to(my_slot[span:], (span,))])
    my_place = jnp.concatenate([my_place[:span], jnp.broadcast_to(my_place[span:], (span,))])

    def sent_rows(step):
        at = place - step * CAPACITY
        hit = jnp.logical_and(mine[:, None, :], at[:, None, :] == jnp.arange(CAPACITY)[None, :, None])
        row = jnp.sum(jnp.where(hit, local[:, None, :] + 1, 0), -1).reshape(-1) - 1
        return (row[:, None] == jnp.arange(block_rows)[None, :]).astype(bf16)

    def used_rows(step):
        slot = my_slot - step * CAPACITY
        inside = jnp.logical_and(my_place >= step * CAPACITY, my_place < (step + 1) * CAPACITY)
        slot = jnp.where(inside, slot, -1)
        return (slot[:, None] == jnp.arange(devices * CAPACITY)[None, :]).astype(bf16)

    def swap(values):
        return lax.all_to_all(values, ALL, 0, 0, tiled=True)

    def look(step):
        sent = dot("kv,vd->kd", sent_rows(step), table).astype(bf16)
        return dot("nk,kd->nd", used_rows(step), exchange(sent))

    def exchange(values):
        return take_small(swap(add_small(values, jnp.zeros((devices, width // 2), f32))))[0]

    def add_small(values, small):
        high = small.astype(bf16)
        pair = [high, (small - high.astype(f32)).astype(bf16)]
        pair = [jnp.pad(part, ((0, 0), (0, width // 2 - part.shape[1]))) for part in pair]
        row = jnp.concatenate(pair, 1)[:, None]
        return jnp.concatenate([values.reshape(devices, CAPACITY, width), row], 1)

    def take_small(both):
        row = both[:, CAPACITY].astype(f32)
        return (
            both[:, :CAPACITY].reshape(devices * CAPACITY, width),
            jnp.sum(row[:, : width // 2] + row[:, width // 2 :], 0),
        )

    def look_sent(step, grad):
        return dot("nk,nd->kd", used_rows(step), grad).astype(bf16)

    def look_back(step, grad):
        return dot("kv,kd->vd", sent_rows(step), exchange(look_sent(step, grad)))

    def more(step_fn, begin):
        return lax.while_loop(
            lambda carry: carry[0] < rounds,
            lambda carry: (carry[0] + 1, carry[1] + step_fn(carry[0])),
            (jnp.int32(1), begin),
        )[1]

    cuts = [int(block_rows * part) // 16 * 16 for part in (0.26, 0.43, 0.63)]
    x, parted, ids_all, places_all, lens_all = fence(
        more(look, look(0)), table, ids_all, places_all, lens_all
    )

    lens = lax.dynamic_index_in_dim(lens_all, my_row, 1, keepdims=False)
    clean_len, masked_len = lens[0], lens[1]
    places = lax.dynamic_slice(places_all, (0, my_row, my_part * span), (2, 1, span))
    tables = rope_tables(places)
    near = jnp.array([0, 1, 0, 1]) ^ at_core
    far = jnp.array([0, 0, 1, 1]) ^ at_grp
    slots = (far * 2 + near)[:, None] * span + jnp.arange(span)[None, :]
    seen = jnp.where(slots.reshape(-1, 1) < clean_len, 0.0, far_below)
    seen = jnp.broadcast_to(seen, (seen.shape[0], 2 * span))

    targets = head_order(my_group(by_device(ids_all[1])))
    target_block = targets // block_rows
    targets = targets % block_rows + jnp.where(target_block == me ^ 1, block_rows, 0)
    valid_all = head_order(
        my_group(by_device((jnp.arange(seq)[None, :] < lens_all[1][:, None]).astype(jnp.int32)))
    ) > 0
    targets = jnp.where(jnp.logical_and(target_block | 1 == me | 1, valid_all), targets, -1)
    targets = jnp.broadcast_to(targets[:, None], targets.shape + (TILE,))
    valid_all = valid_all.astype(f32)

    table_parts = [[part] for part in jnp.split(parted, cuts)]
    x, targets, valid_all, seen, tables, table_parts = fence(
        x, targets, valid_all, seen, tables, table_parts
    )

    kept = []
    for layer in range(layers):
        attn, upper, lower = weights[layer]
        h, q, clean, own = project(x, norm_gains[2 * layer], tables, attn)
        keys = gather_keys(clean)
        if layer == layers - 1:
            q, table_parts = fence(q, table_parts)
        arriving = table_parts if layer == layers - 1 else [(), (), (), ()]
        got = flip(arriving[0], "tl")
        mid, o, log_total = attend(x, q, keys, own, seen, attn)
        mid, got = fence(mid, got)
        other_table = got
        got = flip(arriving[1], "tl")
        final_gains = norm_gains[2 * layers] if layer == layers - 1 else None
        *f_mine, h2, after = feed(mid, norm_gains[2 * layer + 1], upper, lower, final_gains)
        f_mine, after, got = fence(f_mine, after, got)
        other_table += got
        kept.append((x, h, q, keys, own, o, log_total, mid, h2))
        x = after

    last = x[span:]
    f_all, got = gather_head(f_mine[0], *table_parts[2:])
    other_table += got

    parts_low, stats = head_logits(f_all, table, other_table, targets)
    part_total = head_table(stats[:, 1].reshape(-1), (n_grp, n_y, 2, n_t // 2, span))
    group = lax.axis_size(HEAD_GROUP)
    parts = lax.all_to_all(
        jnp.broadcast_to(part_total.reshape(1, -1), (group, group * span)),
        HEAD_GROUP, 0, 0, tiled=True,
    )
    top = jnp.max(parts, 0)
    log_total = top + jnp.log(jnp.sum(jnp.exp(parts - top), 0))
    own_total = lax.dynamic_slice(log_total, (lax.axis_index(HEAD_GROUP) * span,), (span,))
    log_total = head_order(log_total.reshape(part_total.shape))
    target_part = jnp.sum(jnp.where(valid_all > 0.0, stats[:, 2].reshape(-1), 0.0))
    own_valid = my_part * span + jnp.arange(span) < masked_len
    loss_part = jnp.sum(jnp.where(own_valid, own_total, 0.0)) - target_part
    log_total = jnp.where(valid_all > 0.0, log_total, -far_below)
    grad_logits, *grad_f = head_back(
        parts_low, table, other_table, targets, stats, log_total.reshape(stats.shape[0], 1, -1)
    )

    def beside_table():
        return dot("nv,nd->vd", grad_logits[1], f_all).astype(bf16)

    grad_f, pieces = scatter_head(*grad_f, beside_table)
    back_cuts = [int(block_rows * part) // 16 * 16 for part in (0.2, 0.43, 0.71)]
    grad_f, pieces = fence(grad_f, [[piece] for piece in jnp.split(pieces, back_cuts)])

    back, gain_final, bias_final = norm_back(
        last, norm_gains[2 * layers, 0], norm_gains[2 * layers, 1], grad_f
    )
    grad_x = jnp.concatenate([jnp.zeros_like(back), back], 0)
    last_gains = jnp.stack([gain_final, bias_final])[None]
    grad_x, last_gains, loss_part = fence(grad_x, last_gains, loss_part)
    def unpack(inner, outer):
        attn, (up, down) = inner.sums()[0], outer.sums()
        squares = sum(jnp.sum(part * part, 0) for part in (attn, up, down))
        tiles = jnp.split(attn, 2 * width // TILE, 1)
        columns = [[0, 1, 8], [2, 3, 6], [4, 5, 7]]
        qkv = jnp.stack([jnp.concatenate([tiles[i] for i in part], 1) for part in columns], 1)
        out = jnp.concatenate([tiles[10], tiles[11], tiles[9]], 1)
        return squares, (qkv, out, up, down.T)

    gain_parts = [None] * layers
    table_got = []
    nothing = Scatter()
    outer = inner = nothing
    owned = []
    for layer in reversed(range(layers)):
        attn, upper, lower = weights[layer]
        before, h, q, keys, own, o, log_total, mid, h2 = kept[layer]
        first_step = inner is nothing

        outer.restart()
        beside = flip(pieces[0], "tl")
        fed = feed_back(grad_x, mid, h2, norm_gains[2 * layer + 1], upper, lower)
        inner.first()
        fed, inner.sent, outer.moving, beside = fence(fed, inner.sent, outer.moving, beside)
        grad_low, a, grad_u, grad_mid, mid_low, gain_mid = fed
        table_got += beside

        inner.start()
        outer.third()
        grads = weight_grads([(h2, grad_u), (grad_low, a)])
        mid_low, grads, inner.moving, outer.line = fence(
            mid_low, grads, inner.moving, outer.line
        )

        inner.second()
        mid_low, inner.sent = fence(mid_low, inner.sent)

        last_outer, outer = outer, Scatter(grads)
        last_outer.finish()
        inner.restart()
        beside = flip(pieces[1], "tl")
        passed = attend_back(mid_low, q, keys, own, seen, log_total, tables, attn)
        passed, outer.moving, inner.moving, beside = fence(
            passed, outer.moving, inner.moving, beside
        )
        table_got += beside
        grad_q, keep, send, grad_own = passed

        got = flip(send, "core")
        inner.third()
        keep, got, inner.line = fence(keep, got, inner.line)

        far = plus(keep[1], got[1])
        far, outer.moving = fence(far, outer.moving)

        far = flip(far, "grp")
        outer.first()
        far, outer.sent = fence(far, outer.sent)

        inner.finish()
        beside = flip(pieces[2], "tl")
        outer.start()
        backed = back_second(
            keep, got, far, grad_own, grad_q, tables, before, grad_mid, norm_gains[2 * layer], attn
        )
        backed, outer.sent, outer.moving, last_outer.moving, beside = fence(
            backed, outer.sent, outer.moving, last_outer.moving, beside
        )
        table_got += beside
        dz, grad_x, gain_in = backed
        gain_parts[layer] = jnp.stack([gain_in, gain_mid])

        outer.start()
        beside = flip(pieces[3], "tl")
        grads = weight_grads([(h, dz)], (mid_low, o))
        sent = ()
        if first_step:
            grad_logits, dz = fence(grad_logits, dz)
            own_table = dot("nv,nd->vd", grad_logits[0], f_all)
        if layer == 0:
            grad_low = grad_x.astype(bf16)
            gains_grad = jnp.concatenate(gain_parts + [last_gains], 0)
            small = jnp.concatenate([gains_grad.reshape(-1), loss_part[None]])
            small = jnp.pad(small, (0, -small.size % (devices * 128))).reshape(devices, -1)
            sent = add_small(look_sent(0, grad_low), small)
        grad_x, grads, own_table, outer.moving, inner.moving, beside, sent = fence(
            grad_x, grads, own_table, outer.moving, inner.moving, beside, sent
        )
        table_got += beside
        pieces = [[]] * 4

        owned.append(outer)
        inner = Scatter(grads)
        owned.append(inner)
        outer.second()
        outer.sent, inner.moving, sent = fence(outer.sent, inner.moving, sent)

    outer.restart()
    got_rows = swap(sent)
    inner.first()
    inner.sent, outer.moving = fence(inner.sent, outer.moving)

    outer.third()
    inner.sent, outer.line = fence(inner.sent, outer.line)

    inner.start()
    outer.finish()
    squares, unpacked = unpack(owned[1], owned[0])
    inner.moving, got_rows, own_table, table_got, squares, unpacked = fence(
        inner.moving, got_rows, own_table, table_got, squares, unpacked
    )

    inner.second()
    inner.sent, got_rows, own_table, table_got = fence(
        inner.sent, got_rows, own_table, table_got
    )

    inner.restart()
    got_rows, small = take_small(got_rows)
    grad_table = own_table + jnp.concatenate(table_got).astype(f32)
    grad_table = grad_table + dot("kv,kd->vd", sent_rows(0), got_rows)
    inner.moving, grad_table, small = fence(inner.moving, grad_table, small)

    inner.third()
    inner.line, grad_table, small, outer.moving = fence(
        inner.line, grad_table, small, outer.moving
    )
    inner.finish(True)
    grad_table = more(lambda step: look_back(step, grad_low), grad_table)
    unpacked = [unpacked]
    for i in range(1, layers):
        more_squares, more_parts = unpack(owned[2 * i + 1], owned[2 * i])
        squares = squares + more_squares
        unpacked.append(more_parts)
    unpacked = unpacked[::-1]

    mask_count = jnp.sum(lens_all[1]).astype(f32)
    squares = squares + jnp.sum(grad_table * grad_table, 0)
    small = small[: -(-(gains_grad.size + 1) // (devices * 128)) * 128]
    shared = jnp.concatenate([small, squares])
    shared = swap(jnp.broadcast_to(shared[None], (devices, shared.size)))
    squares = jnp.sum(shared[:, small.size :])
    small = shared[:, : small.size].reshape(-1)
    gains_total = small[: gains_grad.size].reshape(gains_grad.shape)
    loss_sum = small[gains_grad.size]
    squares = squares + jnp.sum(gains_total * gains_total)
    grad_norm = jnp.sqrt(squares) / mask_count
    factor = jnp.minimum(1.0, threshold / grad_norm) / mask_count

    qkv_grad, up_grad, down_grad = (
        jnp.stack([part[i] for part in unpacked]) for i in (0, 2, 3)
    )
    out_grads = [part[1] for part in unpacked]
    results = [loss_sum, mask_count, grad_norm]
    results += update(embedding, embedding_mom, embedding_avg, grad_table * factor, rate_matrix)
    results += update(qkv_w, qkv_mom, qkv_avg, qkv_grad * factor, rate_matrix)
    results += update_turned(out_w, out_mom, out_avg, out_grads, factor)
    results += update(up_w, up_mom, up_avg, up_grad * factor, rate_matrix)
    results += update(down_w, down_mom, down_avg, down_grad * factor, rate_matrix)
    results += update(norm_gains, gains_mom, gains_avg, gains_total * factor, rate_gains)
    return tuple(results)


def solution(mesh):
    n_grp, n_dp, n_t = mesh.devices.shape
    split = Mesh(mesh.devices.reshape(n_grp, n_dp // 2, 2, n_t // 2, 2), ALL)
    dp = ("y", "core")
    owners = ("grp", "y", "core")
    rows = P(None, None, dp, None)
    table = P(ALL, None)
    wide = P(None, owners, None, TENSOR)
    tall = P(None, TENSOR, owners)
    flat = P(None, owners, TENSOR)
    return jax.shard_map(
        per_device,
        mesh=split,
        in_specs=(rows, rows, P(None, None, dp))
        + (table,) * 3 + (wide,) * 3 + (tall,) * 3 + (flat,) * 3 + (tall,) * 3 + (P(),) * 3,
        out_specs=(P(),) * 3
        + (table,) * 3 + (wide,) * 3 + (tall,) * 3 + (flat,) * 3 + (tall,) * 3 + (P(),) * 3,
        check_vma=False,
    )
```

```python
import functools

import jax
import jax.numpy as jnp
from jax import lax
from jax.experimental import pallas as pl
from jax.experimental.pallas import tpu as pltpu
from jax.sharding import Mesh
from jax.sharding import PartitionSpec as P

HEAD = 64
CAPACITY = 15

epsilon = 1e-05
threshold = 0.05
momentum = 0.9
average_decay = 0.75
rate_matrix = 2000.0
rate_gains = 5000.0
far_below = -1e30
bf16 = jnp.bfloat16
f32 = jnp.float32
TENSOR = ("th", "tl")
ALL = ("grp", "y", "core", "th", "tl")
OWNERS = ("th", "tl", "grp", "y", "core")
HEAD_GROUP = ("grp", "y", "core", "th")


def rope_tables(places):
    half_size = HEAD // 2
    lane = jnp.arange(TILE)
    frequency = 10000.0 ** (-(lane % half_size).astype(f32) / half_size)
    sign = jnp.where(lane % HEAD < half_size, -1.0, 1.0)
    angles = places.reshape(-1).astype(f32)[:, None] * frequency[None, :]
    return jnp.cos(angles), jnp.sin(angles) * sign


def dot(form, left, right):
    return jnp.einsum(form, left, right, preferred_element_type=f32)


def flip(values, axis):
    return lax.ppermute(values, axis, [(0, 1), (1, 0)])


def square_plane():
    return lax.axis_size("grp") == 2 and lax.axis_size("y") == 2


def coordinates():
    return jnp.stack([lax.axis_index("grp"), lax.axis_index("y"), lax.axis_index("core")])


def fence(*groups):
    return lax.optimization_barrier(groups)


def gather_whole(shards):
    kinds, rows, width = shards.shape
    everything = lax.all_gather(shards, OWNERS, axis=0, tiled=False)
    count = lax.axis_size(TENSOR)
    everything = everything.reshape(count, -1, kinds, rows, width)
    if rows % 16 == 0:
        return everything
    return everything.transpose(0, 2, 1, 3, 4).reshape(count, 1, kinds, -1, width)


def weight_grad_kernel(inputs, extra, at, *refs):
    xs, ys = refs[:inputs], refs[inputs : 2 * inputs]
    keep_ref, send_ref, turned, tile = refs[2 * inputs :]
    blocks, rows, width = tile.shape

    @pl.when(pl.program_id(0) == 0)
    def begin():
        for i in range(inputs):
            turned[i] = xs[i][...].T

    for kind in range(inputs - extra):
        grad = nn(turned[kind], ys[kind][...])
        if extra:
            more = nn(turned[1], ys[1][0])
            split = width - more.shape[1]
            grad = jnp.concatenate([grad[:, :split], grad[:, split:] + more], 1)
        tile[...] = grad.astype(bf16).reshape(blocks, rows, width)
        for by_x in range(2):
            for by_y in range(2):
                for core, ref in enumerate((keep_ref, send_ref)):
                    block = ((at[0] ^ by_x) * 2 + (at[1] ^ by_y)) * 2 + (at[2] ^ core)
                    ref[0, kind, by_x, by_y] = tile[block]


def weight_grads(pairs, extra=None):
    kinds = len(pairs)
    slots, width = pairs[0][0].shape
    count = pairs[0][1].shape[1] // width
    rows = width // 8
    if not square_plane():
        whole = [dot("nd,ntf->tdf", x, y.reshape(slots, count, width)) for x, y in pairs]
        if extra:
            more = dot("nd,tnf->tdf", *extra)
            whole[0] += jnp.pad(more, ((0, 0), (0, 0), (width - more.shape[2], 0)))
        return jnp.stack([part.astype(bf16) for part in whole], 1)
    part = pl.BlockSpec((1, kinds, 2, 2, rows, width), lambda t, at: (t, 0, 0, 0, 0, 0))
    shape = jax.ShapeDtypeStruct((count, kinds, 2, 2, rows, width), bf16)
    x_spec = pl.BlockSpec((slots, width), lambda t, at: (0, 0))
    x_specs = [x_spec] * kinds
    y_specs = [pl.BlockSpec((slots, width), lambda t, at: (0, t))] * kinds
    xs = [x for x, unused in pairs]
    ys = [y for unused, y in pairs]
    if extra:
        xs.append(extra[0])
        ys.append(extra[1])
        x_specs.append(x_spec)
        y_specs.append(pl.BlockSpec((1,) + extra[1].shape[1:], lambda t, at: (t, 0, 0)))
    return pl.pallas_call(
        functools.partial(weight_grad_kernel, len(xs), bool(extra)),
        grid_spec=pltpu.PrefetchScalarGridSpec(
            num_scalar_prefetch=1,
            grid=(count,),
            in_specs=x_specs + y_specs,
            out_specs=[part, part],
            scratch_shapes=[
                pltpu.VMEM((len(xs), width, slots), bf16),
                pltpu.VMEM((8, rows, width), bf16),
            ],
        ),
        out_shape=[shape, shape],
        compiler_params=pltpu.CompilerParams(vmem_limit_bytes=60 * 2**20),
        cost_estimate=pl.CostEstimate(
            flops=2 * slots * width * width * count * kinds,
            bytes_accessed=2 * count * kinds * width * (slots + width),
            transcendentals=0,
        ),
        name="weight_grads",
    )(coordinates(), *xs, *ys)


def plus(left, right):
    return (left.astype(f32) + right.astype(f32)).astype(bf16)


def add_first_kernel(kinds, own_low, own_high, got_low, got_high, low_keep, high_keep, *sends):
    low_keep[0] = plus(own_low[0, :, 0], got_low[0, :, 0])
    high_keep[0] = plus(own_high[0, :, :, 0], got_high[0, :, :, 0])
    for kind in range(kinds):
        low_send, high_send = sends[2 * kind : 2 * kind + 2]
        low_send[0] = plus(own_low[0, kind, 1], got_low[0, kind, 1])
        high_send[0] = plus(own_high[0, kind, :, 1], got_high[0, kind, :, 1])


def add_first(own, got):
    count, kinds, unused, unused, rows, width = own.shape
    half = count // 2
    low = pl.BlockSpec((1, kinds, 2, 2, rows, width), lambda t: (t, 0, 0, 0, 0, 0))
    high = pl.BlockSpec((1, kinds, 2, 2, rows, width), lambda t: (t + half, 0, 0, 0, 0, 0))
    part = pl.BlockSpec((1, kinds, 2, rows, width), lambda t: (t, 0, 0, 0, 0))
    send = pl.BlockSpec((1, 2, rows, width), lambda t: (t, 0, 0, 0))
    low_keep, high_keep, *sends = pl.pallas_call(
        functools.partial(add_first_kernel, kinds),
        grid=(half,),
        in_specs=[low, high, low, high],
        out_specs=[part] * 2 + [send] * (2 * kinds),
        out_shape=[jax.ShapeDtypeStruct((half, kinds, 2, rows, width), bf16)] * 2
        + [jax.ShapeDtypeStruct((half, 2, rows, width), bf16)] * (2 * kinds),
        compiler_params=pltpu.CompilerParams(vmem_limit_bytes=60 * 2**20),
        cost_estimate=pl.CostEstimate(flops=own.size, bytes_accessed=6 * own.size, transcendentals=0),
        name="add_first",
    )(own, own, got, got)
    return (low_keep, high_keep), tuple(zip(sends[::2], sends[1::2]))


def add_second_kernel(kinds, low, high, *refs):
    gots, (low_keep, low_send, high_keep, high_send) = refs[: 2 * kinds], refs[2 * kinds :]
    for kind in range(kinds):
        low_got, high_got = gots[2 * kind : 2 * kind + 2]
        low_keep[0, kind] = plus(low[0, kind, 0], low_got[0, 0])
        low_send[0, kind] = plus(low[0, kind, 1], low_got[0, 1])
        high_keep[0, kind] = plus(high[0, kind, 0], high_got[0, 0])
        high_send[0, kind] = plus(high[0, kind, 1], high_got[0, 1])


def add_second(low, high, gots):
    half, kinds, unused, rows, width = low.shape
    part = pl.BlockSpec((1, kinds, 2, rows, width), lambda t: (t, 0, 0, 0, 0))
    got = pl.BlockSpec((1, 2, rows, width), lambda t: (t, 0, 0, 0))
    out = pl.BlockSpec((1, kinds, rows, width), lambda t: (t, 0, 0, 0))
    return pl.pallas_call(
        functools.partial(add_second_kernel, kinds),
        grid=(half,),
        in_specs=[part] * 2 + [got] * (2 * kinds),
        out_specs=[out] * 4,
        out_shape=[jax.ShapeDtypeStruct((half, kinds, rows, width), bf16)] * 4,
        compiler_params=pltpu.CompilerParams(vmem_limit_bytes=60 * 2**20),
        cost_estimate=pl.CostEstimate(flops=2 * low.size, bytes_accessed=12 * low.size, transcendentals=0),
        name="add_second",
    )(low, high, *[part for pair in gots for part in pair])


def add_third_kernel(low, low_got, high, high_got, out):
    out[0, 0] = plus(low[0], low_got[0])
    out[1, 0] = plus(high[0], high_got[0])


def add_third(low, low_got, high, high_got):
    half, kinds, rows, width = low.shape
    part = pl.BlockSpec((1, kinds, rows, width), lambda t: (t, 0, 0, 0))
    out = pl.pallas_call(
        add_third_kernel,
        grid=(half,),
        in_specs=[part] * 4,
        out_specs=pl.BlockSpec((2, 1, kinds, rows, width), lambda t: (0, t, 0, 0, 0)),
        out_shape=jax.ShapeDtypeStruct((2, half, kinds, rows, width), bf16),
        compiler_params=pltpu.CompilerParams(vmem_limit_bytes=60 * 2**20),
        cost_estimate=pl.CostEstimate(flops=2 * low.size, bytes_accessed=12 * low.size, transcendentals=0),
        name="add_third",
    )(low, low_got, high, high_got)
    return out.reshape(2 * half, kinds, rows, width)


class Scatter:
    def __init__(self, grads=None):
        self.plane = square_plane() and grads is not None
        self.keep = self.sent = self.line = ()
        self.moving = () if grads is None else grads
        if self.plane:
            self.keep, send = grads
            self.moving = flip(send, "core")

    def first(self):
        if self.plane:
            self.keep, self.sent = add_first(self.keep, self.moving)
            self.moving = ()

    def start(self):
        if self.plane:
            low, high = self.sent[0]
            self.sent = self.sent[1:]
            self.moving += ((flip(low, "grp"), flip(high, "y")),)

    def second(self):
        if self.plane:
            low, low_send, high, high_send = add_second(*self.keep, self.moving)
            self.keep, self.sent = (low, high), (low_send, high_send)

    def restart(self):
        if self.plane:
            self.moving = (flip(self.sent[0], "y"), flip(self.sent[1], "grp"))

    def third(self):
        if self.plane:
            (low, high), (low_got, high_got) = self.keep, self.moving
            self.line = add_third(low, low_got, high, high_got)

    def finish(self, swapped=False):
        if self.plane and swapped:
            parts = lax.all_to_all(self.line, TENSOR, 0, 0, tiled=True)
            self.moving = jnp.sum(parts.astype(f32), 0)
        elif self.plane:
            self.moving = lax.psum_scatter(self.line, TENSOR, scatter_dimension=0, tiled=False)
        elif not isinstance(self.moving, tuple):
            count, kinds, width, unused = self.moving.shape
            owners = lax.axis_size(("grp", "y", "core"))
            blocks = self.moving.reshape(count, kinds, owners, width // owners, width)
            blocks = blocks.transpose(0, 2, 1, 3, 4).reshape(count * owners, kinds, -1, width)
            self.moving = lax.psum_scatter(blocks, OWNERS, scatter_dimension=0, tiled=False)

    def sums(self):
        return self.moving.astype(f32)


def gather_keys(own):
    far = flip(own, "grp")
    near = flip(own, "core")
    return own, near, far, flip(far, "core")


def gather_head(own, first, second):
    if not square_plane():
        return lax.all_gather(own, HEAD_GROUP, axis=0, tiled=True), flip(first + second, "tl")
    half = own.shape[0] // 2
    got, first = fence(flip(own, "th"), flip(first, "tl"))
    line = jnp.stack([own, got])
    low, high = line[:, :half], line[:, half:]
    low_got, high_got = flip(low, "grp"), flip(high, "y")
    low, high = jnp.stack([low, low_got]), jnp.stack([high, high_got])
    low_got, high_got = flip(low, "y"), flip(high, "grp")
    low_got, high_got, second = fence(low_got, high_got, flip(second, "tl"))
    low, high = jnp.stack([low, low_got]), jnp.stack([high, high_got])
    plane = jnp.stack([low, high])
    whole = jnp.stack([plane, flip(plane, "core")]).reshape(-1, own.shape[1])
    return whole, first + second


def scatter_head(send, keep, work):
    if not square_plane():
        grad = jnp.concatenate([keep, send])
        total = lax.psum_scatter(grad, HEAD_GROUP, scatter_dimension=0, tiled=True)
        return (total, jnp.zeros_like(total)), work()
    width = keep.shape[1]
    got = flip(send, "core").reshape(2, 2, 2, 2, -1, width)
    blocks = keep.reshape(2, 2, 2, 2, -1, width)
    low_send, high_send = plus(blocks[0, 1], got[0, 1]), plus(blocks[1, 1], got[1, 1])
    low, high = plus(blocks[0, 0], got[0, 0]), plus(blocks[1, 0], got[1, 0])
    low, high, low_send, high_send = fence(low, high, low_send, high_send)
    low_got, high_got = flip(low_send, "y"), flip(high_send, "grp")
    low_got, high_got, low, high, done = fence(low_got, high_got, low, high, work())
    low_next = flip(plus(low[1], low_got[1]), "grp")
    high_next = flip(plus(high[1], high_got[1]), "y")
    low = plus(plus(low[0], low_got[0]), low_next)
    high = plus(plus(high[0], high_got[0]), high_next)
    line, done = fence(jnp.concatenate([low, high], 1), done)
    return (line[0], flip(line[1], "th")), done


def turned(table):
    for dim, axis in enumerate(HEAD_GROUP):
        table = jnp.where(lax.axis_index(axis) == 1, jnp.flip(table, dim), table)
    return table


def head_order(table):
    if not square_plane():
        return table.reshape(-1)
    table = turned(table)
    half = table.shape[-1] // 2
    low = table[..., :half].transpose(2, 1, 0, 3, 4)
    high = table[..., half:].transpose(2, 0, 1, 3, 4)
    return jnp.stack([low, high], 1).reshape(-1)


def head_table(flat, shape):
    if not square_plane():
        return flat.reshape(shape)
    halves = flat.reshape(2, 2, 2, 2, 2, -1)
    low = halves[:, 0].transpose(2, 1, 0, 3, 4)
    high = halves[:, 1].transpose(1, 2, 0, 3, 4)
    return turned(jnp.concatenate([low, high], -1))


def nn(left, right):
    return lax.dot_general(left, right, (((1,), (0,)), ((), ())), preferred_element_type=f32)


def nt(left, right):
    return lax.dot_general(left, right, (((1,), (1,)), ((), ())), preferred_element_type=f32)


def tn(left, right):
    return lax.dot_general(left, right, (((0,), (0,)), ((), ())), preferred_element_type=f32)


def norm_rows(values, gains):
    centre = values - jnp.mean(values, -1, keepdims=True)
    spread = jnp.mean(centre * centre, -1, keepdims=True)
    return centre * lax.rsqrt(spread + epsilon) * gains[0:1] + gains[1:2]


def norm_rows_back(values, gains, upstream):
    centre = values - jnp.mean(values, -1, keepdims=True)
    inverse = lax.rsqrt(jnp.mean(centre * centre, -1, keepdims=True) + epsilon)
    unit = centre * inverse
    inner = upstream * gains[0:1]
    back = inverse * (
        inner
        - jnp.mean(inner, -1, keepdims=True)
        - unit * jnp.mean(inner * unit, -1, keepdims=True)
    )
    gain = jnp.sum(upstream * unit, 0, keepdims=True)
    bias = jnp.sum(upstream, 0, keepdims=True)
    return back, jnp.concatenate([gain, bias], 0)


TILE = 128


def lanes(rows):
    return lax.broadcasted_iota(jnp.int32, (rows, TILE), 1)


def turn(values, cosine, sine, part):
    half = HEAD // 2
    where = lanes(values.shape[0])
    swapped = jnp.where(
        where % HEAD < half,
        pltpu.roll(values, TILE - half, 1),
        pltpu.roll(values, half, 1),
    )
    turned = values * cosine + swapped * sine
    return turned if part == TILE else jnp.where(where < part, turned, values)


def weight_spec(weight, index):
    array, kind = weight
    unused, blocks, unused, rows, width = array.shape
    return pl.BlockSpec((1, blocks, 1, rows, width), lambda s, *at: (index(s), 0, kind, 0, 0))


def matrix(ref):
    blocks, rows, width = ref.shape[1], ref.shape[3], ref.shape[4]
    return ref[0, :, 0].reshape(blocks * rows, width)


def whole_spec(array):
    zeros = (0,) * array.ndim
    return pl.BlockSpec(array.shape, lambda s: zeros)


def spec(shape, index):
    return pl.BlockSpec(shape, index)


def params(limit=60):
    return pltpu.CompilerParams(vmem_limit_bytes=limit * 2**20)


def cost(flops, moved):
    return pl.CostEstimate(flops=int(flops), bytes_accessed=int(moved), transcendentals=0)


def project_kernel(x, gains, cosine, sine, w, h, q, clean, masked, h_now):
    @pl.when(pl.program_id(0) == 0)
    def begin():
        h_now[...] = norm_rows(x[...], gains[...]).astype(bf16)
        h[...] = h_now[...]

    z = nn(h_now[...], matrix(w)[:, : 5 * TILE])
    cos, sin = cosine[...], sine[...]
    tiles = [z[:, TILE * i : TILE * (i + 1)] for i in range(5)]
    rows = z.shape[0]
    low = lanes(rows) < HEAD
    q[0, :, :TILE] = turn(tiles[0], cos, sin, TILE).astype(bf16)
    q[0, :, TILE:] = jnp.where(low, turn(tiles[4], cos, sin, TILE), 0.0).astype(bf16)
    triple = jnp.concatenate(
        [turn(tiles[1], cos, sin, TILE), tiles[2], turn(tiles[3], cos, sin, HEAD)], 1
    ).astype(bf16)
    span = rows // 2
    clean[...] = triple[:span]
    masked[...] = triple[span:]


def project(x, gains, tables, w):
    rows, width = x.shape
    count = w[0].shape[0]
    span = rows // 2
    triple = spec((span, 3 * TILE), lambda t: (0, t))
    return pl.pallas_call(
        project_kernel,
        grid=(count,),
        in_specs=[whole_spec(x), whole_spec(gains)]
        + [whole_spec(table) for table in tables]
        + [weight_spec(w, lambda t: t)],
        out_specs=[
            spec((rows, width), lambda t: (0, 0)),
            spec((1, rows, 2 * TILE), lambda t: (t, 0, 0)),
            triple,
            triple,
        ],
        out_shape=[
            jax.ShapeDtypeStruct((rows, width), bf16),
            jax.ShapeDtypeStruct((count, rows, 2 * TILE), bf16),
            jax.ShapeDtypeStruct((span, count * 3 * TILE), bf16),
            jax.ShapeDtypeStruct((span, count * 3 * TILE), bf16),
        ],
        scratch_shapes=[pltpu.VMEM((rows, width), bf16)],
        compiler_params=params(),
        cost_estimate=cost(2 * rows * width * width * count, 2 * count * width * width),
        name="project",
    )(x, gains, *tables, w[0])


def head_operands(pair, triple, own, j):
    low = lanes(pair.shape[0]) < HEAD
    if j == 2:
        return pair[:, TILE:], triple[:, 2 * TILE :], 2 * TILE, own[:, 2 * TILE :]
    keep = low if j == 0 else jnp.logical_not(low)
    query = jnp.where(keep, pair[:, :TILE], jnp.zeros((), pair.dtype))
    return query, triple[:, :TILE], TILE, own[:, :TILE]


def head_scores(query, key, own_key, seen):
    span = own_key.shape[0]
    query = query * jnp.asarray(HEAD ** (-0.5), query.dtype)
    score = nt(key, query) + seen
    alone = row_sums(query[span:].astype(f32) * own_key.astype(f32))
    return score, jnp.concatenate([jnp.full((1, query.shape[0] - span), far_below, f32), alone], 1)


def row_sums(values):
    return jnp.sum(values.T, 0, keepdims=True)


def attend_kernel(x, q, k0, k1, k2, k3, own, seen, w, mid, o, log_total):
    rows = x.shape[0]
    span = own.shape[0]

    @pl.when(pl.program_id(0) == 0)
    def begin():
        mid[...] = x[...]

    pair = q[0]
    triple = jnp.concatenate([k0[...], k1[...], k2[...], k3[...]], 0)
    low = lax.broadcasted_iota(jnp.int32, (TILE, rows), 0) < HEAD
    turned = {TILE: triple[:, TILE : 2 * TILE].T, 2 * TILE: triple[:, 2 * TILE :].T}
    own_turned = {start: own[:, start : start + TILE].astype(f32).T for start in turned}
    outs = []
    for j in range(3):
        query, key, value_start, own_key = head_operands(pair, triple, own[...], j)
        score, alone = head_scores(query, key, own_key, seen[...])
        top = jnp.maximum(jnp.max(score, 0, keepdims=True), alone)
        part = jnp.exp(score - top)
        part_alone = jnp.exp(alone - top)
        total = jnp.sum(part, 0, keepdims=True) + part_alone
        inverse = 1.0 / total
        log_total[0, j : j + 1, :] = top + jnp.log(total)
        out = nn(turned[value_start], part.astype(bf16)) * inverse
        weight = (part_alone * inverse).astype(bf16).astype(f32)[:, span:]
        out = jnp.concatenate([out[:, :span], out[:, span:] + weight * own_turned[value_start]], 1)
        outs.append(out)
    both = jnp.concatenate(
        [jnp.where(low, 0.0, outs[2]), jnp.where(low, outs[0], outs[1])], 0
    ).T.astype(bf16)
    o[0] = both
    mid[...] += nt(both, matrix(w)[:, 4 * TILE :])


def attend(x, q, keys, own, seen, w):
    rows, width = x.shape
    count = w[0].shape[0]
    span = own.shape[0]
    triple = spec((span, 3 * TILE), lambda t: (0, t))
    return pl.pallas_call(
        attend_kernel,
        grid=(count,),
        in_specs=[
            whole_spec(x),
            spec((1, rows, 2 * TILE), lambda t: (t, 0, 0)),
            triple, triple, triple, triple, triple,
            whole_spec(seen),
            weight_spec(w, lambda t: t),
        ],
        out_specs=[
            spec((rows, width), lambda t: (0, 0)),
            spec((1, rows, 2 * TILE), lambda t: (t, 0, 0)),
            spec((1, 8, rows), lambda t: (t, 0, 0)),
        ],
        out_shape=[
            jax.ShapeDtypeStruct((rows, width), f32),
            jax.ShapeDtypeStruct((count, rows, 2 * TILE), bf16),
            jax.ShapeDtypeStruct((count, 8, rows), f32),
        ],
        compiler_params=params(),
        cost_estimate=cost(16 * rows * 4 * span * HEAD * count, 2 * count * width * width),
        name="attend",
    )(x, q, *keys, own, seen, w[0])


def gelu_parts(u):
    root = 0.7978845608028654
    square = u * u
    th = jnp.tanh(root * (u + 0.044715 * square * u))
    value = 0.5 * u * (1.0 + th)
    slope = 0.5 * (1.0 + th) + 0.5 * u * (1.0 - th * th) * (root * (1.0 + 3 * 0.044715 * square))
    return value, slope


def feed_kernel(mid, gains, up, down, *refs):
    *last, h2, out = refs

    @pl.when(pl.program_id(0) == 0)
    def begin():
        h2[...] = norm_rows(mid[...], gains[...]).astype(bf16)
        out[...] = mid[...]

    u = nn(h2[...], matrix(up))
    out[...] += nt(gelu_parts(u)[0].astype(bf16), matrix(down))
    if last:
        last_gains, final = last

        @pl.when(pl.program_id(0) == pl.num_programs(0) - 1)
        def end():
            final[...] = norm_rows(out[final.shape[0] :], last_gains[...]).astype(bf16)


def feed(mid, gains, up, down, last_gains=None):
    rows, width = mid.shape
    count = up[0].shape[0]
    plain = spec((rows, width), lambda t: (0, 0))
    last = last_gains is not None

    def call(*operands):
        specs = [whole_spec(mid), whole_spec(gains)]
        specs += [weight_spec(up, lambda t: t), weight_spec(down, lambda t: t)]
        shapes = [
            jax.ShapeDtypeStruct((rows, width), bf16),
            jax.ShapeDtypeStruct((rows, width), f32),
        ]
        outs = [plain, plain]
        if last:
            specs.append(whole_spec(last_gains))
            shapes.insert(0, jax.ShapeDtypeStruct((rows // 2, width), bf16))
            outs.insert(0, spec((rows // 2, width), lambda t: (0, 0)))
        return pl.pallas_call(
            feed_kernel,
            grid=(count,),
            in_specs=specs,
            out_specs=outs,
            out_shape=shapes,
            compiler_params=params(),
            cost_estimate=cost(4 * rows * width * width * count, 4 * count * width * width),
            name="feed",
        )(*operands)

    return call(mid, gains, up[0], down[0], *([last_gains] if last else []))


def feed_back_kernel(
    grad, mid, h2, gains, up, down, grad_low, a, grad_u, grad_mid, mid_low, gain_grad, total
):
    step = pl.program_id(0)

    @pl.when(step == 0)
    def begin():
        grad_low[...] = grad[...].astype(bf16)
        total[...] = jnp.zeros_like(total)

    value, slope = gelu_parts(nn(h2[...], matrix(up)))
    a[...] = value.astype(bf16)
    grad_hidden = (nn(grad_low[...], matrix(down)) * slope).astype(bf16)
    grad_u[...] = grad_hidden
    total[...] += nt(grad_hidden, matrix(up))

    @pl.when(step == pl.num_programs(0) - 1)
    def norm():
        back, gain_grad[...] = norm_rows_back(mid[...], gains[...], total[...])
        back = back + grad[...]
        grad_mid[...] = back
        mid_low[...] = back.astype(bf16)


def feed_back(grad, mid, h2, gains, up, down):
    rows, width = grad.shape
    count = up[0].shape[0]
    hidden = spec((rows, width), lambda t: (0, t))
    plain = spec((rows, width), lambda t: (0, 0))

    def rows_of(kind, columns=width):
        return jax.ShapeDtypeStruct((rows, columns), kind)

    return pl.pallas_call(
        feed_back_kernel,
        grid=(count,),
        in_specs=[plain, plain, plain, whole_spec(gains)]
        + [weight_spec(up, lambda t: t), weight_spec(down, lambda t: t)],
        out_specs=[plain, hidden, hidden, plain, plain, whole_spec(gains)],
        out_shape=[
            rows_of(bf16), rows_of(bf16, count * width), rows_of(bf16, count * width),
            rows_of(f32), rows_of(bf16), jax.ShapeDtypeStruct(gains.shape, f32),
        ],
        scratch_shapes=[pltpu.VMEM((rows, width), f32)],
        compiler_params=params(),
        cost_estimate=cost(6 * rows * width * width * count, 4 * count * width * width),
        name="feed_back",
    )(grad, mid, h2, gains, up[0], down[0])


def attend_back_kernel(
    mid_low, q, k0, k1, k2, k3, own, seen, log_total, cosine, sine, w, grad_q, keep, send, grad_own
):
    rows = mid_low.shape[0]
    span = own.shape[0]
    scale = HEAD ** (-0.5)
    grad_o = nn(mid_low[...], matrix(w)[:, 4 * TILE :]).astype(bf16)
    pair = q[0]
    triple = jnp.concatenate([k0[...], k1[...], k2[...], k3[...]], 0)
    low = lanes(rows) < HEAD
    low_rows = lax.broadcasted_iota(jnp.int32, (TILE, rows), 0) < HEAD
    zero = jnp.zeros((), bf16)
    turned = {0: triple[:, :TILE].T, 2 * TILE: triple[:, 2 * TILE :].T}
    own_turned = {start: own[:, start : start + TILE].astype(f32).T for start in turned}
    query_grads, key_grads, value_grads, own_keys, own_values = [], [], [], [], []
    for j in range(3):
        query, key, value_start, own_key = head_operands(pair, triple, own[...], j)
        key_start = 2 * TILE if j == 2 else 0
        value = triple[:, value_start : value_start + TILE]
        own_value = own[:, value_start : value_start + TILE]
        if j == 2:
            upstream = jnp.where(low, zero, grad_o[:, :TILE])
        else:
            keep_lane = low if j == 0 else jnp.logical_not(low)
            upstream = jnp.where(keep_lane, grad_o[:, TILE:], zero)
        score, alone = head_scores(query, key, own_key, seen[...])
        logs = log_total[0, j : j + 1, :]
        prob = jnp.exp(score - logs)
        prob_alone = jnp.exp(alone - logs)
        dprob = nt(value, upstream)
        lone = upstream[span:].astype(f32)
        dalone = row_sums(lone * own_value.astype(f32))
        dalone = jnp.concatenate([jnp.zeros((1, rows - span), f32), dalone], 1)
        delta = jnp.sum(dprob * prob, 0, keepdims=True) + dalone * prob_alone
        dscore = (prob * (dprob - delta)).astype(bf16)
        dself = (prob_alone * (dalone - delta)).astype(bf16).astype(f32)[:, span:]
        lone_weight = prob_alone.astype(bf16).astype(f32)[:, span:]
        query_grad = nn(turned[key_start], dscore)
        query_grads.append(
            jnp.concatenate(
                [
                    query_grad[:, :span],
                    query_grad[:, span:] + dself * own_turned[key_start],
                ],
                1,
            )
        )
        key_grads.append(nn(dscore, query))
        value_grads.append(nn(prob.astype(bf16), upstream))
        own_keys.append(dself * query[span:].astype(f32).T)
        own_values.append(lone_weight * lone.T)
    cos, sin = cosine[...], -sine[...]
    first = (jnp.where(low_rows, query_grads[0], query_grads[1]) * scale).T
    second = (jnp.where(low_rows, query_grads[2], 0.0) * scale).T
    grad_q[0, :, :TILE] = turn(first, cos, sin, TILE).astype(bf16)
    grad_q[0, :, TILE:] = turn(second, cos, sin, TILE).astype(bf16)
    grads = jnp.concatenate(
        [
            (key_grads[0] + key_grads[1]) * scale,
            value_grads[0] + value_grads[1],
            key_grads[2] * scale + value_grads[2],
        ],
        1,
    ).astype(bf16)
    keep[0] = grads[:span]
    send[0] = grads[span : 2 * span]
    keep[1] = grads[2 * span : 3 * span]
    send[1] = grads[3 * span :]
    grad_own[...] = jnp.concatenate(
        [
            (own_keys[0] + own_keys[1]) * scale,
            own_values[0] + own_values[1],
            own_keys[2] * scale + own_values[2],
        ],
        0,
    ).T


def attend_back(mid_low, q, keys, own, seen, log_total, tables, w):
    rows, width = mid_low.shape
    count = w[0].shape[0]
    span = own.shape[0]
    triple = spec((span, 3 * TILE), lambda t: (0, t))
    pair = spec((1, rows, 2 * TILE), lambda t: (t, 0, 0))
    couple = spec((2, span, 3 * TILE), lambda t: (0, 0, t))
    couple_shape = jax.ShapeDtypeStruct((2, span, count * 3 * TILE), bf16)
    return pl.pallas_call(
        attend_back_kernel,
        grid=(count,),
        in_specs=[spec((rows, width), lambda t: (0, 0)), pair]
        + [triple] * 5
        + [whole_spec(seen), spec((1, 8, rows), lambda t: (t, 0, 0))]
        + [whole_spec(table) for table in tables]
        + [weight_spec(w, lambda t: t)],
        out_specs=[pair, couple, couple, triple],
        out_shape=[
            jax.ShapeDtypeStruct((count, rows, 2 * TILE), bf16),
            couple_shape, couple_shape,
            jax.ShapeDtypeStruct((span, count * 3 * TILE), f32),
        ],
        compiler_params=params(),
        cost_estimate=cost(32 * rows * 4 * span * HEAD * count, 2 * count * width * width),
        name="attend_back",
    )(mid_low, q, *keys, own, seen, log_total, *tables, w[0])


def back_second_kernel(
    keep, got, far, grad_own, grad_q, cosine, sine, x, grad_mid, gains, w, dz, out, gain_grad, total
):
    step = pl.program_id(0)

    @pl.when(step == 0)
    def begin():
        total[...] = jnp.zeros_like(total)

    clean = keep[0].astype(f32) + got[0].astype(f32) + far[...].astype(f32)
    triple = jnp.concatenate([clean, grad_own[...]], 0)
    cos, sin = cosine[...], -sine[...]
    pair = grad_q[0]
    grads = jnp.concatenate(
        [
            pair[:, :TILE],
            turn(triple[:, :TILE], cos, sin, TILE).astype(bf16),
            triple[:, TILE : 2 * TILE].astype(bf16),
            turn(triple[:, 2 * TILE :], cos, sin, HEAD).astype(bf16),
            pair[:, TILE:],
        ],
        1,
    )
    dz[:, : 5 * TILE] = grads
    dz[:, 5 * TILE :] = jnp.zeros_like(pair[:, TILE:])
    total[...] += nt(grads, matrix(w)[:, : 5 * TILE])

    @pl.when(step == pl.num_programs(0) - 1)
    def norm():
        back, gain_grad[...] = norm_rows_back(x[...], gains[...], total[...])
        out[...] = grad_mid[...] + back


def back_second(keep, got, far, grad_own, grad_q, tables, x, grad_mid, gains, w):
    rows, width = x.shape
    count = w[0].shape[0]
    span = rows // 2
    triple = spec((span, 3 * TILE), lambda t: (0, t))
    couple = spec((1, span, 3 * TILE), lambda t: (0, 0, t))
    plain = spec((rows, width), lambda t: (0, 0))
    return pl.pallas_call(
        back_second_kernel,
        grid=(count,),
        in_specs=[couple, couple, triple, triple, spec((1, rows, 2 * TILE), lambda t: (t, 0, 0))]
        + [whole_spec(table) for table in tables]
        + [plain, plain, whole_spec(gains), weight_spec(w, lambda t: t)],
        out_specs=[spec((rows, width), lambda t: (0, t)), plain, whole_spec(gains)],
        out_shape=[
            jax.ShapeDtypeStruct((rows, count * width), bf16),
            jax.ShapeDtypeStruct((rows, width), f32),
            jax.ShapeDtypeStruct(gains.shape, f32),
        ],
        scratch_shapes=[pltpu.VMEM((rows, width), f32)],
        compiler_params=params(),
        cost_estimate=cost(2 * rows * width * width * count, 2 * count * width * width),
        name="back_second",
    )(keep, got, far, grad_own, grad_q, *tables, x, grad_mid, gains, w[0])


def logits_kernel(f, table, *refs):
    target, *parts, stats, other = refs[-5:]
    whole_table(refs[:-5], other)
    block = table.shape[0]
    column = lax.broadcasted_iota(jnp.int32, (f.shape[0], block), 1)
    tops, totals, picked = [], [], 0.0
    for i, half in enumerate((table, other)):
        logits = nt(f[...], half[...])
        top = jnp.max(logits, -1, keepdims=True)
        part = jnp.exp(logits - top)
        parts[i][...] = part.astype(bf16)
        tops.append(top)
        totals.append(jnp.sum(part, -1, keepdims=True))
        chosen = jnp.where(column == target[:, :1] - i * block, logits, 0.0)
        picked = picked + jnp.sum(chosen, -1, keepdims=True)
    top = jnp.maximum(*tops)
    total = sum(totals[i] * jnp.exp(tops[i] - top) for i in range(2))
    lane = lanes(f.shape[0])
    columns = jnp.where(lane == 0, tops[0], jnp.where(lane == 3, tops[1], picked))
    columns = jnp.where(lane == 1, top + jnp.log(total), columns)
    stats[0] = columns.T[: stats.shape[1]]


def whole_table(pieces, other):
    @pl.when(pl.program_id(0) == 0)
    def lay():
        start = 0
        for piece in pieces:
            other[start : start + piece.shape[0]] = piece[...]
            start += piece.shape[0]


def head_logits(f, table, pieces, target):
    rows, width = f.shape
    columns = table.shape[0]
    block = 512
    wide = spec((block, columns), lambda i: (i, 0))
    narrow = spec((block, TILE), lambda i: (i, 0))
    *parts, stats = pl.pallas_call(
        logits_kernel,
        grid=(rows // block,),
        in_specs=[spec((block, width), lambda i: (i, 0)), whole_spec(table)]
        + [whole_spec(piece) for piece in pieces]
        + [narrow],
        out_specs=[wide, wide, spec((1, 8, block), lambda i: (i, 0, 0))],
        out_shape=[jax.ShapeDtypeStruct((rows, columns), bf16)] * 2
        + [jax.ShapeDtypeStruct((rows // block, 8, block), f32)],
        scratch_shapes=[pltpu.VMEM(table.shape, bf16)],
        compiler_params=params(60),
        cost_estimate=cost(4 * rows * width * columns, 4 * rows * columns),
        name="head_logits",
    )(f, table, *pieces, target)
    return parts, stats


def logits_back_kernel(first, second, table, *refs):
    target, top, log_total, *grads, send, keep, other = refs[-8:]
    whole_table(refs[:-8], other)
    block = table.shape[0]
    scales = jnp.exp(top[0] - log_total[0])
    scales = jnp.concatenate([scales] * (TILE // scales.shape[0]), 0).T
    column = lax.broadcasted_iota(jnp.int32, first.shape, 1)
    total = 0.0
    for i, (part, half) in enumerate(((first, table), (second, other))):
        prob = part[...].astype(f32) * scales[:, 3 * i : 3 * i + 1]
        hit = column == target[:, :1] - i * block
        grads[i][...] = jnp.where(hit, prob - 1.0, prob).astype(bf16)
        total = total + nn(grads[i][...], half[...])
    total = total.astype(bf16)
    early = pl.program_id(0) < pl.num_programs(0) // 2

    @pl.when(early)
    def to_keep():
        keep[...] = total

    @pl.when(jnp.logical_not(early))
    def to_send():
        send[...] = total


def head_back(parts, table, pieces, target, stats, log_total):
    rows, columns = parts[0].shape
    width = table.shape[1]
    block = stats.shape[2]
    half = rows // block // 2
    wide = spec((block, columns), lambda i: (i, 0))
    *grads, send, keep = pl.pallas_call(
        logits_back_kernel,
        grid=(rows // block,),
        in_specs=[wide, wide, whole_spec(table)]
        + [whole_spec(piece) for piece in pieces]
        + [
            spec((block, TILE), lambda i: (i, 0)),
            spec((1, 8, block), lambda i: (i, 0, 0)),
            spec((1, 1, block), lambda i: (i, 0, 0)),
        ],
        out_specs=[
            wide, wide,
            spec((block, width), lambda i: (jnp.maximum(i - half, 0), 0)),
            spec((block, width), lambda i: (jnp.minimum(i, half - 1), 0)),
        ],
        out_shape=[jax.ShapeDtypeStruct((rows, columns), bf16)] * 2
        + [jax.ShapeDtypeStruct((rows // 2, width), bf16)] * 2,
        scratch_shapes=[pltpu.VMEM(table.shape, bf16)],
        compiler_params=params(60),
        cost_estimate=cost(4 * rows * width * columns, 8 * rows * columns),
        name="head_back",
    )(*parts, table, *pieces, target, stats, log_total)
    return grads, send, keep


def final_back_kernel(x, gains, first, second, grad, gain_grad):
    span = first.shape[0]
    upstream = first[...].astype(f32) + second[...].astype(f32)
    grad[:span] = jnp.zeros_like(upstream)
    grad[span:], gain_grad[...] = norm_rows_back(x[span:], gains[...], upstream)


def final_back(x, gains, parts):
    return pl.pallas_call(
        final_back_kernel,
        out_shape=[
            jax.ShapeDtypeStruct(x.shape, f32),
            jax.ShapeDtypeStruct(gains.shape, f32),
        ],
        compiler_params=params(),
        name="final_back",
    )(x, gains, *parts)


def update(weight, moment, average, grad, rate):
    fresh_mom = momentum * moment + grad
    fresh_w = weight - rate * (grad + momentum * fresh_mom)
    fresh_avg = average_decay * average + (1.0 - average_decay) * fresh_w
    return (fresh_mom, fresh_w, fresh_avg)


def update_turned_kernel(factor, weight, moment, average, *refs):
    *grads, new_moment, new_weight, new_average = refs
    for layer, grad in enumerate(grads):
        turned = grad[...].T * factor[0, 0]
        new_moment[layer], new_weight[layer], new_average[layer] = update(
            weight[layer], moment[layer], average[layer], turned, rate_matrix
        )


def update_turned(weight, moment, average, grads, factor):
    if not square_plane():
        turned = jnp.stack([grad.T for grad in grads])
        return update(weight, moment, average, turned * factor, rate_matrix)
    return pl.pallas_call(
        update_turned_kernel,
        in_specs=[pl.BlockSpec(memory_space=pltpu.SMEM)]
        + [pl.BlockSpec(memory_space=pltpu.VMEM)] * (3 + len(grads)),
        out_specs=[pl.BlockSpec(memory_space=pltpu.VMEM)] * 3,
        out_shape=[jax.ShapeDtypeStruct(weight.shape, f32)] * 3,
        compiler_params=params(),
        name="update_turned",
    )(factor.reshape(1, 1), weight, moment, average, *grads)


def lookup_plan(ids, block_rows):
    slots = ids.shape[1]
    owner = ids // block_rows
    order = jnp.arange(slots)
    same = ids[:, :, None] == ids[:, None, :]
    lead = jnp.min(jnp.where(same, order[None, None, :], slots), -1)
    first = lead == order
    ahead = jnp.logical_and(
        jnp.logical_and(first[:, None, :], owner[:, :, None] == owner[:, None, :]),
        order[None, None, :] < lead[:, :, None],
    )
    place = jnp.sum(ahead.astype(jnp.int32), -1)
    return owner, place, first


def per_device(
    tokens, positions, lengths,
    embedding, embedding_mom, embedding_avg,
    qkv_w, qkv_mom, qkv_avg,
    out_w, out_mom, out_avg,
    up_w, up_mom, up_avg,
    down_w, down_mom, down_avg,
    norm_gains, gains_mom, gains_avg,
):
    n_grp, n_y, n_t = lax.axis_size("grp"), lax.axis_size("y"), lax.axis_size(TENSOR)
    devices = 2 * n_grp * n_y * n_t
    at_grp, at_y, at_core = (lax.axis_index(name) for name in ALL[:3])
    at_t = lax.axis_index(TENSOR)
    me = lax.axis_index(ALL)
    block_rows, width = embedding.shape
    layers = qkv_w.shape[0]
    micros, unused, rows_here, seq = tokens.shape
    rows = rows_here * 2 * n_y
    span = seq // (2 * n_grp)
    my_row = at_y * n_t + at_t
    my_part = at_grp * 2 + at_core

    packed = jnp.concatenate(
        [tokens, positions, jnp.broadcast_to(lengths[..., None], lengths.shape + (128,))], -1
    )
    packed = lax.all_gather(packed, ("y", "core"), axis=2, tiled=True)
    packed = packed.transpose(1, 0, 2, 3).reshape(2, micros * rows, -1)
    ids_all, places_all, lens_all = packed[..., :seq], packed[..., seq : 2 * seq], packed[..., -1]

    def by_device(table):
        split = table.reshape(n_y, n_t, n_grp, 2, span)
        return split.transpose(2, 0, 3, 1, 4).reshape(devices, span)

    shards = []
    for layer in range(layers):
        turned_out = out_w[layer].T
        q_part, k_part, v_part = (qkv_w[layer][:, i] for i in range(3))
        attn = [
            q_part[:, :TILE], k_part[:, :TILE], v_part[:, :TILE],
            k_part[:, TILE:], v_part[:, TILE:], q_part[:, TILE:], turned_out[:, TILE:],
            turned_out[:, :TILE],
        ]
        shards.append(
            jnp.stack([jnp.concatenate(attn, 1), up_w[layer], down_w[layer].T]).astype(bf16)
        )
    front = gather_whole(jnp.concatenate([shards[0], shards[1][:2]]))
    rest = gather_whole(shards[1][2:])
    weights = [
        ((front, 0), (front, 1), (front, 2)),
        ((front, 3), (front, 4), (rest, 0)),
    ]
    table = embedding.astype(bf16)

    def my_group(by_dev):
        split = by_dev.reshape(n_grp, n_y, 2, n_t // 2, 2, span)
        return lax.dynamic_index_in_dim(split, at_t % 2, 4, keepdims=False)

    mask_id = block_rows * devices - 1
    wanted = jnp.concatenate(
        [by_device(ids_all[0]), jnp.full((devices, 1), mask_id, jnp.int32)], 1
    )
    owner, place, first = lookup_plan(wanted, block_rows)
    rounds = jnp.max(place) // CAPACITY + 1
    mine = jnp.logical_and(first, owner == me)
    local = wanted - me * block_rows
    my_owner = lax.dynamic_index_in_dim(owner, me, 0, keepdims=False)
    my_place = lax.dynamic_index_in_dim(place, me, 0, keepdims=False)
    my_slot = my_owner * CAPACITY + my_place
    my_slot = jnp.concatenate([my_slot[:span], jnp.broadcast_to(my_slot[span:], (span,))])
    my_place = jnp.concatenate([my_place[:span], jnp.broadcast_to(my_place[span:], (span,))])

    def sent_rows(step):
        at = place - step * CAPACITY
        hit = jnp.logical_and(mine[:, None, :], at[:, None, :] == jnp.arange(CAPACITY)[None, :, None])
        row = jnp.sum(jnp.where(hit, local[:, None, :] + 1, 0), -1).reshape(-1) - 1
        return (row[:, None] == jnp.arange(block_rows)[None, :]).astype(bf16)

    def used_rows(step):
        slot = my_slot - step * CAPACITY
        inside = jnp.logical_and(my_place >= step * CAPACITY, my_place < (step + 1) * CAPACITY)
        slot = jnp.where(inside, slot, -1)
        return (slot[:, None] == jnp.arange(devices * CAPACITY)[None, :]).astype(bf16)

    def swap(values):
        return lax.all_to_all(values, ALL, 0, 0, tiled=True)

    def look(step):
        sent = dot("kv,vd->kd", sent_rows(step), table).astype(bf16)
        return dot("nk,kd->nd", used_rows(step), exchange(sent))

    def exchange(values):
        return take_small(swap(add_small(values, jnp.zeros((devices, width // 2), f32))))[0]

    def add_small(values, small):
        high = small.astype(bf16)
        pair = [high, (small - high.astype(f32)).astype(bf16)]
        pair = [jnp.pad(part, ((0, 0), (0, width // 2 - part.shape[1]))) for part in pair]
        row = jnp.concatenate(pair, 1)[:, None]
        return jnp.concatenate([values.reshape(devices, CAPACITY, width), row], 1)

    def take_small(both):
        row = both[:, CAPACITY].astype(f32)
        return (
            both[:, :CAPACITY].reshape(devices * CAPACITY, width),
            jnp.sum(row[:, : width // 2] + row[:, width // 2 :], 0),
        )

    def look_sent(step, grad):
        return dot("nk,nd->kd", used_rows(step), grad).astype(bf16)

    def look_back(step, grad):
        return dot("kv,kd->vd", sent_rows(step), exchange(look_sent(step, grad)))

    def more(step_fn, begin):
        return lax.while_loop(
            lambda carry: carry[0] < rounds,
            lambda carry: (carry[0] + 1, carry[1] + step_fn(carry[0])),
            (jnp.int32(1), begin),
        )[1]

    cuts = [int(block_rows * part) // 16 * 16 for part in (0.26, 0.43, 0.63)]
    x, parted, ids_all, places_all, lens_all = fence(
        more(look, look(0)), table, ids_all, places_all, lens_all
    )

    lens = lax.dynamic_index_in_dim(lens_all, my_row, 1, keepdims=False)
    clean_len, masked_len = lens[0], lens[1]
    places = lax.dynamic_slice(places_all, (0, my_row, my_part * span), (2, 1, span))
    tables = rope_tables(places)
    near = jnp.array([0, 1, 0, 1]) ^ at_core
    far = jnp.array([0, 0, 1, 1]) ^ at_grp
    slots = (far * 2 + near)[:, None] * span + jnp.arange(span)[None, :]
    seen = jnp.where(slots.reshape(-1, 1) < clean_len, 0.0, far_below)
    seen = jnp.broadcast_to(seen, (seen.shape[0], 2 * span))

    targets = head_order(my_group(by_device(ids_all[1])))
    target_block = targets // block_rows
    targets = targets % block_rows + jnp.where(target_block == me ^ 1, block_rows, 0)
    valid_all = head_order(
        my_group(by_device((jnp.arange(seq)[None, :] < lens_all[1][:, None]).astype(jnp.int32)))
    ) > 0
    targets = jnp.where(jnp.logical_and(target_block | 1 == me | 1, valid_all), targets, -1)
    targets = jnp.broadcast_to(targets[:, None], targets.shape + (TILE,))
    valid_all = valid_all.astype(f32)

    table_parts = [[part] for part in jnp.split(parted, cuts)]
    x, targets, valid_all, seen, tables, table_parts = fence(
        x, targets, valid_all, seen, tables, table_parts
    )

    kept = []
    for layer in range(layers):
        attn, upper, lower = weights[layer]
        h, q, clean, own = project(x, norm_gains[2 * layer], tables, attn)
        keys = gather_keys(clean)
        if layer == layers - 1:
            q, table_parts = fence(q, table_parts)
        arriving = table_parts if layer == layers - 1 else [(), (), (), ()]
        got = flip(arriving[0], "tl")
        mid, o, log_total = attend(x, q, keys, own, seen, attn)
        mid, got = fence(mid, got)
        other_table = got
        got = flip(arriving[1], "tl")
        final_gains = norm_gains[2 * layers] if layer == layers - 1 else None
        *f_mine, h2, after = feed(mid, norm_gains[2 * layer + 1], upper, lower, final_gains)
        f_mine, after, got = fence(f_mine, after, got)
        other_table += got
        kept.append((x, h, q, keys, own, o, log_total, mid, h2))
        x = after

    f_all, got = gather_head(f_mine[0], *table_parts[2:])
    other_table += got

    parts_low, stats = head_logits(f_all, table, other_table, targets)
    part_total = head_table(stats[:, 1].reshape(-1), (n_grp, n_y, 2, n_t // 2, span))
    group = lax.axis_size(HEAD_GROUP)
    parts = lax.all_to_all(
        jnp.broadcast_to(part_total.reshape(1, -1), (group, group * span)),
        HEAD_GROUP, 0, 0, tiled=True,
    )
    top = jnp.max(parts, 0)
    log_total = top + jnp.log(jnp.sum(jnp.exp(parts - top), 0))
    own_total = lax.dynamic_slice(log_total, (lax.axis_index(HEAD_GROUP) * span,), (span,))
    log_total = head_order(log_total.reshape(part_total.shape))
    target_part = jnp.sum(jnp.where(valid_all > 0.0, stats[:, 2].reshape(-1), 0.0))
    own_valid = my_part * span + jnp.arange(span) < masked_len
    loss_part = jnp.sum(jnp.where(own_valid, own_total, 0.0)) - target_part
    log_total = jnp.where(valid_all > 0.0, log_total, -far_below)
    grad_logits, *grad_f = head_back(
        parts_low, table, other_table, targets, stats, log_total.reshape(stats.shape[0], 1, -1)
    )

    def beside_table():
        return dot("nv,nd->vd", grad_logits[1], f_all).astype(bf16)

    grad_f, pieces = scatter_head(*grad_f, beside_table)
    back_cuts = [int(block_rows * part) // 16 * 16 for part in (0.19, 0.37, 0.65)]
    grad_f, pieces = fence(grad_f, [[piece] for piece in jnp.split(pieces, back_cuts)])

    grad_x, last_gains = final_back(x, norm_gains[2 * layers], grad_f)
    grad_x, last_gains = fence(grad_x, last_gains)
    def unpack(inner, outer):
        attn, (up, down) = inner.sums()[0], outer.sums()
        squares = sum(jnp.sum(part * part, 0) for part in (attn, up, down))
        tiles = jnp.split(attn, 2 * width // TILE, 1)
        columns = [[0, 1, 8], [2, 3, 6], [4, 5, 7]]
        qkv = jnp.stack([jnp.concatenate([tiles[i] for i in part], 1) for part in columns], 1)
        out = jnp.concatenate([tiles[10], tiles[11], tiles[9]], 1)
        return squares, (qkv, out, up, down.T)

    gain_parts = [None] * layers
    table_got = []
    nothing = Scatter()
    outer = inner = nothing
    owned = []
    for layer in reversed(range(layers)):
        attn, upper, lower = weights[layer]
        before, h, q, keys, own, o, log_total, mid, h2 = kept[layer]
        first_step = inner is nothing

        outer.restart()
        beside = flip(pieces[0], "tl")
        fed = feed_back(grad_x, mid, h2, norm_gains[2 * layer + 1], upper, lower)
        inner.first()
        fed, inner.sent, outer.moving, beside = fence(fed, inner.sent, outer.moving, beside)
        grad_low, a, grad_u, grad_mid, mid_low, gain_mid = fed
        table_got += beside

        inner.start()
        outer.third()
        grads = weight_grads([(h2, grad_u), (grad_low, a)])
        mid_low, grads, inner.moving, outer.line = fence(
            mid_low, grads, inner.moving, outer.line
        )

        inner.second()
        mid_low, inner.sent = fence(mid_low, inner.sent)

        last_outer, outer = outer, Scatter(grads)
        last_outer.finish()
        inner.restart()
        beside = flip(pieces[1], "tl")
        passed = attend_back(mid_low, q, keys, own, seen, log_total, tables, attn)
        passed, outer.moving, inner.moving, beside = fence(
            passed, outer.moving, inner.moving, beside
        )
        table_got += beside
        grad_q, keep, send, grad_own = passed

        got = flip(send, "core")
        inner.third()
        keep, got, inner.line = fence(keep, got, inner.line)

        far = plus(keep[1], got[1])
        far, outer.moving = fence(far, outer.moving)

        far = flip(far, "grp")
        outer.first()
        far, outer.sent = fence(far, outer.sent)

        inner.finish()
        beside = flip(pieces[2], "tl")
        outer.start()
        backed = back_second(
            keep, got, far, grad_own, grad_q, tables, before, grad_mid, norm_gains[2 * layer], attn
        )
        backed, outer.sent, outer.moving, last_outer.moving, beside = fence(
            backed, outer.sent, outer.moving, last_outer.moving, beside
        )
        table_got += beside
        dz, grad_x, gain_in = backed
        gain_parts[layer] = jnp.stack([gain_in, gain_mid])

        outer.start()
        beside = flip(pieces[3], "tl")
        grads = weight_grads([(h, dz)], (mid_low, o))
        sent = ()
        if first_step:
            grad_logits, dz = fence(grad_logits, dz)
            own_table = dot("nv,nd->vd", grad_logits[0], f_all)
        if layer == 0:
            grad_low = grad_x.astype(bf16)
            gains_grad = jnp.concatenate(gain_parts + [last_gains[None]], 0)
            small = jnp.concatenate([gains_grad.reshape(-1), loss_part[None]])
            small = jnp.pad(small, (0, -small.size % (devices * 128))).reshape(devices, -1)
            sent = add_small(look_sent(0, grad_low), small)
        grad_x, grads, own_table, outer.moving, inner.moving, beside, sent = fence(
            grad_x, grads, own_table, outer.moving, inner.moving, beside, sent
        )
        table_got += beside
        pieces = [[]] * 4

        owned.append(outer)
        inner = Scatter(grads)
        owned.append(inner)
        outer.second()
        outer.sent, inner.moving, sent = fence(outer.sent, inner.moving, sent)

    outer.restart()
    got_rows = swap(sent)
    inner.first()
    inner.sent, outer.moving = fence(inner.sent, outer.moving)

    outer.third()
    inner.sent, outer.line = fence(inner.sent, outer.line)

    inner.start()
    outer.finish()
    squares, unpacked = unpack(owned[1], owned[0])
    inner.moving, got_rows, own_table, table_got, squares, unpacked = fence(
        inner.moving, got_rows, own_table, table_got, squares, unpacked
    )

    inner.second()
    inner.sent, got_rows, own_table, table_got = fence(
        inner.sent, got_rows, own_table, table_got
    )

    inner.restart()
    got_rows, small = take_small(got_rows)
    grad_table = own_table + jnp.concatenate(table_got).astype(f32)
    grad_table = grad_table + dot("kv,kd->vd", sent_rows(0), got_rows)
    inner.moving, grad_table, small = fence(inner.moving, grad_table, small)

    inner.third()
    inner.line, grad_table, small, outer.moving = fence(
        inner.line, grad_table, small, outer.moving
    )
    inner.finish(True)
    grad_table = more(lambda step: look_back(step, grad_low), grad_table)
    unpacked = [unpacked]
    for i in range(1, layers):
        more_squares, more_parts = unpack(owned[2 * i + 1], owned[2 * i])
        squares = squares + more_squares
        unpacked.append(more_parts)
    unpacked = unpacked[::-1]

    mask_count = jnp.sum(lens_all[1]).astype(f32)
    squares = squares + jnp.sum(grad_table * grad_table, 0)
    small = small[: -(-(gains_grad.size + 1) // (devices * 128)) * 128]
    shared = jnp.concatenate([small, squares])
    shared = swap(jnp.broadcast_to(shared[None], (devices, shared.size)))
    squares = jnp.sum(shared[:, small.size :])
    small = shared[:, : small.size].reshape(-1)
    gains_total = small[: gains_grad.size].reshape(gains_grad.shape)
    loss_sum = small[gains_grad.size]
    squares = squares + jnp.sum(gains_total * gains_total)
    grad_norm = jnp.sqrt(squares) / mask_count
    factor = jnp.minimum(1.0, threshold / grad_norm) / mask_count

    qkv_grad, up_grad, down_grad = (
        jnp.stack([part[i] for part in unpacked]) for i in (0, 2, 3)
    )
    out_grads = [part[1] for part in unpacked]
    results = [loss_sum, mask_count, grad_norm]
    results += update(embedding, embedding_mom, embedding_avg, grad_table * factor, rate_matrix)
    results += update(qkv_w, qkv_mom, qkv_avg, qkv_grad * factor, rate_matrix)
    results += update_turned(out_w, out_mom, out_avg, out_grads, factor)
    results += update(up_w, up_mom, up_avg, up_grad * factor, rate_matrix)
    results += update(down_w, down_mom, down_avg, down_grad * factor, rate_matrix)
    results += update(norm_gains, gains_mom, gains_avg, gains_total * factor, rate_gains)
    return tuple(results)


def solution(mesh):
    n_grp, n_dp, n_t = mesh.devices.shape
    split = Mesh(mesh.devices.reshape(n_grp, n_dp // 2, 2, n_t // 2, 2), ALL)
    dp = ("y", "core")
    owners = ("grp", "y", "core")
    rows = P(None, None, dp, None)
    table = P(ALL, None)
    wide = P(None, owners, None, TENSOR)
    tall = P(None, TENSOR, owners)
    flat = P(None, owners, TENSOR)
    return jax.shard_map(
        per_device,
        mesh=split,
        in_specs=(rows, rows, P(None, None, dp))
        + (table,) * 3 + (wide,) * 3 + (tall,) * 3 + (flat,) * 3 + (tall,) * 3 + (P(),) * 3,
        out_specs=(P(),) * 3
        + (table,) * 3 + (wide,) * 3 + (tall,) * 3 + (flat,) * 3 + (tall,) * 3 + (P(),) * 3,
        check_vma=False,
    )
```
